32 devices in a mesh: ctx: 4 (over x, core), ch: 8 (over z, y).
Axes of the slice: x: 2, y: 2, z: 4, core: 2. Of those that a mesh axis runs over, the one named last changes fastest.
Arguments:
- query_gate: bfloat16 [1024, 8192], P(('ctx', 'ch')), may hold values from -6 to 6
- key_gate: bfloat16 [1024, 8192], P(('ctx', 'ch')), may hold values from -6 to 6
- value_proj: bfloat16 [1024, 8192], P(('ctx', 'ch')), may hold values from -6 to 6
- grad_out: bfloat16 [1024, 8192], P(('ctx', 'ch')), may hold values from -0.375 to 0.375
- long_filters: float32 [512, 1024], P('ch', 'ctx'), may hold values from -0.1875 to 0.1875
Outputs:
- grad_query: bfloat16 [1024, 8192], P(('ctx', 'ch'))
- grad_key: bfloat16 [1024, 8192], P(('ctx', 'ch'))
- grad_value: bfloat16 [1024, 8192], P(('ctx', 'ch'))
- grad_filters: float32 [512, 1024], P('ch', 'ctx')
The draws below stay inside these ranges and needn't reach their ends.
All inputs are finite; a program needn't handle non-finite values.
Results may differ from the reference program's by a relative error of at most 0.0058.
Values may be sent and summed in bfloat16 or wider, within the bound.
A program may use at most 64 MiB of HBM per device.

```python
import jax
import jax.numpy as jnp
from jax import lax

D = 8192
GROUP_CH = 16
GROUPS = 512
SEQ = 1024


def block_levels(rng, shape, pieces, low, high):
    def one(dim, blocks):
        draws = jax.random.uniform(jax.random.fold_in(jax.random.fold_in(rng, 6), dim), (blocks,), jnp.float32, low / len(pieces), high / len(pieces))
        return jnp.repeat(jnp.exp(draws), shape[dim] // blocks).reshape((-1,) + (1,) * (len(shape) - dim - 1))

    gain = one(*pieces[0])
    for cut in pieces[1:]:
        gain = gain * one(*cut)
    return gain


def scatter_about(key, extent, scale, most, shards=(), kind=jnp.bfloat16):
    level = block_levels(key, extent, shards, -0.22, 0.18) if shards else 1.0
    entries = jax.random.normal(key, extent, jnp.float32) * scale * level
    return jnp.minimum(jnp.maximum(entries, -most), most).astype(kind)


def setup_inputs(seed: int = 0) -> dict:
    arg_keys = jax.random.split(jax.random.key(seed), 6)
    return {
        "query_gate": scatter_about(arg_keys[0], (SEQ, D), 1.0, 6.0, ((0, 32),)),
        "key_gate": scatter_about(arg_keys[1], (SEQ, D), 1.0, 6.0, ((0, 32),)),
        "value_proj": scatter_about(arg_keys[2], (SEQ, D), 1.0, 6.0, ((0, 32),)),
        "grad_out": scatter_about(arg_keys[3], (SEQ, D), 0.0625, 0.375, ((0, 32),)),
        "long_filters": scatter_about(arg_keys[4], (GROUPS, SEQ), SEQ ** -0.5, 0.1875, ((0, 8), (1, 4)), jnp.float32),
    }


def reference(query_gate, key_gate, value_proj, grad_out, long_filters):
    seq_len = query_gate.shape[0]
    width = query_gate.shape[1]
    signal = (key_gate.astype(jnp.float32) * value_proj.astype(jnp.float32)).astype(jnp.bfloat16)
    upstream = (grad_out.astype(jnp.float32) * query_gate.astype(jnp.float32)).astype(jnp.bfloat16)
    block_width = 256
    group_count = block_width // GROUP_CH
    length = 2 * seq_len

    def per_block(index):
        start = index * block_width
        sig_vals = lax.dynamic_slice_in_dim(signal, start, block_width, 1).astype(jnp.float32)
        up_vals = lax.dynamic_slice_in_dim(upstream, start, block_width, 1).astype(jnp.float32)
        group_taps = lax.dynamic_slice_in_dim(long_filters, index * group_count, group_count, 0)
        taps = jnp.repeat(group_taps, GROUP_CH, axis=0).T
        sig_freq = jnp.fft.rfft(sig_vals, n=length, axis=0)
        up_freq = jnp.fft.rfft(up_vals, n=length, axis=0)
        tap_freq = jnp.fft.rfft(taps, n=length, axis=0)
        convolved = jnp.fft.irfft(tap_freq * sig_freq, n=length, axis=0)[:seq_len]
        correlated = jnp.fft.irfft(jnp.conj(tap_freq) * up_freq, n=length, axis=0)[:seq_len]
        lagged = jnp.fft.irfft(up_freq * jnp.conj(sig_freq), n=length, axis=0)[:seq_len]
        grouped = lagged.reshape(seq_len, group_count, GROUP_CH).sum(axis=2)
        return convolved, correlated, grouped

    block_ids = jnp.arange(width // block_width, dtype=jnp.int32)
    convolved, correlated, grouped = lax.map(per_block, block_ids)
    convolved = convolved.transpose(1, 0, 2).reshape(seq_len, width)
    correlated = correlated.transpose(1, 0, 2).reshape(seq_len, width)
    convolved = lax.optimization_barrier(convolved.astype(jnp.bfloat16)).astype(jnp.float32)
    correlated = lax.optimization_barrier(correlated.astype(jnp.bfloat16)).astype(jnp.float32)
    grad_filters = grouped.transpose(0, 2, 1).reshape(width // GROUP_CH, seq_len)
    grad_query = (grad_out.astype(jnp.float32) * convolved).astype(jnp.bfloat16)
    grad_key = (correlated * value_proj.astype(jnp.float32)).astype(jnp.bfloat16)
    grad_value = (correlated * key_gate.astype(jnp.float32)).astype(jnp.bfloat16)
    return grad_query, grad_key, grad_value, grad_filters
```

```python
import functools
import math

import jax
import jax.numpy as jnp
from jax import lax
from jax.experimental import pallas as pl
from jax.experimental.pallas import tpu as pltpu
from jax.sharding import PartitionSpec as P

GROUP_CH = 16


HIGHEST_MODE = lax.Precision.HIGHEST
SPLIT_MODE = lax.Precision.HIGH


def passed_along(value, axis, steps):
    count = lax.axis_size(axis)
    leading, last = (max(0, -steps), min(count, count - steps))
    return lax.ppermute(value, axis, [(source, source + steps) for source in range(leading, last)])


def make_tables(block_len):
    period = 2 * block_len
    steps = lax.iota(jnp.int32, block_len)
    phase = steps[:, None] * steps[None, :] % period
    angle = phase.astype(jnp.float32) * (math.pi / block_len)
    cosine = jnp.cos(angle)
    sine = jnp.sin(angle)
    parity = 1.0 - 2.0 * (steps % 2).astype(jnp.float32)
    weights = jnp.where(steps == 0, 1.0, 2.0).astype(jnp.float32) / period
    return (
        cosine,
        -sine,
        parity,
        cosine * weights[None, :],
        -sine * weights[None, :],
        parity / period,
    )


def columns_forward(tables, values):
    return (
        jnp.dot(tables[0], values, precision=SPLIT_MODE),
        jnp.dot(tables[1], values, precision=SPLIT_MODE),
        jnp.dot(tables[2], values, precision=SPLIT_MODE),
    )


def columns_inverse(tables, real_part, imag_part, nyquist):
    return (
        jnp.dot(tables[3], real_part, precision=SPLIT_MODE)
        + jnp.dot(tables[4], imag_part, precision=SPLIT_MODE)
        + tables[5][:, None] * nyquist[None, :]
    )


def rows_forward(tables, values):
    return (
        jnp.dot(values, tables[0], precision=HIGHEST_MODE),
        jnp.dot(values, tables[1], precision=HIGHEST_MODE),
        jnp.dot(values, tables[2], precision=HIGHEST_MODE),
    )


def rows_inverse(tables, real_part, imag_part, nyquist):
    return (
        jnp.dot(real_part, tables[3].T, precision=SPLIT_MODE)
        + jnp.dot(imag_part, tables[4].T, precision=SPLIT_MODE)
        + nyquist[:, None] * tables[5][None, :]
    )


def spread_groups(rows):
    groups, block_len = rows.shape
    return jnp.broadcast_to(rows.T[:, :, None], (block_len, groups, GROUP_CH)).reshape(
        block_len, groups * GROUP_CH
    )


def spread_vector(vector):
    return jnp.broadcast_to(vector[:, None], (vector.shape[0], GROUP_CH)).reshape(-1)


def group_rows(matrix):
    block_len, chans = matrix.shape
    return matrix.reshape(block_len, chans // GROUP_CH, GROUP_CH).sum(axis=2).T


def group_vector(vector):
    return vector.reshape(-1, GROUP_CH).sum(axis=1)


def by_blocks(tables, signal, upstream, long_filters):
    block_len, chans = signal.shape
    groups = long_filters.shape[0]
    nblocks = lax.axis_size("ctx")
    own_block = lax.axis_index("ctx")
    parity = tables[2]
    prev_taps = passed_along(long_filters, "ctx", 1)
    both_re, both_im, both_ny = rows_forward(
        tables, jnp.concatenate([prev_taps, long_filters], axis=0)
    )
    own_re = both_re[:groups] + both_re[groups:] * parity
    own_im = both_im[:groups] + both_im[groups:] * parity
    own_ny = both_ny[:groups] + both_ny[groups:]
    lag_re, lag_im, lag_ny = (
        lax.all_gather(own_re[None], "ctx", axis=0, tiled=True),
        lax.all_gather(own_im[None], "ctx", axis=0, tiled=True),
        lax.all_gather(own_ny[None], "ctx", axis=0, tiled=True),
    )
    mine_re, mine_im, mine_ny = columns_forward(tables, upstream.astype(jnp.float32))
    mine_re = mine_re * parity[:, None]
    mine_im = mine_im * parity[:, None]

    def pick(lag_index):
        return (
            spread_groups(lax.dynamic_index_in_dim(lag_re, lag_index, 0, keepdims=False)),
            spread_groups(lax.dynamic_index_in_dim(lag_im, lag_index, 0, keepdims=False)),
            spread_vector(lax.dynamic_index_in_dim(lag_ny, lag_index, 0, keepdims=False)),
        )

    def add_earlier(totals, block_vals, lag_index):
        conv_re, conv_im, conv_ny, back_re, back_im, back_ny, corr_re, corr_im, corr_ny = totals
        sig_re, sig_im, sig_ny = columns_forward(tables, block_vals)
        tap_re, tap_im, tap_ny = pick(lag_index)
        conv_re = conv_re + tap_re * sig_re - tap_im * sig_im
        conv_im = conv_im + tap_re * sig_im + tap_im * sig_re
        conv_ny = conv_ny + tap_ny * sig_ny
        corr_re = corr_re.at[lag_index].add(group_rows(mine_re * sig_re + mine_im * sig_im))
        corr_im = corr_im.at[lag_index].add(group_rows(mine_im * sig_re - mine_re * sig_im))
        corr_ny = corr_ny.at[lag_index].add(group_vector(mine_ny * sig_ny))
        return (conv_re, conv_im, conv_ny, back_re, back_im, back_ny, corr_re, corr_im, corr_ny)

    def add_later(totals, block_vals, lag_index):
        conv_re, conv_im, conv_ny, back_re, back_im, back_ny, corr_re, corr_im, corr_ny = totals
        up_re, up_im, up_ny = columns_forward(tables, block_vals)
        up_re = up_re * parity[:, None]
        up_im = up_im * parity[:, None]
        tap_re, tap_im, tap_ny = pick(lag_index)
        back_re = back_re + tap_re * up_re + tap_im * up_im
        back_im = back_im + tap_re * up_im - tap_im * up_re
        back_ny = back_ny + tap_ny * up_ny
        return (conv_re, conv_im, conv_ny, back_re, back_im, back_ny, corr_re, corr_im, corr_ny)

    plane = jnp.zeros((block_len, chans), jnp.float32)
    edge = jnp.zeros((chans,), jnp.float32)
    stack = jnp.zeros((nblocks, groups, block_len), jnp.float32)
    stack_edge = jnp.zeros((nblocks, groups), jnp.float32)
    initial = (plane, plane, edge, plane, plane, edge, stack, stack, stack_edge)
    sig_piece = lax.all_gather(signal, "ctx", axis=0, tiled=True)
    up_piece = lax.all_gather(upstream, "ctx", axis=0, tiled=True)
    piece_blocks = sig_piece.shape[0] // block_len

    def one_block(offset, running):
        sig_vals = lax.dynamic_slice_in_dim(sig_piece, offset * block_len, block_len, 0).astype(
            jnp.float32
        )
        up_vals = lax.dynamic_slice_in_dim(up_piece, offset * block_len, block_len, 0).astype(
            jnp.float32
        )
        running = lax.cond(
            offset <= own_block,
            lambda current: add_earlier(current, sig_vals, own_block - offset),
            lambda current: current,
            running,
        )
        running = lax.cond(
            offset >= own_block,
            lambda current: add_later(current, up_vals, offset - own_block),
            lambda current: current,
            running,
        )
        return running

    totals = lax.fori_loop(0, piece_blocks, one_block, initial)
    conv_re, conv_im, conv_ny, back_re, back_im, back_ny, corr_re, corr_im, corr_ny = totals
    convolved = columns_inverse(
        tables, conv_re * parity[:, None], conv_im * parity[:, None], conv_ny
    )
    correlated = columns_inverse(tables, back_re, back_im, back_ny)
    total_re, total_im, total_ny = lax.psum((corr_re, corr_im, corr_ny), "ctx")
    next_block = jnp.minimum(own_block + 1, nblocks - 1)
    valid = (own_block + 1 < nblocks).astype(jnp.float32)
    cur_re = lax.dynamic_index_in_dim(total_re, own_block, 0, keepdims=False)
    cur_im = lax.dynamic_index_in_dim(total_im, own_block, 0, keepdims=False)
    cur_ny = lax.dynamic_index_in_dim(total_ny, own_block, 0, keepdims=False)
    nxt_re = lax.dynamic_index_in_dim(total_re, next_block, 0, keepdims=False)
    nxt_im = lax.dynamic_index_in_dim(total_im, next_block, 0, keepdims=False)
    nxt_ny = lax.dynamic_index_in_dim(total_ny, next_block, 0, keepdims=False)
    upper = rows_inverse(tables, cur_re * parity, cur_im * parity, cur_ny)
    lower = rows_inverse(tables, nxt_re, nxt_im, nxt_ny)
    grad_filters = upper + lower * valid
    return (convolved, correlated, grad_filters)


def on_device(query_gate, key_gate, value_proj, grad_out, long_filters):
    query_cols, key_cols, value_cols, grad_cols = (
        lax.all_to_all(query_gate, "ch", split_axis=1, concat_axis=0, tiled=True),
        lax.all_to_all(key_gate, "ch", split_axis=1, concat_axis=0, tiled=True),
        lax.all_to_all(value_proj, "ch", split_axis=1, concat_axis=0, tiled=True),
        lax.all_to_all(grad_out, "ch", split_axis=1, concat_axis=0, tiled=True),
    )
    query_vals = query_cols.astype(jnp.float32)
    key_vals = key_cols.astype(jnp.float32)
    value_vals = value_cols.astype(jnp.float32)
    grad_vals = grad_cols.astype(jnp.float32)
    signal = (key_vals * value_vals).astype(jnp.bfloat16)
    upstream = (grad_vals * query_vals).astype(jnp.bfloat16)
    tables = make_tables(signal.shape[0])
    convolved, correlated, grad_filters = by_blocks(tables, signal, upstream, long_filters)
    conv_half = convolved.astype(jnp.bfloat16)
    corr_half = correlated.astype(jnp.bfloat16)
    conv_wide = lax.optimization_barrier(conv_half).astype(jnp.float32)
    corr_wide = lax.optimization_barrier(corr_half).astype(jnp.float32)
    grad_query = (grad_vals * conv_wide).astype(jnp.bfloat16)
    grad_key = (corr_wide * value_vals).astype(jnp.bfloat16)
    grad_value = (corr_wide * key_vals).astype(jnp.bfloat16)
    query_rows, key_rows, value_rows = (
        lax.all_to_all(grad_query, "ch", split_axis=0, concat_axis=1, tiled=True),
        lax.all_to_all(grad_key, "ch", split_axis=0, concat_axis=1, tiled=True),
        lax.all_to_all(grad_value, "ch", split_axis=0, concat_axis=1, tiled=True),
    )
    return (query_rows, key_rows, value_rows, grad_filters)


TAPS_BLOCK = 128
CHUNK_CH = 128
MESH = pl.DeviceIdType.MESH
NT = (((1,), (1,)), ((), ()))


def exchange_kernel(
    nctx, nch, chunks,
    query_ref, key_ref, value_ref, grad_ref, taps_ref,
    out_ref, filt_ref,
    staged, landed, back, taps, sums, xt, ut, yt, zt,
    in_send, in_recv, out_send, out_recv, tap_send, tap_recv, sum_send, sum_recv, local_sem,
):
    ctx = lax.axis_index("ctx")
    ch = lax.axis_index("ch")
    ndev = nctx * nch
    me = ctx * nch + ch
    tokens = query_ref.shape[0]
    chans = query_ref.shape[1] // ndev
    groups = chans // GROUP_CH
    span = taps_ref.shape[1]
    seq = tokens * ndev
    block = TAPS_BLOCK
    nblocks = seq // block
    per_block = block // tokens
    chunk_groups = CHUNK_CH // GROUP_CH

    def partner(n):
        order = n // nctx
        step = (order % 2) * (0 - (order + 1) // 2) + (1 - order % 2) * (order // 2)
        other_ch = (ch + nch // 2 + step + nch) % nch
        other_ctx = (ctx + n + 1) % nctx
        return other_ctx, other_ch

    def columns(owner_ctx, owner_ch, chunk):
        start = owner_ch * (nctx * chans) + owner_ctx * chans + chunk * CHUNK_CH
        return pl.ds(pl.multiple_of(start, 128), CHUNK_CH)

    def gate(cols):
        staged[0:tokens, cols] = (
            key_ref[:, cols].astype(jnp.float32) * value_ref[:, cols].astype(jnp.float32)
        ).astype(jnp.bfloat16)
        staged[tokens:, cols] = (
            grad_ref[:, cols].astype(jnp.float32) * query_ref[:, cols].astype(jnp.float32)
        ).astype(jnp.bfloat16)

    def in_copy(chunk, n):
        other_ctx, other_ch = partner(n)
        return pltpu.make_async_remote_copy(
            src_ref=staged.at[:, columns(other_ctx, other_ch, chunk)],
            dst_ref=landed.at[chunk, me],
            send_sem=in_send.at[chunk, n],
            recv_sem=in_recv.at[chunk, me],
            device_id=(other_ctx, other_ch),
            device_id_type=MESH,
        )

    def in_arrival(chunk, n):
        other_ctx, other_ch = partner(n)
        other = other_ctx * nch + other_ch
        return pltpu.make_async_remote_copy(
            src_ref=staged.at[:, columns(other_ctx, other_ch, chunk)],
            dst_ref=landed.at[chunk, other],
            send_sem=in_send.at[chunk, n],
            recv_sem=in_recv.at[chunk, other],
            device_id=(other_ctx, other_ch),
            device_id_type=MESH,
        )

    def out_copy(chunk, n):
        other_ctx, other_ch = partner(n)
        other = other_ctx * nch + other_ch
        return pltpu.make_async_remote_copy(
            src_ref=back.at[chunk, other],
            dst_ref=out_ref.at[:, columns(ctx, ch, chunk)],
            send_sem=out_send.at[chunk, n],
            recv_sem=out_recv.at[chunk, me],
            device_id=(other_ctx, other_ch),
            device_id_type=MESH,
        )

    def out_arrival(chunk, n):
        other_ctx, other_ch = partner(n)
        other = other_ctx * nch + other_ch
        return pltpu.make_async_remote_copy(
            src_ref=back.at[chunk, other],
            dst_ref=out_ref.at[:, columns(other_ctx, other_ch, chunk)],
            send_sem=out_send.at[chunk, n],
            recv_sem=out_recv.at[chunk, other],
            device_id=(other_ctx, other_ch),
            device_id_type=MESH,
        )

    def tap_copy(step, sender):
        other = (ctx + step) % nctx
        slot = ctx if sender else other
        return pltpu.make_async_remote_copy(
            src_ref=taps_ref.at[pl.ds(pl.multiple_of(other * groups, 8), groups), :],
            dst_ref=taps.at[:, pl.ds(pl.multiple_of(slot * span, 128), span)],
            send_sem=tap_send.at[step],
            recv_sem=tap_recv.at[slot],
            device_id=(other, ch),
            device_id_type=MESH,
        )

    def sum_copy(step, sender):
        other = (ctx + step) % nctx
        slot = ctx if sender else other
        return pltpu.make_async_remote_copy(
            src_ref=sums.at[:, pl.ds(pl.multiple_of(other * span, 128), span)],
            dst_ref=filt_ref.at[pl.ds(pl.multiple_of(slot * groups, 8), groups), :],
            send_sem=sum_send.at[step],
            recv_sem=sum_recv.at[slot],
            device_id=(other, ch),
            device_id_type=MESH,
        )

    def own_in(chunk):
        return pltpu.make_async_copy(
            staged.at[:, columns(ctx, ch, chunk)], landed.at[chunk, me], local_sem.at[chunk]
        )

    def own_out(chunk):
        return pltpu.make_async_copy(
            back.at[chunk, me], out_ref.at[:, columns(ctx, ch, chunk)], local_sem.at[chunks + chunk]
        )

    def each(count, body):
        def step(n, carry):
            body(n)
            return carry

        lax.fori_loop(0, count, step, 0)

    barrier = pltpu.get_barrier_semaphore()

    def greet(n):
        other_ctx, other_ch = partner(n)
        pl.semaphore_signal(barrier, inc=1, device_id=(other_ctx, other_ch), device_id_type=MESH)

    each(ndev - 1, greet)

    def gate_chunk(chunk):
        each(
            ndev,
            lambda n: gate(pl.ds(pl.multiple_of(n * chans + chunk * CHUNK_CH, 128), CHUNK_CH)),
        )

    gate_chunk(0)
    pl.semaphore_wait(barrier, ndev - 1)
    each(ndev - 1, lambda n: in_copy(0, n).start())
    for step in range(1, nctx):
        tap_copy(step, True).start()
    own_in(0).start()
    own_taps = pltpu.make_async_copy(
        taps_ref.at[pl.ds(pl.multiple_of(ctx * groups, 8), groups), :],
        taps.at[:, pl.ds(pl.multiple_of(ctx * span, 128), span)],
        local_sem.at[2 * chunks],
    )
    own_taps.start()
    for chunk in range(1, chunks):
        gate_chunk(chunk)
        each(ndev - 1, lambda n: in_copy(chunk, n).start())
        own_in(chunk).start()
    own_taps.wait()
    for step in range(1, nctx):
        tap_copy(step, False).wait_recv()

    row_id = lax.broadcasted_iota(jnp.int32, (block, block), 0)
    col_id = lax.broadcasted_iota(jnp.int32, (block, block), 1)
    flip = (row_id + col_id == block - 1).astype(jnp.bfloat16)
    zeros = jnp.zeros((block, block), jnp.bfloat16)
    width = block + seq

    def slide(values, shift):
        return pltpu.roll(values, shift, 1, stride=1, stride_axis=0)[:, block:]

    def later(stack):
        padded = jnp.concatenate([stack, zeros], axis=0)
        return jnp.concatenate(
            [padded[k * GROUP_CH : k * GROUP_CH + block] for k in range(nblocks)], axis=1
        )

    def earlier(stack):
        padded = jnp.concatenate([zeros, stack], axis=0)
        return jnp.concatenate(
            [padded[block - k * GROUP_CH : 2 * block - k * GROUP_CH] for k in range(nblocks)],
            axis=1,
        )

    def turn_in(chunk):
        for i in range(nblocks):
            src = pl.ds(i * per_block, per_block)
            for rows, dst in ((pl.ds(0, tokens), xt), (pl.ds(tokens, tokens), ut)):
                tile = landed[chunk, src, rows, :].reshape(block, CHUNK_CH)
                dst[:, i] = tile.T.reshape(chunk_groups, GROUP_CH, block)

    def convolve(chunk, g):
        stack_x = xt[g].reshape(block, block)
        stack_u = ut[g].reshape(block, block)
        row = taps[pl.ds(chunk * chunk_groups + g, 1), :]
        row = jnp.concatenate([jnp.zeros((1, block), jnp.float32), row], axis=1)
        wide = slide(jnp.broadcast_to(row, (block, width)), 0)
        high = wide.astype(jnp.bfloat16)
        low = (wide - high.astype(jnp.float32)).astype(jnp.bfloat16)
        x_cat = earlier(stack_x)
        u_cat = later(stack_u)
        conv = jnp.zeros((block, block), jnp.float32)
        corr = jnp.zeros((block, block), jnp.float32)
        for part in (high, low):
            tall = jnp.concatenate(
                [part[:, k * block : (k + 1) * block] for k in range(nblocks)], axis=0
            )
            conv = conv + jnp.dot(x_cat, tall, preferred_element_type=jnp.float32)
            corr = corr + lax.dot_general(u_cat, part, NT, preferred_element_type=jnp.float32)
        yt[:, pl.ds(pl.multiple_of(g * GROUP_CH, GROUP_CH), GROUP_CH), :] = (
            conv.astype(jnp.bfloat16).reshape(nblocks, GROUP_CH, block)
        )
        zt[:, pl.ds(pl.multiple_of(g * GROUP_CH, GROUP_CH), GROUP_CH), :] = (
            corr.astype(jnp.bfloat16).reshape(nblocks, GROUP_CH, block)
        )

    def turn_out(chunk):
        for i in range(nblocks):
            dst = pl.ds(i * per_block, per_block)
            back[chunk, dst, 0:tokens, :] = yt[i].T.reshape(per_block, tokens, CHUNK_CH)
            back[chunk, dst, tokens:, :] = zt[i].T.reshape(per_block, tokens, CHUNK_CH)

    def correlate(chunk, g):
        stack_x = xt[g].reshape(block, block)
        u_cat = later(ut[g].reshape(block, block))
        turned = lax.dot_general(
            flip, stack_x, NT, preferred_element_type=jnp.float32
        ).astype(jnp.bfloat16)
        pairs = jnp.dot(turned, u_cat, preferred_element_type=jnp.float32)
        pairs = jnp.concatenate([pairs, jnp.zeros((block, block), jnp.float32)], axis=1)
        total = jnp.sum(slide(pairs, 1), axis=0, keepdims=True)
        sums[pl.ds(chunk * chunk_groups + g, 1), :] = total

    for chunk in range(chunks):
        own_in(chunk).wait()
        each(ndev - 1, lambda n: in_arrival(chunk, n).wait_recv())
        turn_in(chunk)
        each(chunk_groups, lambda g: convolve(chunk, g))
        turn_out(chunk)
        each(ndev - 1, lambda n: out_copy(chunk, n).start())
        own_out(chunk).start()
        each(chunk_groups, lambda g: correlate(chunk, g))

    for step in range(1, nctx):
        sum_copy(step, True).start()
    own_sums = pltpu.make_async_copy(
        sums.at[:, pl.ds(pl.multiple_of(ctx * span, 128), span)],
        filt_ref.at[pl.ds(pl.multiple_of(ctx * groups, 8), groups), :],
        local_sem.at[2 * chunks + 1],
    )
    own_sums.start()

    for step in range(1, nctx):
        tap_copy(step, True).wait_send()
    for chunk in range(chunks):
        each(ndev - 1, lambda n: in_copy(chunk, n).wait_send())
        each(ndev - 1, lambda n: out_copy(chunk, n).wait_send())
        each(ndev - 1, lambda n: out_arrival(chunk, n).wait_recv())
        own_out(chunk).wait()
    for step in range(1, nctx):
        sum_copy(step, True).wait_send()
        sum_copy(step, False).wait_recv()
    own_sums.wait()


def one_exchange(nctx, nch, query_gate, key_gate, value_proj, grad_out, long_filters):
    tokens, model = query_gate.shape
    ndev = nctx * nch
    chans = model // ndev
    groups = chans // GROUP_CH
    chunks = chans // CHUNK_CH
    seq = tokens * ndev
    nblocks = seq // TAPS_BLOCK
    chunk_groups = CHUNK_CH // GROUP_CH
    vmem = pl.BlockSpec(memory_space=pltpu.VMEM)
    half = jnp.bfloat16
    sem = pltpu.SemaphoreType.DMA
    returned, grad_filters = pl.pallas_call(
        functools.partial(exchange_kernel, nctx, nch, chunks),
        out_shape=(
            jax.ShapeDtypeStruct((2 * tokens, model), half),
            jax.ShapeDtypeStruct(long_filters.shape, jnp.float32),
        ),
        in_specs=[vmem] * 5,
        out_specs=(vmem, vmem),
        scratch_shapes=[
            pltpu.VMEM((2 * tokens, model), half),
            pltpu.VMEM((chunks, ndev, 2 * tokens, CHUNK_CH), half),
            pltpu.VMEM((chunks, ndev, 2 * tokens, CHUNK_CH), half),
            pltpu.VMEM((groups, seq), jnp.float32),
            pltpu.VMEM((groups, seq), jnp.float32),
            pltpu.VMEM((chunk_groups, nblocks, GROUP_CH, TAPS_BLOCK), half),
            pltpu.VMEM((chunk_groups, nblocks, GROUP_CH, TAPS_BLOCK), half),
            pltpu.VMEM((nblocks, CHUNK_CH, TAPS_BLOCK), half),
            pltpu.VMEM((nblocks, CHUNK_CH, TAPS_BLOCK), half),
            sem((chunks, ndev)),
            sem((chunks, ndev)),
            sem((chunks, ndev)),
            sem((chunks, ndev)),
            sem((nctx,)),
            sem((nctx,)),
            sem((nctx,)),
            sem((nctx,)),
            sem((2 * chunks + 2,)),
        ],
        compiler_params=pltpu.CompilerParams(
            collective_id=0, has_side_effects=True, vmem_limit_bytes=40 * 1024 * 1024
        ),
        name="exchange_and_convolve",
    )(query_gate, key_gate, value_proj, grad_out, long_filters)
    convolved = returned[:tokens].astype(jnp.float32)
    correlated = returned[tokens:].astype(jnp.float32)
    return (
        (grad_out.astype(jnp.float32) * convolved).astype(half),
        (correlated * value_proj.astype(jnp.float32)).astype(half),
        (correlated * key_gate.astype(jnp.float32)).astype(half),
        grad_filters,
    )


def fits_one_exchange(nctx, nch, query_shape, filter_shape):
    tokens, model = query_shape
    ndev = nctx * nch
    return (
        model % (ndev * CHUNK_CH) == 0
        and tokens % 16 == 0
        and TAPS_BLOCK % tokens == 0
        and tokens * ndev == TAPS_BLOCK * (TAPS_BLOCK // GROUP_CH)
        and filter_shape[1] % 128 == 0
        and nctx * filter_shape[0] * nch * GROUP_CH == model * nctx
    )


def solution(mesh):
    nctx, nch = mesh.shape["ctx"], mesh.shape["ch"]

    def local(query_gate, key_gate, value_proj, grad_out, long_filters):
        args = (query_gate, key_gate, value_proj, grad_out, long_filters)
        if fits_one_exchange(nctx, nch, query_gate.shape, long_filters.shape):
            return one_exchange(nctx, nch, *args)
        return on_device(*args)

    in_specs = (
        P(("ctx", "ch"), None),
        P(("ctx", "ch"), None),
        P(("ctx", "ch"), None),
        P(("ctx", "ch"), None),
        P("ch", "ctx"),
    )
    out_specs = (
        P(("ctx", "ch"), None),
        P(("ctx", "ch"), None),
        P(("ctx", "ch"), None),
        P("ch", "ctx"),
    )
    return jax.shard_map(
        local, mesh=mesh, in_specs=in_specs, out_specs=out_specs, check_vma=False
    )
```

```python
import functools
import math

import jax
import jax.numpy as jnp
from jax import lax
from jax.experimental import pallas as pl
from jax.experimental.pallas import tpu as pltpu
from jax.sharding import PartitionSpec as P

GROUP_CH = 16


HIGHEST_MODE = lax.Precision.HIGHEST
SPLIT_MODE = lax.Precision.HIGH


def passed_along(value, axis, steps):
    count = lax.axis_size(axis)
    leading, last = (max(0, -steps), min(count, count - steps))
    return lax.ppermute(value, axis, [(source, source + steps) for source in range(leading, last)])


def make_tables(block_len):
    period = 2 * block_len
    steps = lax.iota(jnp.int32, block_len)
    phase = steps[:, None] * steps[None, :] % period
    angle = phase.astype(jnp.float32) * (math.pi / block_len)
    cosine = jnp.cos(angle)
    sine = jnp.sin(angle)
    parity = 1.0 - 2.0 * (steps % 2).astype(jnp.float32)
    weights = jnp.where(steps == 0, 1.0, 2.0).astype(jnp.float32) / period
    return (
        cosine,
        -sine,
        parity,
        cosine * weights[None, :],
        -sine * weights[None, :],
        parity / period,
    )


def columns_forward(tables, values):
    return (
        jnp.dot(tables[0], values, precision=SPLIT_MODE),
        jnp.dot(tables[1], values, precision=SPLIT_MODE),
        jnp.dot(tables[2], values, precision=SPLIT_MODE),
    )


def columns_inverse(tables, real_part, imag_part, nyquist):
    return (
        jnp.dot(tables[3], real_part, precision=SPLIT_MODE)
        + jnp.dot(tables[4], imag_part, precision=SPLIT_MODE)
        + tables[5][:, None] * nyquist[None, :]
    )


def rows_forward(tables, values):
    return (
        jnp.dot(values, tables[0], precision=HIGHEST_MODE),
        jnp.dot(values, tables[1], precision=HIGHEST_MODE),
        jnp.dot(values, tables[2], precision=HIGHEST_MODE),
    )


def rows_inverse(tables, real_part, imag_part, nyquist):
    return (
        jnp.dot(real_part, tables[3].T, precision=SPLIT_MODE)
        + jnp.dot(imag_part, tables[4].T, precision=SPLIT_MODE)
        + nyquist[:, None] * tables[5][None, :]
    )


def spread_groups(rows):
    groups, block_len = rows.shape
    return jnp.broadcast_to(rows.T[:, :, None], (block_len, groups, GROUP_CH)).reshape(
        block_len, groups * GROUP_CH
    )


def spread_vector(vector):
    return jnp.broadcast_to(vector[:, None], (vector.shape[0], GROUP_CH)).reshape(-1)


def group_rows(matrix):
    block_len, chans = matrix.shape
    return matrix.reshape(block_len, chans // GROUP_CH, GROUP_CH).sum(axis=2).T


def group_vector(vector):
    return vector.reshape(-1, GROUP_CH).sum(axis=1)


def by_blocks(tables, signal, upstream, long_filters):
    block_len, chans = signal.shape
    groups = long_filters.shape[0]
    nblocks = lax.axis_size("ctx")
    own_block = lax.axis_index("ctx")
    parity = tables[2]
    prev_taps = passed_along(long_filters, "ctx", 1)
    both_re, both_im, both_ny = rows_forward(
        tables, jnp.concatenate([prev_taps, long_filters], axis=0)
    )
    own_re = both_re[:groups] + both_re[groups:] * parity
    own_im = both_im[:groups] + both_im[groups:] * parity
    own_ny = both_ny[:groups] + both_ny[groups:]
    lag_re, lag_im, lag_ny = (
        lax.all_gather(own_re[None], "ctx", axis=0, tiled=True),
        lax.all_gather(own_im[None], "ctx", axis=0, tiled=True),
        lax.all_gather(own_ny[None], "ctx", axis=0, tiled=True),
    )
    mine_re, mine_im, mine_ny = columns_forward(tables, upstream.astype(jnp.float32))
    mine_re = mine_re * parity[:, None]
    mine_im = mine_im * parity[:, None]

    def pick(lag_index):
        return (
            spread_groups(lax.dynamic_index_in_dim(lag_re, lag_index, 0, keepdims=False)),
            spread_groups(lax.dynamic_index_in_dim(lag_im, lag_index, 0, keepdims=False)),
            spread_vector(lax.dynamic_index_in_dim(lag_ny, lag_index, 0, keepdims=False)),
        )

    def add_earlier(totals, block_vals, lag_index):
        conv_re, conv_im, conv_ny, back_re, back_im, back_ny, corr_re, corr_im, corr_ny = totals
        sig_re, sig_im, sig_ny = columns_forward(tables, block_vals)
        tap_re, tap_im, tap_ny = pick(lag_index)
        conv_re = conv_re + tap_re * sig_re - tap_im * sig_im
        conv_im = conv_im + tap_re * sig_im + tap_im * sig_re
        conv_ny = conv_ny + tap_ny * sig_ny
        corr_re = corr_re.at[lag_index].add(group_rows(mine_re * sig_re + mine_im * sig_im))
        corr_im = corr_im.at[lag_index].add(group_rows(mine_im * sig_re - mine_re * sig_im))
        corr_ny = corr_ny.at[lag_index].add(group_vector(mine_ny * sig_ny))
        return (conv_re, conv_im, conv_ny, back_re, back_im, back_ny, corr_re, corr_im, corr_ny)

    def add_later(totals, block_vals, lag_index):
        conv_re, conv_im, conv_ny, back_re, back_im, back_ny, corr_re, corr_im, corr_ny = totals
        up_re, up_im, up_ny = columns_forward(tables, block_vals)
        up_re = up_re * parity[:, None]
        up_im = up_im * parity[:, None]
        tap_re, tap_im, tap_ny = pick(lag_index)
        back_re = back_re + tap_re * up_re + tap_im * up_im
        back_im = back_im + tap_re * up_im - tap_im * up_re
        back_ny = back_ny + tap_ny * up_ny
        return (conv_re, conv_im, conv_ny, back_re, back_im, back_ny, corr_re, corr_im, corr_ny)

    plane = jnp.zeros((block_len, chans), jnp.float32)
    edge = jnp.zeros((chans,), jnp.float32)
    stack = jnp.zeros((nblocks, groups, block_len), jnp.float32)
    stack_edge = jnp.zeros((nblocks, groups), jnp.float32)
    initial = (plane, plane, edge, plane, plane, edge, stack, stack, stack_edge)
    sig_piece = lax.all_gather(signal, "ctx", axis=0, tiled=True)
    up_piece = lax.all_gather(upstream, "ctx", axis=0, tiled=True)
    piece_blocks = sig_piece.shape[0] // block_len

    def one_block(offset, running):
        sig_vals = lax.dynamic_slice_in_dim(sig_piece, offset * block_len, block_len, 0).astype(
            jnp.float32
        )
        up_vals = lax.dynamic_slice_in_dim(up_piece, offset * block_len, block_len, 0).astype(
            jnp.float32
        )
        running = lax.cond(
            offset <= own_block,
            lambda current: add_earlier(current, sig_vals, own_block - offset),
            lambda current: current,
            running,
        )
        running = lax.cond(
            offset >= own_block,
            lambda current: add_later(current, up_vals, offset - own_block),
            lambda current: current,
            running,
        )
        return running

    totals = lax.fori_loop(0, piece_blocks, one_block, initial)
    conv_re, conv_im, conv_ny, back_re, back_im, back_ny, corr_re, corr_im, corr_ny = totals
    convolved = columns_inverse(
        tables, conv_re * parity[:, None], conv_im * parity[:, None], conv_ny
    )
    correlated = columns_inverse(tables, back_re, back_im, back_ny)
    total_re, total_im, total_ny = lax.psum((corr_re, corr_im, corr_ny), "ctx")
    next_block = jnp.minimum(own_block + 1, nblocks - 1)
    valid = (own_block + 1 < nblocks).astype(jnp.float32)
    cur_re = lax.dynamic_index_in_dim(total_re, own_block, 0, keepdims=False)
    cur_im = lax.dynamic_index_in_dim(total_im, own_block, 0, keepdims=False)
    cur_ny = lax.dynamic_index_in_dim(total_ny, own_block, 0, keepdims=False)
    nxt_re = lax.dynamic_index_in_dim(total_re, next_block, 0, keepdims=False)
    nxt_im = lax.dynamic_index_in_dim(total_im, next_block, 0, keepdims=False)
    nxt_ny = lax.dynamic_index_in_dim(total_ny, next_block, 0, keepdims=False)
    upper = rows_inverse(tables, cur_re * parity, cur_im * parity, cur_ny)
    lower = rows_inverse(tables, nxt_re, nxt_im, nxt_ny)
    grad_filters = upper + lower * valid
    return (convolved, correlated, grad_filters)


def on_device(query_gate, key_gate, value_proj, grad_out, long_filters):
    query_cols, key_cols, value_cols, grad_cols = (
        lax.all_to_all(query_gate, "ch", split_axis=1, concat_axis=0, tiled=True),
        lax.all_to_all(key_gate, "ch", split_axis=1, concat_axis=0, tiled=True),
        lax.all_to_all(value_proj, "ch", split_axis=1, concat_axis=0, tiled=True),
        lax.all_to_all(grad_out, "ch", split_axis=1, concat_axis=0, tiled=True),
    )
    query_vals = query_cols.astype(jnp.float32)
    key_vals = key_cols.astype(jnp.float32)
    value_vals = value_cols.astype(jnp.float32)
    grad_vals = grad_cols.astype(jnp.float32)
    signal = (key_vals * value_vals).astype(jnp.bfloat16)
    upstream = (grad_vals * query_vals).astype(jnp.bfloat16)
    tables = make_tables(signal.shape[0])
    convolved, correlated, grad_filters = by_blocks(tables, signal, upstream, long_filters)
    conv_half = convolved.astype(jnp.bfloat16)
    corr_half = correlated.astype(jnp.bfloat16)
    conv_wide = lax.optimization_barrier(conv_half).astype(jnp.float32)
    corr_wide = lax.optimization_barrier(corr_half).astype(jnp.float32)
    grad_query = (grad_vals * conv_wide).astype(jnp.bfloat16)
    grad_key = (corr_wide * value_vals).astype(jnp.bfloat16)
    grad_value = (corr_wide * key_vals).astype(jnp.bfloat16)
    query_rows, key_rows, value_rows = (
        lax.all_to_all(grad_query, "ch", split_axis=0, concat_axis=1, tiled=True),
        lax.all_to_all(grad_key, "ch", split_axis=0, concat_axis=1, tiled=True),
        lax.all_to_all(grad_value, "ch", split_axis=0, concat_axis=1, tiled=True),
    )
    return (query_rows, key_rows, value_rows, grad_filters)


TAPS_BLOCK = 128
CHUNK_CH = 128
LOAD_PIECES = 4
MESH = pl.DeviceIdType.MESH
NT = (((1,), (1,)), ((), ()))


def exchange_kernel(
    nctx, nch, chunks,
    query_hbm, key_hbm, value_hbm, grad_hbm, taps_ref,
    out_ref, filt_ref,
    query_ref, key_ref, value_ref, grad_ref, staged, landed, back, taps, sums, toeplitz, xt, ut, yt, zt,
    in_send, in_recv, out_send, out_recv, tap_send, tap_recv, sum_send, sum_recv, local_sem, load_sem,
):
    ctx = lax.axis_index("ctx")
    ch = lax.axis_index("ch")
    ndev = nctx * nch
    me = ctx * nch + ch
    tokens = query_ref.shape[0]
    chans = query_ref.shape[1] // ndev
    groups = chans // GROUP_CH
    span = taps_ref.shape[1]
    seq = tokens * ndev
    block = TAPS_BLOCK
    nblocks = seq // block
    per_block = block // tokens
    chunk_groups = CHUNK_CH // GROUP_CH

    def partner(n):
        order = n // nctx
        step = (order % 2) * (0 - (order + 1) // 2) + (1 - order % 2) * (order // 2)
        other_ch = (ch + nch // 2 + step + nch) % nch
        other_ctx = (ctx + n + 1) % nctx
        return other_ctx, other_ch

    def columns(owner_ctx, owner_ch, chunk):
        start = owner_ch * (nctx * chans) + owner_ctx * chans + chunk * CHUNK_CH
        return pl.ds(pl.multiple_of(start, 128), CHUNK_CH)

    def gate(cols):
        staged[0:tokens, cols] = (
            key_ref[:, cols].astype(jnp.float32) * value_ref[:, cols].astype(jnp.float32)
        ).astype(jnp.bfloat16)
        staged[tokens:, cols] = (
            grad_ref[:, cols].astype(jnp.float32) * query_ref[:, cols].astype(jnp.float32)
        ).astype(jnp.bfloat16)

    def in_copy(chunk, n):
        other_ctx, other_ch = partner(n)
        return pltpu.make_async_remote_copy(
            src_ref=staged.at[:, columns(other_ctx, other_ch, chunk)],
            dst_ref=landed.at[chunk, me],
            send_sem=in_send.at[chunk, n],
            recv_sem=in_recv.at[chunk, me],
            device_id=(other_ctx, other_ch),
            device_id_type=MESH,
        )

    def in_arrival(chunk, n):
        other_ctx, other_ch = partner(n)
        other = other_ctx * nch + other_ch
        return pltpu.make_async_remote_copy(
            src_ref=staged.at[:, columns(other_ctx, other_ch, chunk)],
            dst_ref=landed.at[chunk, other],
            send_sem=in_send.at[chunk, n],
            recv_sem=in_recv.at[chunk, other],
            device_id=(other_ctx, other_ch),
            device_id_type=MESH,
        )

    def out_copy(chunk, n):
        other_ctx, other_ch = partner(n)
        other = other_ctx * nch + other_ch
        return pltpu.make_async_remote_copy(
            src_ref=back.at[chunk, other],
            dst_ref=out_ref.at[:, columns(ctx, ch, chunk)],
            send_sem=out_send.at[chunk, n],
            recv_sem=out_recv.at[chunk, me],
            device_id=(other_ctx, other_ch),
            device_id_type=MESH,
        )

    def out_arrival(chunk, n):
        other_ctx, other_ch = partner(n)
        other = other_ctx * nch + other_ch
        return pltpu.make_async_remote_copy(
            src_ref=back.at[chunk, other],
            dst_ref=out_ref.at[:, columns(other_ctx, other_ch, chunk)],
            send_sem=out_send.at[chunk, n],
            recv_sem=out_recv.at[chunk, other],
            device_id=(other_ctx, other_ch),
            device_id_type=MESH,
        )

    def tap_copy(step, sender):
        other = (ctx + step) % nctx
        slot = ctx if sender else other
        return pltpu.make_async_remote_copy(
            src_ref=taps_ref.at[pl.ds(pl.multiple_of(other * groups, 8), groups), :],
            dst_ref=taps.at[:, pl.ds(pl.multiple_of(slot * span, 128), span)],
            send_sem=tap_send.at[step],
            recv_sem=tap_recv.at[slot],
            device_id=(other, ch),
            device_id_type=MESH,
        )

    def sum_copy(step, sender):
        other = (ctx + step) % nctx
        slot = ctx if sender else other
        return pltpu.make_async_remote_copy(
            src_ref=sums.at[:, pl.ds(pl.multiple_of(other * span, 128), span)],
            dst_ref=filt_ref.at[pl.ds(pl.multiple_of(slot * groups, 8), groups), :],
            send_sem=sum_send.at[step],
            recv_sem=sum_recv.at[slot],
            device_id=(other, ch),
            device_id_type=MESH,
        )

    def own_in(chunk):
        return pltpu.make_async_copy(
            staged.at[:, columns(ctx, ch, chunk)], landed.at[chunk, me], local_sem.at[chunk]
        )

    def own_out(chunk):
        return pltpu.make_async_copy(
            back.at[chunk, me], out_ref.at[:, columns(ctx, ch, chunk)], local_sem.at[chunks + chunk]
        )

    def each(count, body, unroll=1):
        def step(n, carry):
            body(n)
            return carry

        lax.fori_loop(0, count, step, 0, unroll=unroll)

    pieces = LOAD_PIECES
    piece = nctx * nch * chans // pieces

    def load(which, part):
        src, dst = (
            (query_hbm, query_ref),
            (key_hbm, key_ref),
            (value_hbm, value_ref),
            (grad_hbm, grad_ref),
        )[which]
        cols = pl.ds(part * piece, piece)
        return pltpu.make_async_copy(src.at[:, cols], dst.at[:, cols], load_sem.at[which, part])

    for part in range(pieces):
        for which in range(4):
            load(which, part).start()

    barrier = pltpu.get_barrier_semaphore()

    def greet(n):
        other_ctx, other_ch = partner(n)
        pl.semaphore_signal(barrier, inc=1, device_id=(other_ctx, other_ch), device_id_type=MESH)

    each(ndev - 1, greet)

    def gate_chunk(chunk, first, count):
        each(
            count,
            lambda n: gate(
                pl.ds(pl.multiple_of((first + n) * chans + chunk * CHUNK_CH, 128), CHUNK_CH)
            ),
            unroll=4,
        )

    own_taps = pltpu.make_async_copy(
        taps_ref.at[pl.ds(pl.multiple_of(ctx * groups, 8), groups), :],
        taps.at[:, pl.ds(pl.multiple_of(ctx * span, 128), span)],
        local_sem.at[2 * chunks],
    )
    own_taps.start()
    for part in range(pieces):
        for which in range(4):
            load(which, part).wait()
        gate_chunk(0, part * (ndev // pieces), ndev // pieces)
    pl.semaphore_wait(barrier, ndev - 1)
    for step in range(1, nctx):
        tap_copy(step, True).start()
    each(ndev - 1, lambda n: in_copy(0, n).start())
    own_in(0).start()
    for chunk in range(1, chunks):
        gate_chunk(chunk, 0, ndev)
        each(ndev - 1, lambda n: in_copy(chunk, n).start())
        own_in(chunk).start()
    own_taps.wait()
    for step in range(1, nctx):
        tap_copy(step, False).wait_recv()

    row_id = lax.broadcasted_iota(jnp.int32, (block, block), 0)
    col_id = lax.broadcasted_iota(jnp.int32, (block, block), 1)
    flip = (row_id + col_id == block - 1).astype(jnp.bfloat16)
    zeros = jnp.zeros((block, block), jnp.bfloat16)
    width = block + seq

    def slide(values, shift):
        return pltpu.roll(values, shift, 1, stride=1, stride_axis=0)[:, block:]

    def later(stack):
        padded = jnp.concatenate([stack, zeros], axis=0)
        return jnp.concatenate(
            [padded[k * GROUP_CH : k * GROUP_CH + block] for k in range(nblocks)], axis=1
        )

    def earlier(stack):
        padded = jnp.concatenate([zeros, stack], axis=0)
        return jnp.concatenate(
            [padded[block - k * GROUP_CH : 2 * block - k * GROUP_CH] for k in range(nblocks)],
            axis=1,
        )

    def turn_in(chunk):
        for i in range(nblocks):
            src = pl.ds(i * per_block, per_block)
            for rows, dst in ((pl.ds(0, tokens), xt), (pl.ds(tokens, tokens), ut)):
                tile = landed[chunk, src, rows, :].reshape(block, CHUNK_CH)
                dst[chunk, :, i] = tile.T.reshape(chunk_groups, GROUP_CH, block)

    def build(group):
        row = taps[pl.ds(group, 1), :]
        row = jnp.concatenate([jnp.zeros((1, block), jnp.float32), row], axis=1)
        wide = slide(jnp.broadcast_to(row, (block, width)), 0)
        high = wide.astype(jnp.bfloat16)
        low = (wide - high.astype(jnp.float32)).astype(jnp.bfloat16)
        for which, part in ((0, high), (1, low)):
            for k in range(nblocks):
                toeplitz[group, which, k] = part[:, k * block : (k + 1) * block]

    def convolve(chunk, g):
        x_cat = earlier(xt[chunk, g].reshape(block, block))
        u_cat = later(ut[chunk, g].reshape(block, block))
        conv = jnp.zeros((block, block), jnp.float32)
        corr = jnp.zeros((block, block), jnp.float32)
        for which in range(2):
            part = toeplitz[chunk * chunk_groups + g, which]
            tall = part.reshape(nblocks * block, block)
            flat = jnp.concatenate([part[k] for k in range(nblocks)], axis=1)
            conv = conv + jnp.dot(x_cat, tall, preferred_element_type=jnp.float32)
            corr = corr + lax.dot_general(u_cat, flat, NT, preferred_element_type=jnp.float32)
        yt[:, pl.ds(pl.multiple_of(g * GROUP_CH, GROUP_CH), GROUP_CH), :] = (
            conv.astype(jnp.bfloat16).reshape(nblocks, GROUP_CH, block)
        )
        zt[:, pl.ds(pl.multiple_of(g * GROUP_CH, GROUP_CH), GROUP_CH), :] = (
            corr.astype(jnp.bfloat16).reshape(nblocks, GROUP_CH, block)
        )

    def turn_out(chunk):
        for i in range(nblocks):
            dst = pl.ds(i * per_block, per_block)
            back[chunk, dst, 0:tokens, :] = yt[i].T.reshape(per_block, tokens, CHUNK_CH)
            back[chunk, dst, tokens:, :] = zt[i].T.reshape(per_block, tokens, CHUNK_CH)

    def correlate(chunk, g):
        stack_x = xt[chunk, g].reshape(block, block)
        u_cat = later(ut[chunk, g].reshape(block, block))
        turned = lax.dot_general(
            flip, stack_x, NT, preferred_element_type=jnp.float32
        ).astype(jnp.bfloat16)
        pairs = jnp.dot(turned, u_cat, preferred_element_type=jnp.float32)
        pairs = jnp.concatenate([pairs, jnp.zeros((block, block), jnp.float32)], axis=1)
        total = jnp.sum(slide(pairs, 1), axis=0, keepdims=True)
        sums[pl.ds(chunk * chunk_groups + g, 1), :] = total

    each(groups, build, unroll=2)
    for chunk in range(chunks):
        own_in(chunk).wait()
        each(ndev - 1, lambda n: in_arrival(chunk, n).wait_recv())
        turn_in(chunk)
        each(chunk_groups, lambda g: convolve(chunk, g), unroll=2)
        turn_out(chunk)
        each(ndev - 1, lambda n: out_copy(chunk, n).start())
        own_out(chunk).start()

    for chunk in range(chunks):
        each(chunk_groups, lambda g: correlate(chunk, g), unroll=2)

    for step in range(1, nctx):
        sum_copy(step, True).start()
    own_sums = pltpu.make_async_copy(
        sums.at[:, pl.ds(pl.multiple_of(ctx * span, 128), span)],
        filt_ref.at[pl.ds(pl.multiple_of(ctx * groups, 8), groups), :],
        local_sem.at[2 * chunks + 1],
    )
    own_sums.start()

    for step in range(1, nctx):
        tap_copy(step, True).wait_send()
    for chunk in range(chunks):
        each(ndev - 1, lambda n: in_copy(chunk, n).wait_send())
        each(ndev - 1, lambda n: out_copy(chunk, n).wait_send())
        each(ndev - 1, lambda n: out_arrival(chunk, n).wait_recv())
        own_out(chunk).wait()
    for step in range(1, nctx):
        sum_copy(step, True).wait_send()
        sum_copy(step, False).wait_recv()
    own_sums.wait()


def one_exchange(nctx, nch, query_gate, key_gate, value_proj, grad_out, long_filters):
    tokens, model = query_gate.shape
    ndev = nctx * nch
    chans = model // ndev
    groups = chans // GROUP_CH
    chunks = chans // CHUNK_CH
    seq = tokens * ndev
    nblocks = seq // TAPS_BLOCK
    chunk_groups = CHUNK_CH // GROUP_CH
    vmem = pl.BlockSpec(memory_space=pltpu.VMEM)
    half = jnp.bfloat16
    sem = pltpu.SemaphoreType.DMA
    returned, grad_filters = pl.pallas_call(
        functools.partial(exchange_kernel, nctx, nch, chunks),
        out_shape=(
            jax.ShapeDtypeStruct((2 * tokens, model), half),
            jax.ShapeDtypeStruct(long_filters.shape, jnp.float32),
        ),
        in_specs=[pl.BlockSpec(memory_space=pltpu.HBM)] * 4 + [vmem],
        out_specs=(vmem, vmem),
        scratch_shapes=[pltpu.VMEM((tokens, model), half)] * 4
        + [
            pltpu.VMEM((2 * tokens, model), half),
            pltpu.VMEM((chunks, ndev, 2 * tokens, CHUNK_CH), half),
            pltpu.VMEM((chunks, ndev, 2 * tokens, CHUNK_CH), half),
            pltpu.VMEM((groups, seq), jnp.float32),
            pltpu.VMEM((groups, seq), jnp.float32),
            pltpu.VMEM((groups, 2, nblocks, TAPS_BLOCK, TAPS_BLOCK), half),
            pltpu.VMEM((chunks, chunk_groups, nblocks, GROUP_CH, TAPS_BLOCK), half),
            pltpu.VMEM((chunks, chunk_groups, nblocks, GROUP_CH, TAPS_BLOCK), half),
            pltpu.VMEM((nblocks, CHUNK_CH, TAPS_BLOCK), half),
            pltpu.VMEM((nblocks, CHUNK_CH, TAPS_BLOCK), half),
            sem((chunks, ndev)),
            sem((chunks, ndev)),
            sem((chunks, ndev)),
            sem((chunks, ndev)),
            sem((nctx,)),
            sem((nctx,)),
            sem((nctx,)),
            sem((nctx,)),
            sem((2 * chunks + 2,)),
            sem((4, LOAD_PIECES)),
        ],
        compiler_params=pltpu.CompilerParams(
            collective_id=0, has_side_effects=True, vmem_limit_bytes=56 * 1024 * 1024
        ),
        name="exchange_and_convolve",
    )(query_gate, key_gate, value_proj, grad_out, long_filters)
    convolved = returned[:tokens].astype(jnp.float32)
    correlated = returned[tokens:].astype(jnp.float32)
    return (
        (grad_out.astype(jnp.float32) * convolved).astype(half),
        (correlated * value_proj.astype(jnp.float32)).astype(half),
        (correlated * key_gate.astype(jnp.float32)).astype(half),
        grad_filters,
    )


def fits_one_exchange(nctx, nch, query_shape, filter_shape):
    tokens, model = query_shape
    ndev = nctx * nch
    return (
        model % (ndev * CHUNK_CH) == 0
        and tokens % 16 == 0
        and TAPS_BLOCK % tokens == 0
        and tokens * ndev == TAPS_BLOCK * (TAPS_BLOCK // GROUP_CH)
        and filter_shape[1] % 128 == 0
        and nctx * filter_shape[0] * nch * GROUP_CH == model * nctx
    )


def solution(mesh):
    nctx, nch = mesh.shape["ctx"], mesh.shape["ch"]

    def local(query_gate, key_gate, value_proj, grad_out, long_filters):
        args = (query_gate, key_gate, value_proj, grad_out, long_filters)
        if fits_one_exchange(nctx, nch, query_gate.shape, long_filters.shape):
            return one_exchange(nctx, nch, *args)
        return on_device(*args)

    in_specs = (
        P(("ctx", "ch"), None),
        P(("ctx", "ch"), None),
        P(("ctx", "ch"), None),
        P(("ctx", "ch"), None),
        P("ch", "ctx"),
    )
    out_specs = (
        P(("ctx", "ch"), None),
        P(("ctx", "ch"), None),
        P(("ctx", "ch"), None),
        P("ch", "ctx"),
    )
    return jax.shard_map(
        local, mesh=mesh, in_specs=in_specs, out_specs=out_specs, check_vma=False
    )
```

```python
import functools
import math

import jax
import jax.numpy as jnp
from jax import lax
from jax.experimental import pallas as pl
from jax.experimental.pallas import tpu as pltpu
from jax.sharding import PartitionSpec as P

GROUP_CH = 16


HIGHEST_MODE = lax.Precision.HIGHEST
SPLIT_MODE = lax.Precision.HIGH


def passed_along(value, axis, steps):
    count = lax.axis_size(axis)
    leading, last = (max(0, -steps), min(count, count - steps))
    return lax.ppermute(value, axis, [(source, source + steps) for source in range(leading, last)])


def make_tables(block_len):
    period = 2 * block_len
    steps = lax.iota(jnp.int32, block_len)
    phase = steps[:, None] * steps[None, :] % period
    angle = phase.astype(jnp.float32) * (math.pi / block_len)
    cosine = jnp.cos(angle)
    sine = jnp.sin(angle)
    parity = 1.0 - 2.0 * (steps % 2).astype(jnp.float32)
    weights = jnp.where(steps == 0, 1.0, 2.0).astype(jnp.float32) / period
    return (
        cosine,
        -sine,
        parity,
        cosine * weights[None, :],
        -sine * weights[None, :],
        parity / period,
    )


def columns_forward(tables, values):
    return (
        jnp.dot(tables[0], values, precision=SPLIT_MODE),
        jnp.dot(tables[1], values, precision=SPLIT_MODE),
        jnp.dot(tables[2], values, precision=SPLIT_MODE),
    )


def columns_inverse(tables, real_part, imag_part, nyquist):
    return (
        jnp.dot(tables[3], real_part, precision=SPLIT_MODE)
        + jnp.dot(tables[4], imag_part, precision=SPLIT_MODE)
        + tables[5][:, None] * nyquist[None, :]
    )


def rows_forward(tables, values):
    return (
        jnp.dot(values, tables[0], precision=HIGHEST_MODE),
        jnp.dot(values, tables[1], precision=HIGHEST_MODE),
        jnp.dot(values, tables[2], precision=HIGHEST_MODE),
    )


def rows_inverse(tables, real_part, imag_part, nyquist):
    return (
        jnp.dot(real_part, tables[3].T, precision=SPLIT_MODE)
        + jnp.dot(imag_part, tables[4].T, precision=SPLIT_MODE)
        + nyquist[:, None] * tables[5][None, :]
    )


def spread_groups(rows):
    groups, block_len = rows.shape
    return jnp.broadcast_to(rows.T[:, :, None], (block_len, groups, GROUP_CH)).reshape(
        block_len, groups * GROUP_CH
    )


def spread_vector(vector):
    return jnp.broadcast_to(vector[:, None], (vector.shape[0], GROUP_CH)).reshape(-1)


def group_rows(matrix):
    block_len, chans = matrix.shape
    return matrix.reshape(block_len, chans // GROUP_CH, GROUP_CH).sum(axis=2).T


def group_vector(vector):
    return vector.reshape(-1, GROUP_CH).sum(axis=1)


def by_blocks(tables, signal, upstream, long_filters):
    block_len, chans = signal.shape
    groups = long_filters.shape[0]
    nblocks = lax.axis_size("ctx")
    own_block = lax.axis_index("ctx")
    parity = tables[2]
    prev_taps = passed_along(long_filters, "ctx", 1)
    both_re, both_im, both_ny = rows_forward(
        tables, jnp.concatenate([prev_taps, long_filters], axis=0)
    )
    own_re = both_re[:groups] + both_re[groups:] * parity
    own_im = both_im[:groups] + both_im[groups:] * parity
    own_ny = both_ny[:groups] + both_ny[groups:]
    lag_re, lag_im, lag_ny = (
        lax.all_gather(own_re[None], "ctx", axis=0, tiled=True),
        lax.all_gather(own_im[None], "ctx", axis=0, tiled=True),
        lax.all_gather(own_ny[None], "ctx", axis=0, tiled=True),
    )
    mine_re, mine_im, mine_ny = columns_forward(tables, upstream.astype(jnp.float32))
    mine_re = mine_re * parity[:, None]
    mine_im = mine_im * parity[:, None]

    def pick(lag_index):
        return (
            spread_groups(lax.dynamic_index_in_dim(lag_re, lag_index, 0, keepdims=False)),
            spread_groups(lax.dynamic_index_in_dim(lag_im, lag_index, 0, keepdims=False)),
            spread_vector(lax.dynamic_index_in_dim(lag_ny, lag_index, 0, keepdims=False)),
        )

    def add_earlier(totals, block_vals, lag_index):
        conv_re, conv_im, conv_ny, back_re, back_im, back_ny, corr_re, corr_im, corr_ny = totals
        sig_re, sig_im, sig_ny = columns_forward(tables, block_vals)
        tap_re, tap_im, tap_ny = pick(lag_index)
        conv_re = conv_re + tap_re * sig_re - tap_im * sig_im
        conv_im = conv_im + tap_re * sig_im + tap_im * sig_re
        conv_ny = conv_ny + tap_ny * sig_ny
        corr_re = corr_re.at[lag_index].add(group_rows(mine_re * sig_re + mine_im * sig_im))
        corr_im = corr_im.at[lag_index].add(group_rows(mine_im * sig_re - mine_re * sig_im))
        corr_ny = corr_ny.at[lag_index].add(group_vector(mine_ny * sig_ny))
        return (conv_re, conv_im, conv_ny, back_re, back_im, back_ny, corr_re, corr_im, corr_ny)

    def add_later(totals, block_vals, lag_index):
        conv_re, conv_im, conv_ny, back_re, back_im, back_ny, corr_re, corr_im, corr_ny = totals
        up_re, up_im, up_ny = columns_forward(tables, block_vals)
        up_re = up_re * parity[:, None]
        up_im = up_im * parity[:, None]
        tap_re, tap_im, tap_ny = pick(lag_index)
        back_re = back_re + tap_re * up_re + tap_im * up_im
        back_im = back_im + tap_re * up_im - tap_im * up_re
        back_ny = back_ny + tap_ny * up_ny
        return (conv_re, conv_im, conv_ny, back_re, back_im, back_ny, corr_re, corr_im, corr_ny)

    plane = jnp.zeros((block_len, chans), jnp.float32)
    edge = jnp.zeros((chans,), jnp.float32)
    stack = jnp.zeros((nblocks, groups, block_len), jnp.float32)
    stack_edge = jnp.zeros((nblocks, groups), jnp.float32)
    initial = (plane, plane, edge, plane, plane, edge, stack, stack, stack_edge)
    sig_piece = lax.all_gather(signal, "ctx", axis=0, tiled=True)
    up_piece = lax.all_gather(upstream, "ctx", axis=0, tiled=True)
    piece_blocks = sig_piece.shape[0] // block_len

    def one_block(offset, running):
        sig_vals = lax.dynamic_slice_in_dim(sig_piece, offset * block_len, block_len, 0).astype(
            jnp.float32
        )
        up_vals = lax.dynamic_slice_in_dim(up_piece, offset * block_len, block_len, 0).astype(
            jnp.float32
        )
        running = lax.cond(
            offset <= own_block,
            lambda current: add_earlier(current, sig_vals, own_block - offset),
            lambda current: current,
            running,
        )
        running = lax.cond(
            offset >= own_block,
            lambda current: add_later(current, up_vals, offset - own_block),
            lambda current: current,
            running,
        )
        return running

    totals = lax.fori_loop(0, piece_blocks, one_block, initial)
    conv_re, conv_im, conv_ny, back_re, back_im, back_ny, corr_re, corr_im, corr_ny = totals
    convolved = columns_inverse(
        tables, conv_re * parity[:, None], conv_im * parity[:, None], conv_ny
    )
    correlated = columns_inverse(tables, back_re, back_im, back_ny)
    total_re, total_im, total_ny = lax.psum((corr_re, corr_im, corr_ny), "ctx")
    next_block = jnp.minimum(own_block + 1, nblocks - 1)
    valid = (own_block + 1 < nblocks).astype(jnp.float32)
    cur_re = lax.dynamic_index_in_dim(total_re, own_block, 0, keepdims=False)
    cur_im = lax.dynamic_index_in_dim(total_im, own_block, 0, keepdims=False)
    cur_ny = lax.dynamic_index_in_dim(total_ny, own_block, 0, keepdims=False)
    nxt_re = lax.dynamic_index_in_dim(total_re, next_block, 0, keepdims=False)
    nxt_im = lax.dynamic_index_in_dim(total_im, next_block, 0, keepdims=False)
    nxt_ny = lax.dynamic_index_in_dim(total_ny, next_block, 0, keepdims=False)
    upper = rows_inverse(tables, cur_re * parity, cur_im * parity, cur_ny)
    lower = rows_inverse(tables, nxt_re, nxt_im, nxt_ny)
    grad_filters = upper + lower * valid
    return (convolved, correlated, grad_filters)


def on_device(query_gate, key_gate, value_proj, grad_out, long_filters):
    query_cols, key_cols, value_cols, grad_cols = (
        lax.all_to_all(query_gate, "ch", split_axis=1, concat_axis=0, tiled=True),
        lax.all_to_all(key_gate, "ch", split_axis=1, concat_axis=0, tiled=True),
        lax.all_to_all(value_proj, "ch", split_axis=1, concat_axis=0, tiled=True),
        lax.all_to_all(grad_out, "ch", split_axis=1, concat_axis=0, tiled=True),
    )
    query_vals = query_cols.astype(jnp.float32)
    key_vals = key_cols.astype(jnp.float32)
    value_vals = value_cols.astype(jnp.float32)
    grad_vals = grad_cols.astype(jnp.float32)
    signal = (key_vals * value_vals).astype(jnp.bfloat16)
    upstream = (grad_vals * query_vals).astype(jnp.bfloat16)
    tables = make_tables(signal.shape[0])
    convolved, correlated, grad_filters = by_blocks(tables, signal, upstream, long_filters)
    conv_half = convolved.astype(jnp.bfloat16)
    corr_half = correlated.astype(jnp.bfloat16)
    conv_wide = lax.optimization_barrier(conv_half).astype(jnp.float32)
    corr_wide = lax.optimization_barrier(corr_half).astype(jnp.float32)
    grad_query = (grad_vals * conv_wide).astype(jnp.bfloat16)
    grad_key = (corr_wide * value_vals).astype(jnp.bfloat16)
    grad_value = (corr_wide * key_vals).astype(jnp.bfloat16)
    query_rows, key_rows, value_rows = (
        lax.all_to_all(grad_query, "ch", split_axis=0, concat_axis=1, tiled=True),
        lax.all_to_all(grad_key, "ch", split_axis=0, concat_axis=1, tiled=True),
        lax.all_to_all(grad_value, "ch", split_axis=0, concat_axis=1, tiled=True),
    )
    return (query_rows, key_rows, value_rows, grad_filters)


TAPS_BLOCK = 128
CHUNK_CH = 128
LOAD_PIECES = 4
MESH = pl.DeviceIdType.MESH
NT = (((1,), (1,)), ((), ()))


def exchange_kernel(
    nctx, nch, chunks,
    query_hbm, key_hbm, value_hbm, grad_hbm, taps_ref,
    conv_ref, corr_ref, filt_ref, key_ref, value_ref, grad_ref,
    query_ref, staged, landed, back, taps, sums, toeplitz, xt, ut, yt, zt,
    in_send, in_recv, out_send, out_recv, tap_send, tap_recv, sum_send, sum_recv, local_sem, load_sem,
):
    ctx = lax.axis_index("ctx")
    ch = lax.axis_index("ch")
    ndev = nctx * nch
    me = ctx * nch + ch
    tokens = query_ref.shape[0]
    chans = query_ref.shape[1] // ndev
    groups = chans // GROUP_CH
    span = taps_ref.shape[1]
    seq = tokens * ndev
    block = TAPS_BLOCK
    nblocks = seq // block
    per_block = block // tokens
    chunk_groups = CHUNK_CH // GROUP_CH

    partners = []
    for order in range(nch):
        step = -(order + 1) // 2 if order % 2 else order // 2
        other_ch = lax.rem(ch + (nch // 2 + step) % nch, nch)
        for turn in range(1, nctx + 1):
            if (nch // 2 + step) % nch or turn < nctx:
                other_ctx = lax.rem(ctx + turn, nctx)
                partners.append((other_ctx, other_ch, other_ctx * nch + other_ch))

    def columns(owner_ctx, owner_ch, chunk):
        start = owner_ch * (nctx * chans) + owner_ctx * chans + chunk * CHUNK_CH
        return pl.ds(pl.multiple_of(start, 128), CHUNK_CH)

    def gate(cols):
        staged[0:tokens, cols] = (
            key_ref[:, cols].astype(jnp.float32) * value_ref[:, cols].astype(jnp.float32)
        ).astype(jnp.bfloat16)
        staged[tokens:, cols] = (
            grad_ref[:, cols].astype(jnp.float32) * query_ref[:, cols].astype(jnp.float32)
        ).astype(jnp.bfloat16)

    def send_in(chunk):
        for other_ctx, other_ch, other in partners:
            pltpu.make_async_remote_copy(
                src_ref=staged.at[:, columns(other_ctx, other_ch, chunk)],
                dst_ref=landed.at[chunk, me],
                send_sem=in_send.at[chunk],
                recv_sem=in_recv.at[chunk],
                device_id=(other_ctx, other_ch),
                device_id_type=MESH,
            ).start()

    def send_out(chunk):
        own = columns(ctx, ch, chunk)
        for other_ctx, other_ch, other in partners:
            for half, dst in ((0, conv_ref), (tokens, corr_ref)):
                pltpu.make_async_remote_copy(
                    src_ref=back.at[chunk, other, pl.ds(half, tokens)],
                    dst_ref=dst.at[:, own],
                    send_sem=out_send.at[chunk],
                    recv_sem=out_recv.at[chunk],
                    device_id=(other_ctx, other_ch),
                    device_id_type=MESH,
                ).start()

    def all_of(sem, chunk):
        whole = landed.at[chunk, pl.ds(0, ndev - 1)]
        pltpu.make_async_copy(whole, whole, sem.at[chunk]).wait()

    def tap_copy(step, sender):
        other = (ctx + step) % nctx
        slot = ctx if sender else other
        return pltpu.make_async_remote_copy(
            src_ref=taps_ref.at[pl.ds(pl.multiple_of(other * groups, 8), groups), :],
            dst_ref=taps.at[:, pl.ds(pl.multiple_of(slot * span, 128), span)],
            send_sem=tap_send.at[step],
            recv_sem=tap_recv.at[slot],
            device_id=(other, ch),
            device_id_type=MESH,
        )

    def sum_copy(step, sender):
        other = (ctx + step) % nctx
        slot = ctx if sender else other
        return pltpu.make_async_remote_copy(
            src_ref=sums.at[:, pl.ds(pl.multiple_of(other * span, 128), span)],
            dst_ref=filt_ref.at[pl.ds(pl.multiple_of(slot * groups, 8), groups), :],
            send_sem=sum_send.at[step],
            recv_sem=sum_recv.at[slot],
            device_id=(other, ch),
            device_id_type=MESH,
        )

    def own_in(chunk):
        return pltpu.make_async_copy(
            staged.at[:, columns(ctx, ch, chunk)], landed.at[chunk, me], local_sem.at[chunk]
        )

    def own_out(chunk, half):
        dst = (conv_ref, corr_ref)[half]
        return pltpu.make_async_copy(
            back.at[chunk, me, pl.ds(half * tokens, tokens)],
            dst.at[:, columns(ctx, ch, chunk)],
            local_sem.at[chunks + 2 * chunk + half],
        )

    def each(count, body, unroll=1):
        def step(n, carry):
            body(n)
            return carry

        lax.fori_loop(0, count, step, 0, unroll=unroll)

    pieces = LOAD_PIECES
    piece = nctx * nch * chans // pieces

    def load(which, part):
        src, dst = (
            (query_hbm, query_ref),
            (key_hbm, key_ref),
            (value_hbm, value_ref),
            (grad_hbm, grad_ref),
        )[which]
        cols = pl.ds(part * piece, piece)
        return pltpu.make_async_copy(src.at[:, cols], dst.at[:, cols], load_sem.at[which, part])

    for part in range(pieces):
        for which in range(4):
            load(which, part).start()

    barrier = pltpu.get_barrier_semaphore()

    for other_ctx, other_ch, _ in partners:
        pl.semaphore_signal(barrier, inc=1, device_id=(other_ctx, other_ch), device_id_type=MESH)

    def gate_chunk(chunk, first, count):
        each(
            count,
            lambda n: gate(
                pl.ds(pl.multiple_of((first + n) * chans + chunk * CHUNK_CH, 128), CHUNK_CH)
            ),
            unroll=4,
        )

    own_taps = pltpu.make_async_copy(
        taps_ref.at[pl.ds(pl.multiple_of(ctx * groups, 8), groups), :],
        taps.at[:, pl.ds(pl.multiple_of(ctx * span, 128), span)],
        local_sem.at[3 * chunks],
    )
    own_taps.start()
    for part in range(pieces):
        for which in range(4):
            load(which, part).wait()
        gate_chunk(0, part * (ndev // pieces), ndev // pieces)
    pl.semaphore_wait(barrier, ndev - 1)
    for step in range(1, nctx):
        tap_copy(step, True).start()
    send_in(0)
    own_in(0).start()
    for chunk in range(1, chunks):
        gate_chunk(chunk, 0, ndev)
        send_in(chunk)
        own_in(chunk).start()
    own_taps.wait()
    for step in range(1, nctx):
        tap_copy(step, False).wait_recv()

    row_id = lax.broadcasted_iota(jnp.int32, (block, block), 0)
    col_id = lax.broadcasted_iota(jnp.int32, (block, block), 1)
    flip = (row_id + col_id == block - 1).astype(jnp.bfloat16)
    zeros = jnp.zeros((block, block), jnp.bfloat16)
    width = block + seq

    def slide(values, shift):
        return pltpu.roll(values, shift, 1, stride=1, stride_axis=0)[:, block:]

    def later(stack):
        padded = jnp.concatenate([stack, zeros], axis=0)
        return jnp.concatenate(
            [padded[k * GROUP_CH : k * GROUP_CH + block] for k in range(nblocks)], axis=1
        )

    def earlier(stack):
        padded = jnp.concatenate([zeros, stack], axis=0)
        return jnp.concatenate(
            [padded[block - k * GROUP_CH : 2 * block - k * GROUP_CH] for k in range(nblocks)],
            axis=1,
        )

    def turn_in(chunk):
        for i in range(nblocks):
            src = pl.ds(i * per_block, per_block)
            for rows, dst in ((pl.ds(0, tokens), xt), (pl.ds(tokens, tokens), ut)):
                tile = landed[chunk, src, rows, :].reshape(block, CHUNK_CH)
                dst[chunk, :, i] = tile.T.reshape(chunk_groups, GROUP_CH, block)

    def build(group):
        row = taps[pl.ds(group, 1), :]
        row = jnp.concatenate([jnp.zeros((1, block), jnp.float32), row], axis=1)
        wide = slide(jnp.broadcast_to(row, (block, width)), 0)
        high = wide.astype(jnp.bfloat16)
        low = (wide - high.astype(jnp.float32)).astype(jnp.bfloat16)
        for which, part in ((0, high), (1, low)):
            for k in range(nblocks):
                toeplitz[group, which, k] = part[:, k * block : (k + 1) * block]

    def convolve(chunk, g):
        x_cat = earlier(xt[chunk, g].reshape(block, block))
        u_cat = later(ut[chunk, g].reshape(block, block))
        conv = jnp.zeros((block, block), jnp.float32)
        corr = jnp.zeros((block, block), jnp.float32)
        for which in range(2):
            part = toeplitz[chunk * chunk_groups + g, which]
            tall = part.reshape(nblocks * block, block)
            flat = jnp.concatenate([part[k] for k in range(nblocks)], axis=1)
            conv = conv + jnp.dot(x_cat, tall, preferred_element_type=jnp.float32)
            corr = corr + lax.dot_general(u_cat, flat, NT, preferred_element_type=jnp.float32)
        yt[:, pl.ds(pl.multiple_of(g * GROUP_CH, GROUP_CH), GROUP_CH), :] = (
            conv.astype(jnp.bfloat16).reshape(nblocks, GROUP_CH, block)
        )
        zt[:, pl.ds(pl.multiple_of(g * GROUP_CH, GROUP_CH), GROUP_CH), :] = (
            corr.astype(jnp.bfloat16).reshape(nblocks, GROUP_CH, block)
        )

    def turn_out(chunk):
        for i in range(nblocks):
            dst = pl.ds(i * per_block, per_block)
            back[chunk, dst, 0:tokens, :] = yt[i].T.reshape(per_block, tokens, CHUNK_CH)
            back[chunk, dst, tokens:, :] = zt[i].T.reshape(per_block, tokens, CHUNK_CH)

    def correlate(chunk, g):
        stack_x = xt[chunk, g].reshape(block, block)
        u_cat = later(ut[chunk, g].reshape(block, block))
        turned = lax.dot_general(
            flip, stack_x, NT, preferred_element_type=jnp.float32
        ).astype(jnp.bfloat16)
        pairs = jnp.dot(turned, u_cat, preferred_element_type=jnp.float32)
        pairs = jnp.concatenate([pairs, jnp.zeros((block, block), jnp.float32)], axis=1)
        total = jnp.sum(slide(pairs, 1), axis=0, keepdims=True)
        sums[pl.ds(chunk * chunk_groups + g, 1), :] = total

    each(groups, build, unroll=2)
    for chunk in range(chunks):
        own_in(chunk).wait()
        all_of(in_recv, chunk)
        turn_in(chunk)
        each(chunk_groups, lambda g: convolve(chunk, g), unroll=2)
        turn_out(chunk)
        send_out(chunk)
        own_out(chunk, 0).start()
        own_out(chunk, 1).start()

    for chunk in range(chunks):
        each(chunk_groups, lambda g: correlate(chunk, g), unroll=2)

    for step in range(1, nctx):
        sum_copy(step, True).start()
    own_sums = pltpu.make_async_copy(
        sums.at[:, pl.ds(pl.multiple_of(ctx * span, 128), span)],
        filt_ref.at[pl.ds(pl.multiple_of(ctx * groups, 8), groups), :],
        local_sem.at[3 * chunks + 1],
    )
    own_sums.start()

    for step in range(1, nctx):
        tap_copy(step, True).wait_send()
    for chunk in range(chunks):
        all_of(in_send, chunk)
        all_of(out_send, chunk)
        all_of(out_recv, chunk)
        own_out(chunk, 0).wait()
        own_out(chunk, 1).wait()
    for step in range(1, nctx):
        sum_copy(step, True).wait_send()
        sum_copy(step, False).wait_recv()
    own_sums.wait()


def one_exchange(nctx, nch, query_gate, key_gate, value_proj, grad_out, long_filters):
    tokens, model = query_gate.shape
    ndev = nctx * nch
    chans = model // ndev
    groups = chans // GROUP_CH
    chunks = chans // CHUNK_CH
    seq = tokens * ndev
    nblocks = seq // TAPS_BLOCK
    chunk_groups = CHUNK_CH // GROUP_CH
    vmem = pl.BlockSpec(memory_space=pltpu.VMEM)
    half = jnp.bfloat16
    sem = pltpu.SemaphoreType.DMA
    convolved, correlated, grad_filters, key_near, value_near, grad_near = pl.pallas_call(
        functools.partial(exchange_kernel, nctx, nch, chunks),
        out_shape=(
            jax.ShapeDtypeStruct((tokens, model), half),
            jax.ShapeDtypeStruct((tokens, model), half),
            jax.ShapeDtypeStruct(long_filters.shape, jnp.float32),
        )
        + (jax.ShapeDtypeStruct((tokens, model), half),) * 3,
        in_specs=[pl.BlockSpec(memory_space=pltpu.HBM)] * 4 + [vmem],
        out_specs=(vmem,) * 6,
        scratch_shapes=[
            pltpu.VMEM((tokens, model), half),
            pltpu.VMEM((2 * tokens, model), half),
            pltpu.VMEM((chunks, ndev, 2 * tokens, CHUNK_CH), half),
            pltpu.VMEM((chunks, ndev, 2 * tokens, CHUNK_CH), half),
            pltpu.VMEM((groups, seq), jnp.float32),
            pltpu.VMEM((groups, seq), jnp.float32),
            pltpu.VMEM((groups, 2, nblocks, TAPS_BLOCK, TAPS_BLOCK), half),
            pltpu.VMEM((chunks, chunk_groups, nblocks, GROUP_CH, TAPS_BLOCK), half),
            pltpu.VMEM((chunks, chunk_groups, nblocks, GROUP_CH, TAPS_BLOCK), half),
            pltpu.VMEM((nblocks, CHUNK_CH, TAPS_BLOCK), half),
            pltpu.VMEM((nblocks, CHUNK_CH, TAPS_BLOCK), half),
            sem((chunks,)),
            sem((chunks,)),
            sem((chunks,)),
            sem((chunks,)),
            sem((nctx,)),
            sem((nctx,)),
            sem((nctx,)),
            sem((nctx,)),
            sem((3 * chunks + 2,)),
            sem((4, LOAD_PIECES)),
        ],
        compiler_params=pltpu.CompilerParams(
            collective_id=0, has_side_effects=True, vmem_limit_bytes=51 * 1024 * 1024
        ),
        name="exchange_and_convolve",
    )(query_gate, key_gate, value_proj, grad_out, long_filters)
    convolved = convolved.astype(jnp.float32)
    correlated = correlated.astype(jnp.float32)
    return (
        (grad_near.astype(jnp.float32) * convolved).astype(half),
        (correlated * value_near.astype(jnp.float32)).astype(half),
        (correlated * key_near.astype(jnp.float32)).astype(half),
        grad_filters,
    )


def fits_one_exchange(nctx, nch, query_shape, filter_shape):
    tokens, model = query_shape
    ndev = nctx * nch
    return (
        model % (ndev * CHUNK_CH) == 0
        and tokens % 16 == 0
        and TAPS_BLOCK % tokens == 0
        and tokens * ndev == TAPS_BLOCK * (TAPS_BLOCK // GROUP_CH)
        and filter_shape[1] % 128 == 0
        and nctx * filter_shape[0] * nch * GROUP_CH == model * nctx
    )


def solution(mesh):
    nctx, nch = mesh.shape["ctx"], mesh.shape["ch"]

    def local(query_gate, key_gate, value_proj, grad_out, long_filters):
        args = (query_gate, key_gate, value_proj, grad_out, long_filters)
        if fits_one_exchange(nctx, nch, query_gate.shape, long_filters.shape):
            return one_exchange(nctx, nch, *args)
        return on_device(*args)

    in_specs = (
        P(("ctx", "ch"), None),
        P(("ctx", "ch"), None),
        P(("ctx", "ch"), None),
        P(("ctx", "ch"), None),
        P("ch", "ctx"),
    )
    out_specs = (
        P(("ctx", "ch"), None),
        P(("ctx", "ch"), None),
        P(("ctx", "ch"), None),
        P("ch", "ctx"),
    )
    return jax.shard_map(
        local, mesh=mesh, in_specs=in_specs, out_specs=out_specs, check_vma=False
    )
```

```python
import functools
import math

import jax
import jax.numpy as jnp
from jax import lax
from jax.experimental import pallas as pl
from jax.experimental.pallas import tpu as pltpu
from jax.sharding import PartitionSpec as P

GROUP_CH = 16


HIGHEST_MODE = lax.Precision.HIGHEST
SPLIT_MODE = lax.Precision.HIGH


def passed_along(value, axis, steps):
    count = lax.axis_size(axis)
    leading, last = (max(0, -steps), min(count, count - steps))
    return lax.ppermute(value, axis, [(source, source + steps) for source in range(leading, last)])


def make_tables(block_len):
    period = 2 * block_len
    steps = lax.iota(jnp.int32, block_len)
    phase = steps[:, None] * steps[None, :] % period
    angle = phase.astype(jnp.float32) * (math.pi / block_len)
    cosine = jnp.cos(angle)
    sine = jnp.sin(angle)
    parity = 1.0 - 2.0 * (steps % 2).astype(jnp.float32)
    weights = jnp.where(steps == 0, 1.0, 2.0).astype(jnp.float32) / period
    return (
        cosine,
        -sine,
        parity,
        cosine * weights[None, :],
        -sine * weights[None, :],
        parity / period,
    )


def columns_forward(tables, values):
    return (
        jnp.dot(tables[0], values, precision=SPLIT_MODE),
        jnp.dot(tables[1], values, precision=SPLIT_MODE),
        jnp.dot(tables[2], values, precision=SPLIT_MODE),
    )


def columns_inverse(tables, real_part, imag_part, nyquist):
    return (
        jnp.dot(tables[3], real_part, precision=SPLIT_MODE)
        + jnp.dot(tables[4], imag_part, precision=SPLIT_MODE)
        + tables[5][:, None] * nyquist[None, :]
    )


def rows_forward(tables, values):
    return (
        jnp.dot(values, tables[0], precision=HIGHEST_MODE),
        jnp.dot(values, tables[1], precision=HIGHEST_MODE),
        jnp.dot(values, tables[2], precision=HIGHEST_MODE),
    )


def rows_inverse(tables, real_part, imag_part, nyquist):
    return (
        jnp.dot(real_part, tables[3].T, precision=SPLIT_MODE)
        + jnp.dot(imag_part, tables[4].T, precision=SPLIT_MODE)
        + nyquist[:, None] * tables[5][None, :]
    )


def spread_groups(rows):
    groups, block_len = rows.shape
    return jnp.broadcast_to(rows.T[:, :, None], (block_len, groups, GROUP_CH)).reshape(
        block_len, groups * GROUP_CH
    )


def spread_vector(vector):
    return jnp.broadcast_to(vector[:, None], (vector.shape[0], GROUP_CH)).reshape(-1)


def group_rows(matrix):
    block_len, chans = matrix.shape
    return matrix.reshape(block_len, chans // GROUP_CH, GROUP_CH).sum(axis=2).T


def group_vector(vector):
    return vector.reshape(-1, GROUP_CH).sum(axis=1)


def by_blocks(tables, signal, upstream, long_filters):
    block_len, chans = signal.shape
    groups = long_filters.shape[0]
    nblocks = lax.axis_size("ctx")
    own_block = lax.axis_index("ctx")
    parity = tables[2]
    prev_taps = passed_along(long_filters, "ctx", 1)
    both_re, both_im, both_ny = rows_forward(
        tables, jnp.concatenate([prev_taps, long_filters], axis=0)
    )
    own_re = both_re[:groups] + both_re[groups:] * parity
    own_im = both_im[:groups] + both_im[groups:] * parity
    own_ny = both_ny[:groups] + both_ny[groups:]
    lag_re, lag_im, lag_ny = (
        lax.all_gather(own_re[None], "ctx", axis=0, tiled=True),
        lax.all_gather(own_im[None], "ctx", axis=0, tiled=True),
        lax.all_gather(own_ny[None], "ctx", axis=0, tiled=True),
    )
    mine_re, mine_im, mine_ny = columns_forward(tables, upstream.astype(jnp.float32))
    mine_re = mine_re * parity[:, None]
    mine_im = mine_im * parity[:, None]

    def pick(lag_index):
        return (
            spread_groups(lax.dynamic_index_in_dim(lag_re, lag_index, 0, keepdims=False)),
            spread_groups(lax.dynamic_index_in_dim(lag_im, lag_index, 0, keepdims=False)),
            spread_vector(lax.dynamic_index_in_dim(lag_ny, lag_index, 0, keepdims=False)),
        )

    def add_earlier(totals, block_vals, lag_index):
        conv_re, conv_im, conv_ny, back_re, back_im, back_ny, corr_re, corr_im, corr_ny = totals
        sig_re, sig_im, sig_ny = columns_forward(tables, block_vals)
        tap_re, tap_im, tap_ny = pick(lag_index)
        conv_re = conv_re + tap_re * sig_re - tap_im * sig_im
        conv_im = conv_im + tap_re * sig_im + tap_im * sig_re
        conv_ny = conv_ny + tap_ny * sig_ny
        corr_re = corr_re.at[lag_index].add(group_rows(mine_re * sig_re + mine_im * sig_im))
        corr_im = corr_im.at[lag_index].add(group_rows(mine_im * sig_re - mine_re * sig_im))
        corr_ny = corr_ny.at[lag_index].add(group_vector(mine_ny * sig_ny))
        return (conv_re, conv_im, conv_ny, back_re, back_im, back_ny, corr_re, corr_im, corr_ny)

    def add_later(totals, block_vals, lag_index):
        conv_re, conv_im, conv_ny, back_re, back_im, back_ny, corr_re, corr_im, corr_ny = totals
        up_re, up_im, up_ny = columns_forward(tables, block_vals)
        up_re = up_re * parity[:, None]
        up_im = up_im * parity[:, None]
        tap_re, tap_im, tap_ny = pick(lag_index)
        back_re = back_re + tap_re * up_re + tap_im * up_im
        back_im = back_im + tap_re * up_im - tap_im * up_re
        back_ny = back_ny + tap_ny * up_ny
        return (conv_re, conv_im, conv_ny, back_re, back_im, back_ny, corr_re, corr_im, corr_ny)

    plane = jnp.zeros((block_len, chans), jnp.float32)
    edge = jnp.zeros((chans,), jnp.float32)
    stack = jnp.zeros((nblocks, groups, block_len), jnp.float32)
    stack_edge = jnp.zeros((nblocks, groups), jnp.float32)
    initial = (plane, plane, edge, plane, plane, edge, stack, stack, stack_edge)
    sig_piece = lax.all_gather(signal, "ctx", axis=0, tiled=True)
    up_piece = lax.all_gather(upstream, "ctx", axis=0, tiled=True)
    piece_blocks = sig_piece.shape[0] // block_len

    def one_block(offset, running):
        sig_vals = lax.dynamic_slice_in_dim(sig_piece, offset * block_len, block_len, 0).astype(
            jnp.float32
        )
        up_vals = lax.dynamic_slice_in_dim(up_piece, offset * block_len, block_len, 0).astype(
            jnp.float32
        )
        running = lax.cond(
            offset <= own_block,
            lambda current: add_earlier(current, sig_vals, own_block - offset),
            lambda current: current,
            running,
        )
        running = lax.cond(
            offset >= own_block,
            lambda current: add_later(current, up_vals, offset - own_block),
            lambda current: current,
            running,
        )
        return running

    totals = lax.fori_loop(0, piece_blocks, one_block, initial)
    conv_re, conv_im, conv_ny, back_re, back_im, back_ny, corr_re, corr_im, corr_ny = totals
    convolved = columns_inverse(
        tables, conv_re * parity[:, None], conv_im * parity[:, None], conv_ny
    )
    correlated = columns_inverse(tables, back_re, back_im, back_ny)
    total_re, total_im, total_ny = lax.psum((corr_re, corr_im, corr_ny), "ctx")
    next_block = jnp.minimum(own_block + 1, nblocks - 1)
    valid = (own_block + 1 < nblocks).astype(jnp.float32)
    cur_re = lax.dynamic_index_in_dim(total_re, own_block, 0, keepdims=False)
    cur_im = lax.dynamic_index_in_dim(total_im, own_block, 0, keepdims=False)
    cur_ny = lax.dynamic_index_in_dim(total_ny, own_block, 0, keepdims=False)
    nxt_re = lax.dynamic_index_in_dim(total_re, next_block, 0, keepdims=False)
    nxt_im = lax.dynamic_index_in_dim(total_im, next_block, 0, keepdims=False)
    nxt_ny = lax.dynamic_index_in_dim(total_ny, next_block, 0, keepdims=False)
    upper = rows_inverse(tables, cur_re * parity, cur_im * parity, cur_ny)
    lower = rows_inverse(tables, nxt_re, nxt_im, nxt_ny)
    grad_filters = upper + lower * valid
    return (convolved, correlated, grad_filters)


def on_device(query_gate, key_gate, value_proj, grad_out, long_filters):
    query_cols, key_cols, value_cols, grad_cols = (
        lax.all_to_all(query_gate, "ch", split_axis=1, concat_axis=0, tiled=True),
        lax.all_to_all(key_gate, "ch", split_axis=1, concat_axis=0, tiled=True),
        lax.all_to_all(value_proj, "ch", split_axis=1, concat_axis=0, tiled=True),
        lax.all_to_all(grad_out, "ch", split_axis=1, concat_axis=0, tiled=True),
    )
    query_vals = query_cols.astype(jnp.float32)
    key_vals = key_cols.astype(jnp.float32)
    value_vals = value_cols.astype(jnp.float32)
    grad_vals = grad_cols.astype(jnp.float32)
    signal = (key_vals * value_vals).astype(jnp.bfloat16)
    upstream = (grad_vals * query_vals).astype(jnp.bfloat16)
    tables = make_tables(signal.shape[0])
    convolved, correlated, grad_filters = by_blocks(tables, signal, upstream, long_filters)
    conv_half = convolved.astype(jnp.bfloat16)
    corr_half = correlated.astype(jnp.bfloat16)
    conv_wide = lax.optimization_barrier(conv_half).astype(jnp.float32)
    corr_wide = lax.optimization_barrier(corr_half).astype(jnp.float32)
    grad_query = (grad_vals * conv_wide).astype(jnp.bfloat16)
    grad_key = (corr_wide * value_vals).astype(jnp.bfloat16)
    grad_value = (corr_wide * key_vals).astype(jnp.bfloat16)
    query_rows, key_rows, value_rows = (
        lax.all_to_all(grad_query, "ch", split_axis=0, concat_axis=1, tiled=True),
        lax.all_to_all(grad_key, "ch", split_axis=0, concat_axis=1, tiled=True),
        lax.all_to_all(grad_value, "ch", split_axis=0, concat_axis=1, tiled=True),
    )
    return (query_rows, key_rows, value_rows, grad_filters)


TAPS_BLOCK = 128
CHUNK_CH = 128
MESH = pl.DeviceIdType.MESH
NT = (((1,), (1,)), ((), ()))


def exchange_kernel(
    nctx, nch, chunks,
    query_hbm, key_hbm, value_hbm, grad_hbm, taps_ref,
    conv_ref, corr_ref, filt_ref, key_ref, value_ref, grad_ref,
    query_ref, staged, landed, back, taps, sums, toeplitz, turned, result,
    in_send, in_recv, out_send, out_recv, tap_send, tap_recv, sum_send, sum_recv, local_sem, load_sem,
):
    ctx = lax.axis_index("ctx")
    ch = lax.axis_index("ch")
    ndev = nctx * nch
    me = ctx * nch + ch
    tokens = query_ref.shape[0]
    chans = query_ref.shape[1] // ndev
    groups = chans // GROUP_CH
    span = taps_ref.shape[1]
    seq = tokens * ndev
    block = TAPS_BLOCK
    nblocks = seq // block
    per_block = block // tokens
    chunk_groups = CHUNK_CH // GROUP_CH
    phases = 2 * chunks

    rounds = []
    for order in range(nch):
        step = -(order + 1) // 2 if order % 2 else order // 2
        offset = (nch // 2 + step) % nch
        other_ch = lax.rem(ch + offset, nch)
        turns = []
        for turn in range(1, nctx + 1):
            if offset or turn < nctx:
                other_ctx = lax.rem(ctx + turn, nctx)
                turns.append((other_ctx, other_ctx * nch + other_ch))
        rounds.append((other_ch, turns))

    def columns(owner_ctx, owner_ch, chunk):
        start = owner_ch * (nctx * chans) + owner_ctx * chans + chunk * CHUNK_CH
        return pl.ds(pl.multiple_of(start, 128), CHUNK_CH)

    def gate(phase, other_ch):
        near, far = ((key_ref, value_ref), (grad_ref, query_ref))[phase % 2]
        rows = pl.ds(phase % 2 * tokens, tokens)
        for owner in range(nctx):
            cols = columns(owner, other_ch, phase // 2)
            staged[rows, cols] = (
                near[:, cols].astype(jnp.float32) * far[:, cols].astype(jnp.float32)
            ).astype(jnp.bfloat16)

    def send_in(phase, other_ch, turns):
        rows = pl.ds(phase % 2 * tokens, tokens)
        for other_ctx, _ in turns:
            pltpu.make_async_remote_copy(
                src_ref=staged.at[rows, columns(other_ctx, other_ch, phase // 2)],
                dst_ref=landed.at[phase, me],
                send_sem=in_send.at[phase],
                recv_sem=in_recv.at[phase],
                device_id=(other_ctx, other_ch),
                device_id_type=MESH,
            ).start()

    def send_out(phase):
        own = columns(ctx, ch, phase // 2)
        for other_ch, turns in rounds:
            for other_ctx, other in turns:
                pltpu.make_async_remote_copy(
                    src_ref=back.at[phase, other],
                    dst_ref=(conv_ref, corr_ref)[phase % 2].at[:, own],
                    send_sem=out_send.at[phase],
                    recv_sem=out_recv.at[phase],
                    device_id=(other_ctx, other_ch),
                    device_id_type=MESH,
                ).start()

    def all_of(sem, phase):
        whole = landed.at[phase, pl.ds(0, ndev - 1)]
        pltpu.make_async_copy(whole, whole, sem.at[phase]).wait()

    def tap_copy(step, sender):
        other = (ctx + step) % nctx
        slot = ctx if sender else other
        return pltpu.make_async_remote_copy(
            src_ref=taps_ref.at[pl.ds(pl.multiple_of(other * groups, 8), groups), :],
            dst_ref=taps.at[:, pl.ds(pl.multiple_of(slot * span, 128), span)],
            send_sem=tap_send.at[step],
            recv_sem=tap_recv.at[slot],
            device_id=(other, ch),
            device_id_type=MESH,
        )

    def sum_copy(step, sender):
        other = (ctx + step) % nctx
        slot = ctx if sender else other
        return pltpu.make_async_remote_copy(
            src_ref=sums.at[:, pl.ds(pl.multiple_of(other * span, 128), span)],
            dst_ref=filt_ref.at[pl.ds(pl.multiple_of(slot * groups, 8), groups), :],
            send_sem=sum_send.at[step],
            recv_sem=sum_recv.at[slot],
            device_id=(other, ch),
            device_id_type=MESH,
        )

    def own_in(phase):
        return pltpu.make_async_copy(
            staged.at[pl.ds(phase % 2 * tokens, tokens), columns(ctx, ch, phase // 2)],
            landed.at[phase, me],
            local_sem.at[phase],
        )

    def own_out(phase):
        return pltpu.make_async_copy(
            back.at[phase, me],
            (conv_ref, corr_ref)[phase % 2].at[:, columns(ctx, ch, phase // 2)],
            local_sem.at[phases + phase],
        )

    def each(count, body, unroll=1):
        def step(n, carry):
            body(n)
            return carry

        lax.fori_loop(0, count, step, 0, unroll=unroll)

    def load(which, order):
        src, dst = (
            (key_hbm, key_ref),
            (value_hbm, value_ref),
            (grad_hbm, grad_ref),
            (query_hbm, query_ref),
        )[which]
        piece = nctx * chans
        cols = pl.ds(pl.multiple_of(rounds[order][0] * piece, 128), piece)
        return pltpu.make_async_copy(src.at[:, cols], dst.at[:, cols], load_sem.at[which, order])

    barrier = pltpu.get_barrier_semaphore()
    for other_ch, turns in rounds:
        for other_ctx, _ in turns:
            pl.semaphore_signal(
                barrier, inc=1, device_id=(other_ctx, other_ch), device_id_type=MESH
            )
    for kind in range(2):
        for order in range(nch):
            load(2 * kind, order).start()
            load(2 * kind + 1, order).start()
    own_taps = pltpu.make_async_copy(
        taps_ref.at[pl.ds(pl.multiple_of(ctx * groups, 8), groups), :],
        taps.at[:, pl.ds(pl.multiple_of(ctx * span, 128), span)],
        local_sem.at[2 * phases],
    )
    own_taps.start()
    for phase in range(phases):
        for order, (other_ch, turns) in enumerate(rounds):
            if phase < 2:
                load(2 * phase, order).wait()
                load(2 * phase + 1, order).wait()
            gate(phase, other_ch)
            if phase == 0 and order == 0:
                pl.semaphore_wait(barrier, ndev - 1)
                for step in range(1, nctx):
                    tap_copy(step, True).start()
            send_in(phase, other_ch, turns)
        own_in(phase).start()
    own_taps.wait()
    for step in range(1, nctx):
        tap_copy(step, False).wait_recv()

    row_id = lax.broadcasted_iota(jnp.int32, (block, block), 0)
    col_id = lax.broadcasted_iota(jnp.int32, (block, block), 1)
    flip = (row_id + col_id == block - 1).astype(jnp.bfloat16)
    zeros = jnp.zeros((block, block), jnp.bfloat16)
    width = block + seq

    def slide(values, shift):
        return pltpu.roll(values, shift, 1, stride=1, stride_axis=0)[:, block:]

    def later(stack):
        padded = jnp.concatenate([stack, zeros], axis=0)
        return jnp.concatenate(
            [padded[k * GROUP_CH : k * GROUP_CH + block] for k in range(nblocks)], axis=1
        )

    def turn_in(phase):
        for i in range(nblocks):
            tile = landed[phase, pl.ds(i * per_block, per_block)].reshape(block, CHUNK_CH)
            turned[phase, :, i] = tile.T.reshape(chunk_groups, GROUP_CH, block)

    def build(group):
        row = taps[pl.ds(group, 1), :]
        row = jnp.concatenate([jnp.zeros((1, block), jnp.float32), row], axis=1)
        wide = slide(jnp.broadcast_to(row, (block, width)), 0)
        high = wide.astype(jnp.bfloat16)
        low = (wide - high.astype(jnp.float32)).astype(jnp.bfloat16)
        for which, part in ((0, high), (1, low)):
            for k in range(nblocks):
                toeplitz[group, which, k] = part[:, k * block : (k + 1) * block]

    def convolve(phase, g):
        stack = turned[phase, g].reshape(block, block)
        edge = jnp.zeros((GROUP_CH, block), jnp.bfloat16)
        group = phase // 2 * chunk_groups + g
        total = None
        for pair in range(nblocks // 2):
            cut = 2 * pair * GROUP_CH
            high, low = [
                [toeplitz[group, which, 2 * pair + k] for k in range(2)] for which in range(2)
            ]
            if phase % 2 == 0:
                shifted = jnp.concatenate([edge, stack[: block - cut - GROUP_CH]], axis=0)
                left = jnp.concatenate([stack[: block - cut], shifted], axis=1)
                right = jnp.concatenate(
                    [jnp.concatenate(high, axis=0), jnp.concatenate(low, axis=0)], axis=1
                )
                both = jnp.dot(left, right, preferred_element_type=jnp.float32)
            else:
                shifted = jnp.concatenate([stack[cut + GROUP_CH :], edge], axis=0)
                left = jnp.concatenate([stack[cut:], shifted], axis=1)
                right = jnp.concatenate(
                    [jnp.concatenate(high, axis=1), jnp.concatenate(low, axis=1)], axis=0
                )
                both = lax.dot_general(left, right, NT, preferred_element_type=jnp.float32)
            part = both[:, :block] + both[:, block:]
            if pair:
                blank = jnp.zeros((cut, block), jnp.float32)
                part = jnp.concatenate([blank, part] if phase % 2 == 0 else [part, blank], axis=0)
                total = total + part
            else:
                total = part
        result[phase % 2, :, pl.ds(pl.multiple_of(g * GROUP_CH, GROUP_CH), GROUP_CH), :] = (
            total.astype(jnp.bfloat16).reshape(nblocks, GROUP_CH, block)
        )

    def turn_out(phase):
        for i in range(nblocks):
            back[phase, pl.ds(i * per_block, per_block)] = result[phase % 2, i].T.reshape(
                per_block, tokens, CHUNK_CH
            )

    def correlate(chunk, g):
        stack_x = turned[2 * chunk, g].reshape(block, block)
        u_cat = later(turned[2 * chunk + 1, g].reshape(block, block))
        mirrored = lax.dot_general(
            flip, stack_x, NT, preferred_element_type=jnp.float32
        ).astype(jnp.bfloat16)
        pairs = jnp.dot(mirrored, u_cat, preferred_element_type=jnp.float32)
        pairs = jnp.concatenate([pairs, jnp.zeros((block, block), jnp.float32)], axis=1)
        total = jnp.sum(slide(pairs, 1), axis=0, keepdims=True)
        sums[pl.ds(chunk * chunk_groups + g, 1), :] = total

    each(groups, build, unroll=2)
    for phase in range(phases):
        own_in(phase).wait()
        all_of(in_recv, phase)
        turn_in(phase)
        each(chunk_groups, lambda g: convolve(phase, g), unroll=2)
        turn_out(phase)
        send_out(phase)
        own_out(phase).start()

    for chunk in range(chunks):
        each(chunk_groups, lambda g: correlate(chunk, g), unroll=2)

    for step in range(1, nctx):
        sum_copy(step, True).start()
    own_sums = pltpu.make_async_copy(
        sums.at[:, pl.ds(pl.multiple_of(ctx * span, 128), span)],
        filt_ref.at[pl.ds(pl.multiple_of(ctx * groups, 8), groups), :],
        local_sem.at[2 * phases + 1],
    )
    own_sums.start()

    for step in range(1, nctx):
        tap_copy(step, True).wait_send()
    for phase in range(phases):
        all_of(in_send, phase)
        all_of(out_send, phase)
        all_of(out_recv, phase)
        own_out(phase).wait()
    for step in range(1, nctx):
        sum_copy(step, True).wait_send()
        sum_copy(step, False).wait_recv()
    own_sums.wait()


def one_exchange(nctx, nch, query_gate, key_gate, value_proj, grad_out, long_filters):
    tokens, model = query_gate.shape
    ndev = nctx * nch
    chans = model // ndev
    groups = chans // GROUP_CH
    chunks = chans // CHUNK_CH
    seq = tokens * ndev
    nblocks = seq // TAPS_BLOCK
    chunk_groups = CHUNK_CH // GROUP_CH
    vmem = pl.BlockSpec(memory_space=pltpu.VMEM)
    half = jnp.bfloat16
    sem = pltpu.SemaphoreType.DMA
    convolved, correlated, grad_filters, key_near, value_near, grad_near = pl.pallas_call(
        functools.partial(exchange_kernel, nctx, nch, chunks),
        out_shape=(
            jax.ShapeDtypeStruct((tokens, model), half),
            jax.ShapeDtypeStruct((tokens, model), half),
            jax.ShapeDtypeStruct(long_filters.shape, jnp.float32),
        )
        + (jax.ShapeDtypeStruct((tokens, model), half),) * 3,
        in_specs=[pl.BlockSpec(memory_space=pltpu.HBM)] * 5,
        out_specs=(vmem,) * 6,
        scratch_shapes=[
            pltpu.VMEM((tokens, model), half),
            pltpu.VMEM((2 * tokens, model), half),
            pltpu.VMEM((2 * chunks, ndev, tokens, CHUNK_CH), half),
            pltpu.VMEM((2 * chunks, ndev, tokens, CHUNK_CH), half),
            pltpu.VMEM((groups, seq), jnp.float32),
            pltpu.VMEM((groups, seq), jnp.float32),
            pltpu.VMEM((groups, 2, nblocks, TAPS_BLOCK, TAPS_BLOCK), half),
            pltpu.VMEM((2 * chunks, chunk_groups, nblocks, GROUP_CH, TAPS_BLOCK), half),
            pltpu.VMEM((2, nblocks, CHUNK_CH, TAPS_BLOCK), half),
            sem((2 * chunks,)),
            sem((2 * chunks,)),
            sem((2 * chunks,)),
            sem((2 * chunks,)),
            sem((nctx,)),
            sem((nctx,)),
            sem((nctx,)),
            sem((nctx,)),
            sem((4 * chunks + 2,)),
            sem((4, nch)),
        ],
        compiler_params=pltpu.CompilerParams(
            collective_id=0, has_side_effects=True, vmem_limit_bytes=51 * 1024 * 1024
        ),
        name="exchange_and_convolve",
    )(query_gate, key_gate, value_proj, grad_out, long_filters)
    convolved = convolved.astype(jnp.float32)
    correlated = correlated.astype(jnp.float32)
    return (
        (grad_near.astype(jnp.float32) * convolved).astype(half),
        (correlated * value_near.astype(jnp.float32)).astype(half),
        (correlated * key_near.astype(jnp.float32)).astype(half),
        grad_filters,
    )


def fits_one_exchange(nctx, nch, query_shape, filter_shape):
    tokens, model = query_shape
    ndev = nctx * nch
    return (
        model % (ndev * CHUNK_CH) == 0
        and tokens % 16 == 0
        and TAPS_BLOCK % tokens == 0
        and tokens * ndev == TAPS_BLOCK * (TAPS_BLOCK // GROUP_CH)
        and filter_shape[1] % 128 == 0
        and nctx * filter_shape[0] * nch * GROUP_CH == model * nctx
    )


def solution(mesh):
    nctx, nch = mesh.shape["ctx"], mesh.shape["ch"]

    def local(query_gate, key_gate, value_proj, grad_out, long_filters):
        args = (query_gate, key_gate, value_proj, grad_out, long_filters)
        if fits_one_exchange(nctx, nch, query_gate.shape, long_filters.shape):
            return one_exchange(nctx, nch, *args)
        return on_device(*args)

    in_specs = (
        P(("ctx", "ch"), None),
        P(("ctx", "ch"), None),
        P(("ctx", "ch"), None),
        P(("ctx", "ch"), None),
        P("ch", "ctx"),
    )
    out_specs = (
        P(("ctx", "ch"), None),
        P(("ctx", "ch"), None),
        P(("ctx", "ch"), None),
        P("ch", "ctx"),
    )
    return jax.shard_map(
        local, mesh=mesh, in_specs=in_specs, out_specs=out_specs, check_vma=False
    )
```

```python
import functools
import math

import jax
import jax.numpy as jnp
from jax import lax
from jax.experimental import pallas as pl
from jax.experimental.pallas import tpu as pltpu
from jax.sharding import PartitionSpec as P

GROUP_CH = 16


HIGHEST_MODE = lax.Precision.HIGHEST
SPLIT_MODE = lax.Precision.HIGH


def passed_along(value, axis, steps):
    count = lax.axis_size(axis)
    leading, last = (max(0, -steps), min(count, count - steps))
    return lax.ppermute(value, axis, [(source, source + steps) for source in range(leading, last)])


def make_tables(block_len):
    period = 2 * block_len
    steps = lax.iota(jnp.int32, block_len)
    phase = steps[:, None] * steps[None, :] % period
    angle = phase.astype(jnp.float32) * (math.pi / block_len)
    cosine = jnp.cos(angle)
    sine = jnp.sin(angle)
    parity = 1.0 - 2.0 * (steps % 2).astype(jnp.float32)
    weights = jnp.where(steps == 0, 1.0, 2.0).astype(jnp.float32) / period
    return (
        cosine,
        -sine,
        parity,
        cosine * weights[None, :],
        -sine * weights[None, :],
        parity / period,
    )


def columns_forward(tables, values):
    return (
        jnp.dot(tables[0], values, precision=SPLIT_MODE),
        jnp.dot(tables[1], values, precision=SPLIT_MODE),
        jnp.dot(tables[2], values, precision=SPLIT_MODE),
    )


def columns_inverse(tables, real_part, imag_part, nyquist):
    return (
        jnp.dot(tables[3], real_part, precision=SPLIT_MODE)
        + jnp.dot(tables[4], imag_part, precision=SPLIT_MODE)
        + tables[5][:, None] * nyquist[None, :]
    )


def rows_forward(tables, values):
    return (
        jnp.dot(values, tables[0], precision=HIGHEST_MODE),
        jnp.dot(values, tables[1], precision=HIGHEST_MODE),
        jnp.dot(values, tables[2], precision=HIGHEST_MODE),
    )


def rows_inverse(tables, real_part, imag_part, nyquist):
    return (
        jnp.dot(real_part, tables[3].T, precision=SPLIT_MODE)
        + jnp.dot(imag_part, tables[4].T, precision=SPLIT_MODE)
        + nyquist[:, None] * tables[5][None, :]
    )


def spread_groups(rows):
    groups, block_len = rows.shape
    return jnp.broadcast_to(rows.T[:, :, None], (block_len, groups, GROUP_CH)).reshape(
        block_len, groups * GROUP_CH
    )


def spread_vector(vector):
    return jnp.broadcast_to(vector[:, None], (vector.shape[0], GROUP_CH)).reshape(-1)


def group_rows(matrix):
    block_len, chans = matrix.shape
    return matrix.reshape(block_len, chans // GROUP_CH, GROUP_CH).sum(axis=2).T


def group_vector(vector):
    return vector.reshape(-1, GROUP_CH).sum(axis=1)


def by_blocks(tables, signal, upstream, long_filters):
    block_len, chans = signal.shape
    groups = long_filters.shape[0]
    nblocks = lax.axis_size("ctx")
    own_block = lax.axis_index("ctx")
    parity = tables[2]
    prev_taps = passed_along(long_filters, "ctx", 1)
    both_re, both_im, both_ny = rows_forward(
        tables, jnp.concatenate([prev_taps, long_filters], axis=0)
    )
    own_re = both_re[:groups] + both_re[groups:] * parity
    own_im = both_im[:groups] + both_im[groups:] * parity
    own_ny = both_ny[:groups] + both_ny[groups:]
    lag_re, lag_im, lag_ny = (
        lax.all_gather(own_re[None], "ctx", axis=0, tiled=True),
        lax.all_gather(own_im[None], "ctx", axis=0, tiled=True),
        lax.all_gather(own_ny[None], "ctx", axis=0, tiled=True),
    )
    mine_re, mine_im, mine_ny = columns_forward(tables, upstream.astype(jnp.float32))
    mine_re = mine_re * parity[:, None]
    mine_im = mine_im * parity[:, None]

    def pick(lag_index):
        return (
            spread_groups(lax.dynamic_index_in_dim(lag_re, lag_index, 0, keepdims=False)),
            spread_groups(lax.dynamic_index_in_dim(lag_im, lag_index, 0, keepdims=False)),
            spread_vector(lax.dynamic_index_in_dim(lag_ny, lag_index, 0, keepdims=False)),
        )

    def add_earlier(totals, block_vals, lag_index):
        conv_re, conv_im, conv_ny, back_re, back_im, back_ny, corr_re, corr_im, corr_ny = totals
        sig_re, sig_im, sig_ny = columns_forward(tables, block_vals)
        tap_re, tap_im, tap_ny = pick(lag_index)
        conv_re = conv_re + tap_re * sig_re - tap_im * sig_im
        conv_im = conv_im + tap_re * sig_im + tap_im * sig_re
        conv_ny = conv_ny + tap_ny * sig_ny
        corr_re = corr_re.at[lag_index].add(group_rows(mine_re * sig_re + mine_im * sig_im))
        corr_im = corr_im.at[lag_index].add(group_rows(mine_im * sig_re - mine_re * sig_im))
        corr_ny = corr_ny.at[lag_index].add(group_vector(mine_ny * sig_ny))
        return (conv_re, conv_im, conv_ny, back_re, back_im, back_ny, corr_re, corr_im, corr_ny)

    def add_later(totals, block_vals, lag_index):
        conv_re, conv_im, conv_ny, back_re, back_im, back_ny, corr_re, corr_im, corr_ny = totals
        up_re, up_im, up_ny = columns_forward(tables, block_vals)
        up_re = up_re * parity[:, None]
        up_im = up_im * parity[:, None]
        tap_re, tap_im, tap_ny = pick(lag_index)
        back_re = back_re + tap_re * up_re + tap_im * up_im
        back_im = back_im + tap_re * up_im - tap_im * up_re
        back_ny = back_ny + tap_ny * up_ny
        return (conv_re, conv_im, conv_ny, back_re, back_im, back_ny, corr_re, corr_im, corr_ny)

    plane = jnp.zeros((block_len, chans), jnp.float32)
    edge = jnp.zeros((chans,), jnp.float32)
    stack = jnp.zeros((nblocks, groups, block_len), jnp.float32)
    stack_edge = jnp.zeros((nblocks, groups), jnp.float32)
    initial = (plane, plane, edge, plane, plane, edge, stack, stack, stack_edge)
    sig_piece = lax.all_gather(signal, "ctx", axis=0, tiled=True)
    up_piece = lax.all_gather(upstream, "ctx", axis=0, tiled=True)
    piece_blocks = sig_piece.shape[0] // block_len

    def one_block(offset, running):
        sig_vals = lax.dynamic_slice_in_dim(sig_piece, offset * block_len, block_len, 0).astype(
            jnp.float32
        )
        up_vals = lax.dynamic_slice_in_dim(up_piece, offset * block_len, block_len, 0).astype(
            jnp.float32
        )
        running = lax.cond(
            offset <= own_block,
            lambda current: add_earlier(current, sig_vals, own_block - offset),
            lambda current: current,
            running,
        )
        running = lax.cond(
            offset >= own_block,
            lambda current: add_later(current, up_vals, offset - own_block),
            lambda current: current,
            running,
        )
        return running

    totals = lax.fori_loop(0, piece_blocks, one_block, initial)
    conv_re, conv_im, conv_ny, back_re, back_im, back_ny, corr_re, corr_im, corr_ny = totals
    convolved = columns_inverse(
        tables, conv_re * parity[:, None], conv_im * parity[:, None], conv_ny
    )
    correlated = columns_inverse(tables, back_re, back_im, back_ny)
    total_re, total_im, total_ny = lax.psum((corr_re, corr_im, corr_ny), "ctx")
    next_block = jnp.minimum(own_block + 1, nblocks - 1)
    valid = (own_block + 1 < nblocks).astype(jnp.float32)
    cur_re = lax.dynamic_index_in_dim(total_re, own_block, 0, keepdims=False)
    cur_im = lax.dynamic_index_in_dim(total_im, own_block, 0, keepdims=False)
    cur_ny = lax.dynamic_index_in_dim(total_ny, own_block, 0, keepdims=False)
    nxt_re = lax.dynamic_index_in_dim(total_re, next_block, 0, keepdims=False)
    nxt_im = lax.dynamic_index_in_dim(total_im, next_block, 0, keepdims=False)
    nxt_ny = lax.dynamic_index_in_dim(total_ny, next_block, 0, keepdims=False)
    upper = rows_inverse(tables, cur_re * parity, cur_im * parity, cur_ny)
    lower = rows_inverse(tables, nxt_re, nxt_im, nxt_ny)
    grad_filters = upper + lower * valid
    return (convolved, correlated, grad_filters)


def on_device(query_gate, key_gate, value_proj, grad_out, long_filters):
    query_cols, key_cols, value_cols, grad_cols = (
        lax.all_to_all(query_gate, "ch", split_axis=1, concat_axis=0, tiled=True),
        lax.all_to_all(key_gate, "ch", split_axis=1, concat_axis=0, tiled=True),
        lax.all_to_all(value_proj, "ch", split_axis=1, concat_axis=0, tiled=True),
        lax.all_to_all(grad_out, "ch", split_axis=1, concat_axis=0, tiled=True),
    )
    query_vals = query_cols.astype(jnp.float32)
    key_vals = key_cols.astype(jnp.float32)
    value_vals = value_cols.astype(jnp.float32)
    grad_vals = grad_cols.astype(jnp.float32)
    signal = (key_vals * value_vals).astype(jnp.bfloat16)
    upstream = (grad_vals * query_vals).astype(jnp.bfloat16)
    tables = make_tables(signal.shape[0])
    convolved, correlated, grad_filters = by_blocks(tables, signal, upstream, long_filters)
    conv_half = convolved.astype(jnp.bfloat16)
    corr_half = correlated.astype(jnp.bfloat16)
    conv_wide = lax.optimization_barrier(conv_half).astype(jnp.float32)
    corr_wide = lax.optimization_barrier(corr_half).astype(jnp.float32)
    grad_query = (grad_vals * conv_wide).astype(jnp.bfloat16)
    grad_key = (corr_wide * value_vals).astype(jnp.bfloat16)
    grad_value = (corr_wide * key_vals).astype(jnp.bfloat16)
    query_rows, key_rows, value_rows = (
        lax.all_to_all(grad_query, "ch", split_axis=0, concat_axis=1, tiled=True),
        lax.all_to_all(grad_key, "ch", split_axis=0, concat_axis=1, tiled=True),
        lax.all_to_all(grad_value, "ch", split_axis=0, concat_axis=1, tiled=True),
    )
    return (query_rows, key_rows, value_rows, grad_filters)


TAPS_BLOCK = 128
CHUNK_CH = 128
LOAD_PIECES = 4
MESH = pl.DeviceIdType.MESH
NT = (((1,), (1,)), ((), ()))


def exchange_kernel(
    nctx, nch, chunks,
    query_hbm, key_hbm, value_hbm, grad_hbm, taps_ref,
    conv_ref, corr_ref, filt_ref, key_ref, value_ref, grad_ref,
    query_ref, staged, landed, back, taps, sums, toeplitz, xt, ut, yt, zt,
    in_send, in_recv, out_send, out_recv, tap_send, tap_recv, sum_send, sum_recv, local_sem, load_sem,
):
    ctx = lax.axis_index("ctx")
    ch = lax.axis_index("ch")
    ndev = nctx * nch
    me = ctx * nch + ch
    tokens = query_ref.shape[0]
    chans = query_ref.shape[1] // ndev
    groups = chans // GROUP_CH
    span = taps_ref.shape[1]
    seq = tokens * ndev
    block = TAPS_BLOCK
    nblocks = seq // block
    per_block = block // tokens
    chunk_groups = CHUNK_CH // GROUP_CH

    offsets = []
    for order in range(nch // 2):
        far = nch // 2 + (-(order + 1) // 2 if order % 2 else order // 2)
        offsets.append((far, (far + nch // 2) % nch))
    partners = []
    for pair in offsets:
        for turn in range(1, nctx + 1):
            for offset in pair:
                if offset or turn < nctx:
                    other_ch = lax.rem(ch + offset, nch)
                    other_ctx = lax.rem(ctx + turn, nctx)
                    partners.append((other_ctx, other_ch, other_ctx * nch + other_ch))

    def columns(owner_ctx, owner_ch, chunk):
        start = owner_ch * (nctx * chans) + owner_ctx * chans + chunk * CHUNK_CH
        return pl.ds(pl.multiple_of(start, 128), CHUNK_CH)

    def gate(cols):
        staged[0:tokens, cols] = (
            key_ref[:, cols].astype(jnp.float32) * value_ref[:, cols].astype(jnp.float32)
        ).astype(jnp.bfloat16)
        staged[tokens:, cols] = (
            grad_ref[:, cols].astype(jnp.float32) * query_ref[:, cols].astype(jnp.float32)
        ).astype(jnp.bfloat16)

    def send_in(chunk):
        for other_ctx, other_ch, other in partners:
            pltpu.make_async_remote_copy(
                src_ref=staged.at[:, columns(other_ctx, other_ch, chunk)],
                dst_ref=landed.at[chunk, me],
                send_sem=in_send.at[chunk],
                recv_sem=in_recv.at[chunk],
                device_id=(other_ctx, other_ch),
                device_id_type=MESH,
            ).start()

    def send_out(chunk):
        own = columns(ctx, ch, chunk)
        for other_ctx, other_ch, other in partners:
            for half, dst in ((0, conv_ref), (tokens, corr_ref)):
                pltpu.make_async_remote_copy(
                    src_ref=back.at[chunk, other, pl.ds(half, tokens)],
                    dst_ref=dst.at[:, own],
                    send_sem=out_send.at[chunk],
                    recv_sem=out_recv.at[chunk],
                    device_id=(other_ctx, other_ch),
                    device_id_type=MESH,
                ).start()

    def all_of(sem, chunk):
        whole = landed.at[chunk, pl.ds(0, ndev - 1)]
        pltpu.make_async_copy(whole, whole, sem.at[chunk]).wait()

    def tap_copy(step, sender):
        other = (ctx + step) % nctx
        slot = ctx if sender else other
        return pltpu.make_async_remote_copy(
            src_ref=taps_ref.at[pl.ds(pl.multiple_of(other * groups, 8), groups), :],
            dst_ref=taps.at[:, pl.ds(pl.multiple_of(slot * span, 128), span)],
            send_sem=tap_send.at[step],
            recv_sem=tap_recv.at[slot],
            device_id=(other, ch),
            device_id_type=MESH,
        )

    def sum_copy(step, sender):
        other = (ctx + step) % nctx
        slot = ctx if sender else other
        return pltpu.make_async_remote_copy(
            src_ref=sums.at[:, pl.ds(pl.multiple_of(other * span, 128), span)],
            dst_ref=filt_ref.at[pl.ds(pl.multiple_of(slot * groups, 8), groups), :],
            send_sem=sum_send.at[step],
            recv_sem=sum_recv.at[slot],
            device_id=(other, ch),
            device_id_type=MESH,
        )

    def own_in(chunk):
        return pltpu.make_async_copy(
            staged.at[:, columns(ctx, ch, chunk)], landed.at[chunk, me], local_sem.at[chunk]
        )

    def own_out(chunk, half):
        dst = (conv_ref, corr_ref)[half]
        return pltpu.make_async_copy(
            back.at[chunk, me, pl.ds(half * tokens, tokens)],
            dst.at[:, columns(ctx, ch, chunk)],
            local_sem.at[chunks + 2 * chunk + half],
        )

    def each(count, body, unroll=1):
        def step(n, carry):
            body(n)
            return carry

        lax.fori_loop(0, count, step, 0, unroll=unroll)

    pieces = LOAD_PIECES
    piece = nctx * nch * chans // pieces

    def load(which, part):
        src, dst = (
            (query_hbm, query_ref),
            (key_hbm, key_ref),
            (value_hbm, value_ref),
            (grad_hbm, grad_ref),
        )[which]
        cols = pl.ds(part * piece, piece)
        return pltpu.make_async_copy(src.at[:, cols], dst.at[:, cols], load_sem.at[which, part])

    for part in range(pieces):
        for which in range(4):
            load(which, part).start()

    barrier = pltpu.get_barrier_semaphore()

    for other_ctx, other_ch, _ in partners:
        pl.semaphore_signal(barrier, inc=1, device_id=(other_ctx, other_ch), device_id_type=MESH)

    def gate_chunk(chunk, first, count):
        each(
            count,
            lambda n: gate(
                pl.ds(pl.multiple_of((first + n) * chans + chunk * CHUNK_CH, 128), CHUNK_CH)
            ),
            unroll=4,
        )

    own_taps = pltpu.make_async_copy(
        taps_ref.at[pl.ds(pl.multiple_of(ctx * groups, 8), groups), :],
        taps.at[:, pl.ds(pl.multiple_of(ctx * span, 128), span)],
        local_sem.at[3 * chunks],
    )
    own_taps.start()
    for part in range(pieces):
        for which in range(4):
            load(which, part).wait()
        gate_chunk(0, part * (ndev // pieces), ndev // pieces)
    pl.semaphore_wait(barrier, ndev - 1)
    for step in range(1, nctx):
        tap_copy(step, True).start()
    send_in(0)
    own_in(0).start()
    for chunk in range(1, chunks):
        gate_chunk(chunk, 0, ndev)
        send_in(chunk)
        own_in(chunk).start()
    own_taps.wait()
    for step in range(1, nctx):
        tap_copy(step, False).wait_recv()

    row_id = lax.broadcasted_iota(jnp.int32, (block, block), 0)
    col_id = lax.broadcasted_iota(jnp.int32, (block, block), 1)
    flip = (row_id + col_id == block - 1).astype(jnp.bfloat16)
    zeros = jnp.zeros((block, block), jnp.bfloat16)
    width = block + seq

    def slide(values, shift):
        return pltpu.roll(values, shift, 1, stride=1, stride_axis=0)[:, block:]

    def later(stack):
        padded = jnp.concatenate([stack, zeros], axis=0)
        return jnp.concatenate(
            [padded[k * GROUP_CH : k * GROUP_CH + block] for k in range(nblocks)], axis=1
        )

    def earlier(stack):
        padded = jnp.concatenate([zeros, stack], axis=0)
        return jnp.concatenate(
            [padded[block - k * GROUP_CH : 2 * block - k * GROUP_CH] for k in range(nblocks)],
            axis=1,
        )

    def turn_in(chunk):
        for i in range(nblocks):
            src = pl.ds(i * per_block, per_block)
            for rows, dst in ((pl.ds(0, tokens), xt), (pl.ds(tokens, tokens), ut)):
                tile = landed[chunk, src, rows, :].reshape(block, CHUNK_CH)
                dst[chunk, :, i] = tile.T.reshape(chunk_groups, GROUP_CH, block)

    def build(group):
        row = taps[pl.ds(group, 1), :]
        row = jnp.concatenate([jnp.zeros((1, block), jnp.float32), row], axis=1)
        wide = slide(jnp.broadcast_to(row, (block, width)), 0)
        high = wide.astype(jnp.bfloat16)
        low = (wide - high.astype(jnp.float32)).astype(jnp.bfloat16)
        for which, part in ((0, high), (1, low)):
            for k in range(nblocks):
                toeplitz[group, which, k] = part[:, k * block : (k + 1) * block]

    def convolve(chunk, g):
        x_cat = earlier(xt[chunk, g].reshape(block, block))
        u_cat = later(ut[chunk, g].reshape(block, block))
        conv = jnp.zeros((block, block), jnp.float32)
        corr = jnp.zeros((block, block), jnp.float32)
        for which in range(2):
            part = toeplitz[chunk * chunk_groups + g, which]
            tall = part.reshape(nblocks * block, block)
            flat = jnp.concatenate([part[k] for k in range(nblocks)], axis=1)
            conv = conv + jnp.dot(x_cat, tall, preferred_element_type=jnp.float32)
            corr = corr + lax.dot_general(u_cat, flat, NT, preferred_element_type=jnp.float32)
        yt[:, pl.ds(pl.multiple_of(g * GROUP_CH, GROUP_CH), GROUP_CH), :] = (
            conv.astype(jnp.bfloat16).reshape(nblocks, GROUP_CH, block)
        )
        zt[:, pl.ds(pl.multiple_of(g * GROUP_CH, GROUP_CH), GROUP_CH), :] = (
            corr.astype(jnp.bfloat16).reshape(nblocks, GROUP_CH, block)
        )

    def turn_out(chunk):
        for i in range(nblocks):
            dst = pl.ds(i * per_block, per_block)
            back[chunk, dst, 0:tokens, :] = yt[i].T.reshape(per_block, tokens, CHUNK_CH)
            back[chunk, dst, tokens:, :] = zt[i].T.reshape(per_block, tokens, CHUNK_CH)

    def correlate(chunk, g):
        stack_x = xt[chunk, g].reshape(block, block)
        u_cat = later(ut[chunk, g].reshape(block, block))
        turned = lax.dot_general(
            flip, stack_x, NT, preferred_element_type=jnp.float32
        ).astype(jnp.bfloat16)
        pairs = jnp.dot(turned, u_cat, preferred_element_type=jnp.float32)
        pairs = jnp.concatenate([pairs, jnp.zeros((block, block), jnp.float32)], axis=1)
        total = jnp.sum(slide(pairs, 1), axis=0, keepdims=True)
        sums[pl.ds(chunk * chunk_groups + g, 1), :] = total

    each(groups, build, unroll=2)
    for chunk in range(chunks):
        own_in(chunk).wait()
        all_of(in_recv, chunk)
        turn_in(chunk)
        each(chunk_groups, lambda g: convolve(chunk, g), unroll=2)
        turn_out(chunk)
        send_out(chunk)
        own_out(chunk, 0).start()
        own_out(chunk, 1).start()

    for chunk in range(chunks):
        each(chunk_groups, lambda g: correlate(chunk, g), unroll=2)

    for step in range(1, nctx):
        sum_copy(step, True).start()
    own_sums = pltpu.make_async_copy(
        sums.at[:, pl.ds(pl.multiple_of(ctx * span, 128), span)],
        filt_ref.at[pl.ds(pl.multiple_of(ctx * groups, 8), groups), :],
        local_sem.at[3 * chunks + 1],
    )
    own_sums.start()

    for step in range(1, nctx):
        tap_copy(step, True).wait_send()
    for chunk in range(chunks):
        all_of(in_send, chunk)
        all_of(out_send, chunk)
        all_of(out_recv, chunk)
        own_out(chunk, 0).wait()
        own_out(chunk, 1).wait()
    for step in range(1, nctx):
        sum_copy(step, True).wait_send()
        sum_copy(step, False).wait_recv()
    own_sums.wait()


def one_exchange(nctx, nch, query_gate, key_gate, value_proj, grad_out, long_filters):
    tokens, model = query_gate.shape
    ndev = nctx * nch
    chans = model // ndev
    groups = chans // GROUP_CH
    chunks = chans // CHUNK_CH
    seq = tokens * ndev
    nblocks = seq // TAPS_BLOCK
    chunk_groups = CHUNK_CH // GROUP_CH
    vmem = pl.BlockSpec(memory_space=pltpu.VMEM)
    half = jnp.bfloat16
    sem = pltpu.SemaphoreType.DMA
    convolved, correlated, grad_filters, key_near, value_near, grad_near = pl.pallas_call(
        functools.partial(exchange_kernel, nctx, nch, chunks),
        out_shape=(
            jax.ShapeDtypeStruct((tokens, model), half),
            jax.ShapeDtypeStruct((tokens, model), half),
            jax.ShapeDtypeStruct(long_filters.shape, jnp.float32),
        )
        + (jax.ShapeDtypeStruct((tokens, model), half),) * 3,
        in_specs=[pl.BlockSpec(memory_space=pltpu.HBM)] * 4 + [vmem],
        out_specs=(vmem,) * 6,
        scratch_shapes=[
            pltpu.VMEM((tokens, model), half),
            pltpu.VMEM((2 * tokens, model), half),
            pltpu.VMEM((chunks, ndev, 2 * tokens, CHUNK_CH), half),
            pltpu.VMEM((chunks, ndev, 2 * tokens, CHUNK_CH), half),
            pltpu.VMEM((groups, seq), jnp.float32),
            pltpu.VMEM((groups, seq), jnp.float32),
            pltpu.VMEM((groups, 2, nblocks, TAPS_BLOCK, TAPS_BLOCK), half),
            pltpu.VMEM((chunks, chunk_groups, nblocks, GROUP_CH, TAPS_BLOCK), half),
            pltpu.VMEM((chunks, chunk_groups, nblocks, GROUP_CH, TAPS_BLOCK), half),
            pltpu.VMEM((nblocks, CHUNK_CH, TAPS_BLOCK), half),
            pltpu.VMEM((nblocks, CHUNK_CH, TAPS_BLOCK), half),
            sem((chunks,)),
            sem((chunks,)),
            sem((chunks,)),
            sem((chunks,)),
            sem((nctx,)),
            sem((nctx,)),
            sem((nctx,)),
            sem((nctx,)),
            sem((3 * chunks + 2,)),
            sem((4, LOAD_PIECES)),
        ],
        compiler_params=pltpu.CompilerParams(
            collective_id=0, has_side_effects=True, vmem_limit_bytes=51 * 1024 * 1024
        ),
        name="exchange_and_convolve",
    )(query_gate, key_gate, value_proj, grad_out, long_filters)
    convolved = convolved.astype(jnp.float32)
    correlated = correlated.astype(jnp.float32)
    return (
        (grad_near.astype(jnp.float32) * convolved).astype(half),
        (correlated * value_near.astype(jnp.float32)).astype(half),
        (correlated * key_near.astype(jnp.float32)).astype(half),
        grad_filters,
    )


def fits_one_exchange(nctx, nch, query_shape, filter_shape):
    tokens, model = query_shape
    ndev = nctx * nch
    return (
        model % (ndev * CHUNK_CH) == 0
        and tokens % 16 == 0
        and TAPS_BLOCK % tokens == 0
        and tokens * ndev == TAPS_BLOCK * (TAPS_BLOCK // GROUP_CH)
        and filter_shape[1] % 128 == 0
        and nctx * filter_shape[0] * nch * GROUP_CH == model * nctx
    )


def solution(mesh):
    nctx, nch = mesh.shape["ctx"], mesh.shape["ch"]

    def local(query_gate, key_gate, value_proj, grad_out, long_filters):
        args = (query_gate, key_gate, value_proj, grad_out, long_filters)
        if fits_one_exchange(nctx, nch, query_gate.shape, long_filters.shape):
            return one_exchange(nctx, nch, *args)
        return on_device(*args)

    in_specs = (
        P(("ctx", "ch"), None),
        P(("ctx", "ch"), None),
        P(("ctx", "ch"), None),
        P(("ctx", "ch"), None),
        P("ch", "ctx"),
    )
    out_specs = (
        P(("ctx", "ch"), None),
        P(("ctx", "ch"), None),
        P(("ctx", "ch"), None),
        P("ch", "ctx"),
    )
    return jax.shard_map(
        local, mesh=mesh, in_specs=in_specs, out_specs=out_specs, check_vma=False
    )
```

```python
import functools
import math

import jax
import jax.numpy as jnp
from jax import lax
from jax.experimental import pallas as pl
from jax.experimental.pallas import tpu as pltpu
from jax.sharding import PartitionSpec as P

GROUP_CH = 16


HIGHEST_MODE = lax.Precision.HIGHEST
SPLIT_MODE = lax.Precision.HIGH


def passed_along(value, axis, steps):
    count = lax.axis_size(axis)
    leading, last = (max(0, -steps), min(count, count - steps))
    return lax.ppermute(value, axis, [(source, source + steps) for source in range(leading, last)])


def make_tables(block_len):
    period = 2 * block_len
    steps = lax.iota(jnp.int32, block_len)
    phase = steps[:, None] * steps[None, :] % period
    angle = phase.astype(jnp.float32) * (math.pi / block_len)
    cosine = jnp.cos(angle)
    sine = jnp.sin(angle)
    parity = 1.0 - 2.0 * (steps % 2).astype(jnp.float32)
    weights = jnp.where(steps == 0, 1.0, 2.0).astype(jnp.float32) / period
    return (
        cosine,
        -sine,
        parity,
        cosine * weights[None, :],
        -sine * weights[None, :],
        parity / period,
    )


def columns_forward(tables, values):
    return (
        jnp.dot(tables[0], values, precision=SPLIT_MODE),
        jnp.dot(tables[1], values, precision=SPLIT_MODE),
        jnp.dot(tables[2], values, precision=SPLIT_MODE),
    )


def columns_inverse(tables, real_part, imag_part, nyquist):
    return (
        jnp.dot(tables[3], real_part, precision=SPLIT_MODE)
        + jnp.dot(tables[4], imag_part, precision=SPLIT_MODE)
        + tables[5][:, None] * nyquist[None, :]
    )


def rows_forward(tables, values):
    return (
        jnp.dot(values, tables[0], precision=HIGHEST_MODE),
        jnp.dot(values, tables[1], precision=HIGHEST_MODE),
        jnp.dot(values, tables[2], precision=HIGHEST_MODE),
    )


def rows_inverse(tables, real_part, imag_part, nyquist):
    return (
        jnp.dot(real_part, tables[3].T, precision=SPLIT_MODE)
        + jnp.dot(imag_part, tables[4].T, precision=SPLIT_MODE)
        + nyquist[:, None] * tables[5][None, :]
    )


def spread_groups(rows):
    groups, block_len = rows.shape
    return jnp.broadcast_to(rows.T[:, :, None], (block_len, groups, GROUP_CH)).reshape(
        block_len, groups * GROUP_CH
    )


def spread_vector(vector):
    return jnp.broadcast_to(vector[:, None], (vector.shape[0], GROUP_CH)).reshape(-1)


def group_rows(matrix):
    block_len, chans = matrix.shape
    return matrix.reshape(block_len, chans // GROUP_CH, GROUP_CH).sum(axis=2).T


def group_vector(vector):
    return vector.reshape(-1, GROUP_CH).sum(axis=1)


def by_blocks(tables, signal, upstream, long_filters):
    block_len, chans = signal.shape
    groups = long_filters.shape[0]
    nblocks = lax.axis_size("ctx")
    own_block = lax.axis_index("ctx")
    parity = tables[2]
    prev_taps = passed_along(long_filters, "ctx", 1)
    both_re, both_im, both_ny = rows_forward(
        tables, jnp.concatenate([prev_taps, long_filters], axis=0)
    )
    own_re = both_re[:groups] + both_re[groups:] * parity
    own_im = both_im[:groups] + both_im[groups:] * parity
    own_ny = both_ny[:groups] + both_ny[groups:]
    lag_re, lag_im, lag_ny = (
        lax.all_gather(own_re[None], "ctx", axis=0, tiled=True),
        lax.all_gather(own_im[None], "ctx", axis=0, tiled=True),
        lax.all_gather(own_ny[None], "ctx", axis=0, tiled=True),
    )
    mine_re, mine_im, mine_ny = columns_forward(tables, upstream.astype(jnp.float32))
    mine_re = mine_re * parity[:, None]
    mine_im = mine_im * parity[:, None]

    def pick(lag_index):
        return (
            spread_groups(lax.dynamic_index_in_dim(lag_re, lag_index, 0, keepdims=False)),
            spread_groups(lax.dynamic_index_in_dim(lag_im, lag_index, 0, keepdims=False)),
            spread_vector(lax.dynamic_index_in_dim(lag_ny, lag_index, 0, keepdims=False)),
        )

    def add_earlier(totals, block_vals, lag_index):
        conv_re, conv_im, conv_ny, back_re, back_im, back_ny, corr_re, corr_im, corr_ny = totals
        sig_re, sig_im, sig_ny = columns_forward(tables, block_vals)
        tap_re, tap_im, tap_ny = pick(lag_index)
        conv_re = conv_re + tap_re * sig_re - tap_im * sig_im
        conv_im = conv_im + tap_re * sig_im + tap_im * sig_re
        conv_ny = conv_ny + tap_ny * sig_ny
        corr_re = corr_re.at[lag_index].add(group_rows(mine_re * sig_re + mine_im * sig_im))
        corr_im = corr_im.at[lag_index].add(group_rows(mine_im * sig_re - mine_re * sig_im))
        corr_ny = corr_ny.at[lag_index].add(group_vector(mine_ny * sig_ny))
        return (conv_re, conv_im, conv_ny, back_re, back_im, back_ny, corr_re, corr_im, corr_ny)

    def add_later(totals, block_vals, lag_index):
        conv_re, conv_im, conv_ny, back_re, back_im, back_ny, corr_re, corr_im, corr_ny = totals
        up_re, up_im, up_ny = columns_forward(tables, block_vals)
        up_re = up_re * parity[:, None]
        up_im = up_im * parity[:, None]
        tap_re, tap_im, tap_ny = pick(lag_index)
        back_re = back_re + tap_re * up_re + tap_im * up_im
        back_im = back_im + tap_re * up_im - tap_im * up_re
        back_ny = back_ny + tap_ny * up_ny
        return (conv_re, conv_im, conv_ny, back_re, back_im, back_ny, corr_re, corr_im, corr_ny)

    plane = jnp.zeros((block_len, chans), jnp.float32)
    edge = jnp.zeros((chans,), jnp.float32)
    stack = jnp.zeros((nblocks, groups, block_len), jnp.float32)
    stack_edge = jnp.zeros((nblocks, groups), jnp.float32)
    initial = (plane, plane, edge, plane, plane, edge, stack, stack, stack_edge)
    sig_piece = lax.all_gather(signal, "ctx", axis=0, tiled=True)
    up_piece = lax.all_gather(upstream, "ctx", axis=0, tiled=True)
    piece_blocks = sig_piece.shape[0] // block_len

    def one_block(offset, running):
        sig_vals = lax.dynamic_slice_in_dim(sig_piece, offset * block_len, block_len, 0).astype(
            jnp.float32
        )
        up_vals = lax.dynamic_slice_in_dim(up_piece, offset * block_len, block_len, 0).astype(
            jnp.float32
        )
        running = lax.cond(
            offset <= own_block,
            lambda current: add_earlier(current, sig_vals, own_block - offset),
            lambda current: current,
            running,
        )
        running = lax.cond(
            offset >= own_block,
            lambda current: add_later(current, up_vals, offset - own_block),
            lambda current: current,
            running,
        )
        return running

    totals = lax.fori_loop(0, piece_blocks, one_block, initial)
    conv_re, conv_im, conv_ny, back_re, back_im, back_ny, corr_re, corr_im, corr_ny = totals
    convolved = columns_inverse(
        tables, conv_re * parity[:, None], conv_im * parity[:, None], conv_ny
    )
    correlated = columns_inverse(tables, back_re, back_im, back_ny)
    total_re, total_im, total_ny = lax.psum((corr_re, corr_im, corr_ny), "ctx")
    next_block = jnp.minimum(own_block + 1, nblocks - 1)
    valid = (own_block + 1 < nblocks).astype(jnp.float32)
    cur_re = lax.dynamic_index_in_dim(total_re, own_block, 0, keepdims=False)
    cur_im = lax.dynamic_index_in_dim(total_im, own_block, 0, keepdims=False)
    cur_ny = lax.dynamic_index_in_dim(total_ny, own_block, 0, keepdims=False)
    nxt_re = lax.dynamic_index_in_dim(total_re, next_block, 0, keepdims=False)
    nxt_im = lax.dynamic_index_in_dim(total_im, next_block, 0, keepdims=False)
    nxt_ny = lax.dynamic_index_in_dim(total_ny, next_block, 0, keepdims=False)
    upper = rows_inverse(tables, cur_re * parity, cur_im * parity, cur_ny)
    lower = rows_inverse(tables, nxt_re, nxt_im, nxt_ny)
    grad_filters = upper + lower * valid
    return (convolved, correlated, grad_filters)


def on_device(query_gate, key_gate, value_proj, grad_out, long_filters):
    query_cols, key_cols, value_cols, grad_cols = (
        lax.all_to_all(query_gate, "ch", split_axis=1, concat_axis=0, tiled=True),
        lax.all_to_all(key_gate, "ch", split_axis=1, concat_axis=0, tiled=True),
        lax.all_to_all(value_proj, "ch", split_axis=1, concat_axis=0, tiled=True),
        lax.all_to_all(grad_out, "ch", split_axis=1, concat_axis=0, tiled=True),
    )
    query_vals = query_cols.astype(jnp.float32)
    key_vals = key_cols.astype(jnp.float32)
    value_vals = value_cols.astype(jnp.float32)
    grad_vals = grad_cols.astype(jnp.float32)
    signal = (key_vals * value_vals).astype(jnp.bfloat16)
    upstream = (grad_vals * query_vals).astype(jnp.bfloat16)
    tables = make_tables(signal.shape[0])
    convolved, correlated, grad_filters = by_blocks(tables, signal, upstream, long_filters)
    conv_half = convolved.astype(jnp.bfloat16)
    corr_half = correlated.astype(jnp.bfloat16)
    conv_wide = lax.optimization_barrier(conv_half).astype(jnp.float32)
    corr_wide = lax.optimization_barrier(corr_half).astype(jnp.float32)
    grad_query = (grad_vals * conv_wide).astype(jnp.bfloat16)
    grad_key = (corr_wide * value_vals).astype(jnp.bfloat16)
    grad_value = (corr_wide * key_vals).astype(jnp.bfloat16)
    query_rows, key_rows, value_rows = (
        lax.all_to_all(grad_query, "ch", split_axis=0, concat_axis=1, tiled=True),
        lax.all_to_all(grad_key, "ch", split_axis=0, concat_axis=1, tiled=True),
        lax.all_to_all(grad_value, "ch", split_axis=0, concat_axis=1, tiled=True),
    )
    return (query_rows, key_rows, value_rows, grad_filters)


TAPS_BLOCK = 128
CHUNK_CH = 128
LOAD_PIECES = 4
MESH = pl.DeviceIdType.MESH
NT = (((1,), (1,)), ((), ()))


def exchange_kernel(
    nctx, nch, chunks,
    query_hbm, key_hbm, value_hbm, grad_hbm, taps_ref,
    conv_ref, corr_ref, filt_ref, key_ref, value_ref, grad_ref,
    query_ref, staged, landed, back, taps, sums, toeplitz, xt, ut, yt, zt,
    in_send, in_recv, out_send, out_recv, tap_send, tap_recv, sum_send, sum_recv, local_sem, load_sem,
):
    ctx = lax.axis_index("ctx")
    ch = lax.axis_index("ch")
    ndev = nctx * nch
    me = ctx * nch + ch
    tokens = query_ref.shape[0]
    chans = query_ref.shape[1] // ndev
    groups = chans // GROUP_CH
    span = taps_ref.shape[1]
    seq = tokens * ndev
    block = TAPS_BLOCK
    nblocks = seq // block
    per_block = block // tokens
    chunk_groups = CHUNK_CH // GROUP_CH

    offsets = []
    for order in range(nch // 2):
        far = nch // 2 + (-(order + 1) // 2 if order % 2 else order // 2)
        offsets.append((far, (far + nch // 2) % nch))
    partners = []
    for pair in offsets:
        for turn in range(1, nctx + 1):
            for offset in pair:
                if offset or turn < nctx:
                    other_ch = lax.rem(ch + offset, nch)
                    other_ctx = lax.rem(ctx + turn, nctx)
                    partners.append((other_ctx, other_ch, other_ctx * nch + other_ch))

    def columns(owner_ctx, owner_ch, chunk):
        start = owner_ch * (nctx * chans) + owner_ctx * chans + chunk * CHUNK_CH
        return pl.ds(pl.multiple_of(start, 128), CHUNK_CH)

    def gate(cols):
        staged[0:tokens, cols] = (
            key_ref[:, cols].astype(jnp.float32) * value_ref[:, cols].astype(jnp.float32)
        ).astype(jnp.bfloat16)
        staged[tokens:, cols] = (
            grad_ref[:, cols].astype(jnp.float32) * query_ref[:, cols].astype(jnp.float32)
        ).astype(jnp.bfloat16)

    def send_in(chunk):
        for other_ctx, other_ch, other in partners:
            pltpu.make_async_remote_copy(
                src_ref=staged.at[:, columns(other_ctx, other_ch, chunk)],
                dst_ref=landed.at[chunk, me],
                send_sem=in_send.at[chunk],
                recv_sem=in_recv.at[chunk],
                device_id=(other_ctx, other_ch),
                device_id_type=MESH,
            ).start()

    def send_out(chunk):
        own = columns(ctx, ch, chunk)
        for other_ctx, other_ch, other in partners:
            for half, dst in ((0, conv_ref), (tokens, corr_ref)):
                pltpu.make_async_remote_copy(
                    src_ref=back.at[chunk, other, pl.ds(half, tokens)],
                    dst_ref=dst.at[:, own],
                    send_sem=out_send.at[chunk],
                    recv_sem=out_recv.at[chunk],
                    device_id=(other_ctx, other_ch),
                    device_id_type=MESH,
                ).start()

    def all_of(sem, chunk):
        whole = landed.at[chunk, pl.ds(0, ndev - 1)]
        pltpu.make_async_copy(whole, whole, sem.at[chunk]).wait()

    def tap_copy(step, sender):
        other = (ctx + step) % nctx
        slot = ctx if sender else other
        return pltpu.make_async_remote_copy(
            src_ref=taps_ref.at[pl.ds(pl.multiple_of(other * groups, 8), groups), :],
            dst_ref=taps.at[:, pl.ds(pl.multiple_of(slot * span, 128), span)],
            send_sem=tap_send.at[step],
            recv_sem=tap_recv.at[slot],
            device_id=(other, ch),
            device_id_type=MESH,
        )

    def sum_copy(step, sender):
        other = (ctx + step) % nctx
        slot = ctx if sender else other
        return pltpu.make_async_remote_copy(
            src_ref=sums.at[:, pl.ds(pl.multiple_of(other * span, 128), span)],
            dst_ref=filt_ref.at[pl.ds(pl.multiple_of(slot * groups, 8), groups), :],
            send_sem=sum_send.at[step],
            recv_sem=sum_recv.at[slot],
            device_id=(other, ch),
            device_id_type=MESH,
        )

    def own_in(chunk):
        return pltpu.make_async_copy(
            staged.at[:, columns(ctx, ch, chunk)], landed.at[chunk, me], local_sem.at[chunk]
        )

    def own_out(chunk, half):
        dst = (conv_ref, corr_ref)[half]
        return pltpu.make_async_copy(
            back.at[chunk, me, pl.ds(half * tokens, tokens)],
            dst.at[:, columns(ctx, ch, chunk)],
            local_sem.at[chunks + 2 * chunk + half],
        )

    def each(count, body, unroll=1):
        def step(n, carry):
            body(n)
            return carry

        lax.fori_loop(0, count, step, 0, unroll=unroll)

    pieces = LOAD_PIECES
    piece = nctx * nch * chans // pieces

    def load(which, part):
        src, dst = (
            (query_hbm, query_ref),
            (key_hbm, key_ref),
            (value_hbm, value_ref),
            (grad_hbm, grad_ref),
        )[which]
        cols = pl.ds(part * piece, piece)
        return pltpu.make_async_copy(src.at[:, cols], dst.at[:, cols], load_sem.at[which, part])

    for part in range(pieces):
        for which in range(4):
            load(which, part).start()

    barrier = pltpu.get_barrier_semaphore()

    for other_ctx, other_ch, _ in partners:
        pl.semaphore_signal(barrier, inc=1, device_id=(other_ctx, other_ch), device_id_type=MESH)

    def gate_chunk(chunk, first, count):
        each(
            count,
            lambda n: gate(
                pl.ds(pl.multiple_of((first + n) * chans + chunk * CHUNK_CH, 128), CHUNK_CH)
            ),
            unroll=4,
        )

    own_taps = pltpu.make_async_copy(
        taps_ref.at[pl.ds(pl.multiple_of(ctx * groups, 8), groups), :],
        taps.at[:, pl.ds(pl.multiple_of(ctx * span, 128), span)],
        local_sem.at[3 * chunks],
    )
    own_taps.start()
    for part in range(pieces):
        for which in range(4):
            load(which, part).wait()
        gate_chunk(0, part * (ndev // pieces), ndev // pieces)
    pl.semaphore_wait(barrier, ndev - 1)
    for step in range(1, nctx):
        tap_copy(step, True).start()
    send_in(0)
    own_in(0).start()
    for chunk in range(1, chunks):
        gate_chunk(chunk, 0, ndev)
        send_in(chunk)
        own_in(chunk).start()
    own_taps.wait()
    for step in range(1, nctx):
        tap_copy(step, False).wait_recv()

    row_id = lax.broadcasted_iota(jnp.int32, (block, block), 0)
    col_id = lax.broadcasted_iota(jnp.int32, (block, block), 1)
    flip = (row_id + col_id == block - 1).astype(jnp.bfloat16)
    zeros = jnp.zeros((block, block), jnp.bfloat16)
    width = block + seq

    doubling = [8 << n for n in range((block // 8).bit_length() - 1)]

    def spread_diagonals(row):
        wide = pltpu.roll(jnp.broadcast_to(row, (8, width)), 0, 1, stride=1, stride_axis=0)
        for rows in doubling:
            wide = jnp.concatenate([wide, pltpu.roll(wide, rows, 1)], axis=0)
        return wide[:, block:]

    def sum_diagonals(values):
        for rows in doubling[::-1]:
            values = values[:rows] + pltpu.roll(values[rows:], rows, 1)
        values = pltpu.roll(values, 1, 1, stride=1, stride_axis=0)[:, block:]
        return jnp.sum(values, axis=0, keepdims=True)

    def later(stack):
        padded = jnp.concatenate([stack, zeros], axis=0)
        return jnp.concatenate(
            [padded[k * GROUP_CH : k * GROUP_CH + block] for k in range(nblocks)], axis=1
        )

    def earlier(stack):
        padded = jnp.concatenate([zeros, stack], axis=0)
        return jnp.concatenate(
            [padded[block - k * GROUP_CH : 2 * block - k * GROUP_CH] for k in range(nblocks)],
            axis=1,
        )

    def turn_in(chunk):
        for i in range(nblocks):
            src = pl.ds(i * per_block, per_block)
            for rows, dst in ((pl.ds(0, tokens), xt), (pl.ds(tokens, tokens), ut)):
                tile = landed[chunk, src, rows, :].reshape(block, CHUNK_CH)
                dst[chunk, :, i] = tile.T.reshape(chunk_groups, GROUP_CH, block)

    def build(group):
        row = taps[pl.ds(group, 1), :]
        row = jnp.concatenate([jnp.zeros((1, block), jnp.float32), row], axis=1)
        wide = spread_diagonals(row)
        high = wide.astype(jnp.bfloat16)
        low = (wide - high.astype(jnp.float32)).astype(jnp.bfloat16)
        for which, part in ((0, high), (1, low)):
            for k in range(nblocks):
                toeplitz[group, which, k] = part[:, k * block : (k + 1) * block]

    def convolve(chunk, g):
        x_cat = earlier(xt[chunk, g].reshape(block, block))
        u_cat = later(ut[chunk, g].reshape(block, block))
        conv = jnp.zeros((block, block), jnp.float32)
        corr = jnp.zeros((block, block), jnp.float32)
        for which in range(2):
            part = toeplitz[chunk * chunk_groups + g, which]
            tall = part.reshape(nblocks * block, block)
            flat = jnp.concatenate([part[k] for k in range(nblocks)], axis=1)
            conv = conv + jnp.dot(x_cat, tall, preferred_element_type=jnp.float32)
            corr = corr + lax.dot_general(u_cat, flat, NT, preferred_element_type=jnp.float32)
        yt[:, pl.ds(pl.multiple_of(g * GROUP_CH, GROUP_CH), GROUP_CH), :] = (
            conv.astype(jnp.bfloat16).reshape(nblocks, GROUP_CH, block)
        )
        zt[:, pl.ds(pl.multiple_of(g * GROUP_CH, GROUP_CH), GROUP_CH), :] = (
            corr.astype(jnp.bfloat16).reshape(nblocks, GROUP_CH, block)
        )

    def turn_out(chunk):
        for i in range(nblocks):
            dst = pl.ds(i * per_block, per_block)
            back[chunk, dst, 0:tokens, :] = yt[i].T.reshape(per_block, tokens, CHUNK_CH)
            back[chunk, dst, tokens:, :] = zt[i].T.reshape(per_block, tokens, CHUNK_CH)

    def correlate(chunk, g):
        stack_x = xt[chunk, g].reshape(block, block)
        u_cat = later(ut[chunk, g].reshape(block, block))
        turned = lax.dot_general(
            flip, stack_x, NT, preferred_element_type=jnp.float32
        ).astype(jnp.bfloat16)
        pairs = jnp.dot(turned, u_cat, preferred_element_type=jnp.float32)
        pairs = jnp.concatenate([pairs, jnp.zeros((block, block), jnp.float32)], axis=1)
        sums[pl.ds(chunk * chunk_groups + g, 1), :] = sum_diagonals(pairs)

    each(groups, build, unroll=2)
    for chunk in range(chunks):
        own_in(chunk).wait()
        all_of(in_recv, chunk)
        turn_in(chunk)
        each(chunk_groups, lambda g: convolve(chunk, g), unroll=2)
        turn_out(chunk)
        send_out(chunk)
        own_out(chunk, 0).start()
        own_out(chunk, 1).start()

    for chunk in range(chunks):
        each(chunk_groups, lambda g: correlate(chunk, g), unroll=2)

    for step in range(1, nctx):
        sum_copy(step, True).start()
    own_sums = pltpu.make_async_copy(
        sums.at[:, pl.ds(pl.multiple_of(ctx * span, 128), span)],
        filt_ref.at[pl.ds(pl.multiple_of(ctx * groups, 8), groups), :],
        local_sem.at[3 * chunks + 1],
    )
    own_sums.start()

    for step in range(1, nctx):
        tap_copy(step, True).wait_send()
    for chunk in range(chunks):
        all_of(in_send, chunk)
        all_of(out_send, chunk)
        all_of(out_recv, chunk)
        own_out(chunk, 0).wait()
        own_out(chunk, 1).wait()
    for step in range(1, nctx):
        sum_copy(step, True).wait_send()
        sum_copy(step, False).wait_recv()
    own_sums.wait()


def one_exchange(nctx, nch, query_gate, key_gate, value_proj, grad_out, long_filters):
    tokens, model = query_gate.shape
    ndev = nctx * nch
    chans = model // ndev
    groups = chans // GROUP_CH
    chunks = chans // CHUNK_CH
    seq = tokens * ndev
    nblocks = seq // TAPS_BLOCK
    chunk_groups = CHUNK_CH // GROUP_CH
    vmem = pl.BlockSpec(memory_space=pltpu.VMEM)
    half = jnp.bfloat16
    sem = pltpu.SemaphoreType.DMA
    convolved, correlated, grad_filters, key_near, value_near, grad_near = pl.pallas_call(
        functools.partial(exchange_kernel, nctx, nch, chunks),
        out_shape=(
            jax.ShapeDtypeStruct((tokens, model), half),
            jax.ShapeDtypeStruct((tokens, model), half),
            jax.ShapeDtypeStruct(long_filters.shape, jnp.float32),
        )
        + (jax.ShapeDtypeStruct((tokens, model), half),) * 3,
        in_specs=[pl.BlockSpec(memory_space=pltpu.HBM)] * 4 + [vmem],
        out_specs=(vmem,) * 6,
        scratch_shapes=[
            pltpu.VMEM((tokens, model), half),
            pltpu.VMEM((2 * tokens, model), half),
            pltpu.VMEM((chunks, ndev, 2 * tokens, CHUNK_CH), half),
            pltpu.VMEM((chunks, ndev, 2 * tokens, CHUNK_CH), half),
            pltpu.VMEM((groups, seq), jnp.float32),
            pltpu.VMEM((groups, seq), jnp.float32),
            pltpu.VMEM((groups, 2, nblocks, TAPS_BLOCK, TAPS_BLOCK), half),
            pltpu.VMEM((chunks, chunk_groups, nblocks, GROUP_CH, TAPS_BLOCK), half),
            pltpu.VMEM((chunks, chunk_groups, nblocks, GROUP_CH, TAPS_BLOCK), half),
            pltpu.VMEM((nblocks, CHUNK_CH, TAPS_BLOCK), half),
            pltpu.VMEM((nblocks, CHUNK_CH, TAPS_BLOCK), half),
            sem((chunks,)),
            sem((chunks,)),
            sem((chunks,)),
            sem((chunks,)),
            sem((nctx,)),
            sem((nctx,)),
            sem((nctx,)),
            sem((nctx,)),
            sem((3 * chunks + 2,)),
            sem((4, LOAD_PIECES)),
        ],
        compiler_params=pltpu.CompilerParams(
            collective_id=0, has_side_effects=True, vmem_limit_bytes=51 * 1024 * 1024
        ),
        name="exchange_and_convolve",
    )(query_gate, key_gate, value_proj, grad_out, long_filters)
    convolved = convolved.astype(jnp.float32)
    correlated = correlated.astype(jnp.float32)
    return (
        (grad_near.astype(jnp.float32) * convolved).astype(half),
        (correlated * value_near.astype(jnp.float32)).astype(half),
        (correlated * key_near.astype(jnp.float32)).astype(half),
        grad_filters,
    )


def fits_one_exchange(nctx, nch, query_shape, filter_shape):
    tokens, model = query_shape
    ndev = nctx * nch
    return (
        model % (ndev * CHUNK_CH) == 0
        and tokens % 16 == 0
        and TAPS_BLOCK % tokens == 0
        and tokens * ndev == TAPS_BLOCK * (TAPS_BLOCK // GROUP_CH)
        and filter_shape[1] % 128 == 0
        and nctx * filter_shape[0] * nch * GROUP_CH == model * nctx
    )


def solution(mesh):
    nctx, nch = mesh.shape["ctx"], mesh.shape["ch"]

    def local(query_gate, key_gate, value_proj, grad_out, long_filters):
        args = (query_gate, key_gate, value_proj, grad_out, long_filters)
        if fits_one_exchange(nctx, nch, query_gate.shape, long_filters.shape):
            return one_exchange(nctx, nch, *args)
        return on_device(*args)

    in_specs = (
        P(("ctx", "ch"), None),
        P(("ctx", "ch"), None),
        P(("ctx", "ch"), None),
        P(("ctx", "ch"), None),
        P("ch", "ctx"),
    )
    out_specs = (
        P(("ctx", "ch"), None),
        P(("ctx", "ch"), None),
        P(("ctx", "ch"), None),
        P("ch", "ctx"),
    )
    return jax.shard_map(
        local, mesh=mesh, in_specs=in_specs, out_specs=out_specs, check_vma=False
    )
```

```python
import functools
import math

import jax
import jax.numpy as jnp
from jax import lax
from jax.experimental import pallas as pl
from jax.experimental.pallas import tpu as pltpu
from jax.sharding import PartitionSpec as P

GROUP_CH = 16


HIGHEST_MODE = lax.Precision.HIGHEST
SPLIT_MODE = lax.Precision.HIGH


def passed_along(value, axis, steps):
    count = lax.axis_size(axis)
    leading, last = (max(0, -steps), min(count, count - steps))
    return lax.ppermute(value, axis, [(source, source + steps) for source in range(leading, last)])


def make_tables(block_len):
    period = 2 * block_len
    steps = lax.iota(jnp.int32, block_len)
    phase = steps[:, None] * steps[None, :] % period
    angle = phase.astype(jnp.float32) * (math.pi / block_len)
    cosine = jnp.cos(angle)
    sine = jnp.sin(angle)
    parity = 1.0 - 2.0 * (steps % 2).astype(jnp.float32)
    weights = jnp.where(steps == 0, 1.0, 2.0).astype(jnp.float32) / period
    return (
        cosine,
        -sine,
        parity,
        cosine * weights[None, :],
        -sine * weights[None, :],
        parity / period,
    )


def columns_forward(tables, values):
    return (
        jnp.dot(tables[0], values, precision=SPLIT_MODE),
        jnp.dot(tables[1], values, precision=SPLIT_MODE),
        jnp.dot(tables[2], values, precision=SPLIT_MODE),
    )


def columns_inverse(tables, real_part, imag_part, nyquist):
    return (
        jnp.dot(tables[3], real_part, precision=SPLIT_MODE)
        + jnp.dot(tables[4], imag_part, precision=SPLIT_MODE)
        + tables[5][:, None] * nyquist[None, :]
    )


def rows_forward(tables, values):
    return (
        jnp.dot(values, tables[0], precision=HIGHEST_MODE),
        jnp.dot(values, tables[1], precision=HIGHEST_MODE),
        jnp.dot(values, tables[2], precision=HIGHEST_MODE),
    )


def rows_inverse(tables, real_part, imag_part, nyquist):
    return (
        jnp.dot(real_part, tables[3].T, precision=SPLIT_MODE)
        + jnp.dot(imag_part, tables[4].T, precision=SPLIT_MODE)
        + nyquist[:, None] * tables[5][None, :]
    )


def spread_groups(rows):
    groups, block_len = rows.shape
    return jnp.broadcast_to(rows.T[:, :, None], (block_len, groups, GROUP_CH)).reshape(
        block_len, groups * GROUP_CH
    )


def spread_vector(vector):
    return jnp.broadcast_to(vector[:, None], (vector.shape[0], GROUP_CH)).reshape(-1)


def group_rows(matrix):
    block_len, chans = matrix.shape
    return matrix.reshape(block_len, chans // GROUP_CH, GROUP_CH).sum(axis=2).T


def group_vector(vector):
    return vector.reshape(-1, GROUP_CH).sum(axis=1)


def by_blocks(tables, signal, upstream, long_filters):
    block_len, chans = signal.shape
    groups = long_filters.shape[0]
    nblocks = lax.axis_size("ctx")
    own_block = lax.axis_index("ctx")
    parity = tables[2]
    prev_taps = passed_along(long_filters, "ctx", 1)
    both_re, both_im, both_ny = rows_forward(
        tables, jnp.concatenate([prev_taps, long_filters], axis=0)
    )
    own_re = both_re[:groups] + both_re[groups:] * parity
    own_im = both_im[:groups] + both_im[groups:] * parity
    own_ny = both_ny[:groups] + both_ny[groups:]
    lag_re, lag_im, lag_ny = (
        lax.all_gather(own_re[None], "ctx", axis=0, tiled=True),
        lax.all_gather(own_im[None], "ctx", axis=0, tiled=True),
        lax.all_gather(own_ny[None], "ctx", axis=0, tiled=True),
    )
    mine_re, mine_im, mine_ny = columns_forward(tables, upstream.astype(jnp.float32))
    mine_re = mine_re * parity[:, None]
    mine_im = mine_im * parity[:, None]

    def pick(lag_index):
        return (
            spread_groups(lax.dynamic_index_in_dim(lag_re, lag_index, 0, keepdims=False)),
            spread_groups(lax.dynamic_index_in_dim(lag_im, lag_index, 0, keepdims=False)),
            spread_vector(lax.dynamic_index_in_dim(lag_ny, lag_index, 0, keepdims=False)),
        )

    def add_earlier(totals, block_vals, lag_index):
        conv_re, conv_im, conv_ny, back_re, back_im, back_ny, corr_re, corr_im, corr_ny = totals
        sig_re, sig_im, sig_ny = columns_forward(tables, block_vals)
        tap_re, tap_im, tap_ny = pick(lag_index)
        conv_re = conv_re + tap_re * sig_re - tap_im * sig_im
        conv_im = conv_im + tap_re * sig_im + tap_im * sig_re
        conv_ny = conv_ny + tap_ny * sig_ny
        corr_re = corr_re.at[lag_index].add(group_rows(mine_re * sig_re + mine_im * sig_im))
        corr_im = corr_im.at[lag_index].add(group_rows(mine_im * sig_re - mine_re * sig_im))
        corr_ny = corr_ny.at[lag_index].add(group_vector(mine_ny * sig_ny))
        return (conv_re, conv_im, conv_ny, back_re, back_im, back_ny, corr_re, corr_im, corr_ny)

    def add_later(totals, block_vals, lag_index):
        conv_re, conv_im, conv_ny, back_re, back_im, back_ny, corr_re, corr_im, corr_ny = totals
        up_re, up_im, up_ny = columns_forward(tables, block_vals)
        up_re = up_re * parity[:, None]
        up_im = up_im * parity[:, None]
        tap_re, tap_im, tap_ny = pick(lag_index)
        back_re = back_re + tap_re * up_re + tap_im * up_im
        back_im = back_im + tap_re * up_im - tap_im * up_re
        back_ny = back_ny + tap_ny * up_ny
        return (conv_re, conv_im, conv_ny, back_re, back_im, back_ny, corr_re, corr_im, corr_ny)

    plane = jnp.zeros((block_len, chans), jnp.float32)
    edge = jnp.zeros((chans,), jnp.float32)
    stack = jnp.zeros((nblocks, groups, block_len), jnp.float32)
    stack_edge = jnp.zeros((nblocks, groups), jnp.float32)
    initial = (plane, plane, edge, plane, plane, edge, stack, stack, stack_edge)
    sig_piece = lax.all_gather(signal, "ctx", axis=0, tiled=True)
    up_piece = lax.all_gather(upstream, "ctx", axis=0, tiled=True)
    piece_blocks = sig_piece.shape[0] // block_len

    def one_block(offset, running):
        sig_vals = lax.dynamic_slice_in_dim(sig_piece, offset * block_len, block_len, 0).astype(
            jnp.float32
        )
        up_vals = lax.dynamic_slice_in_dim(up_piece, offset * block_len, block_len, 0).astype(
            jnp.float32
        )
        running = lax.cond(
            offset <= own_block,
            lambda current: add_earlier(current, sig_vals, own_block - offset),
            lambda current: current,
            running,
        )
        running = lax.cond(
            offset >= own_block,
            lambda current: add_later(current, up_vals, offset - own_block),
            lambda current: current,
            running,
        )
        return running

    totals = lax.fori_loop(0, piece_blocks, one_block, initial)
    conv_re, conv_im, conv_ny, back_re, back_im, back_ny, corr_re, corr_im, corr_ny = totals
    convolved = columns_inverse(
        tables, conv_re * parity[:, None], conv_im * parity[:, None], conv_ny
    )
    correlated = columns_inverse(tables, back_re, back_im, back_ny)
    total_re, total_im, total_ny = lax.psum((corr_re, corr_im, corr_ny), "ctx")
    next_block = jnp.minimum(own_block + 1, nblocks - 1)
    valid = (own_block + 1 < nblocks).astype(jnp.float32)
    cur_re = lax.dynamic_index_in_dim(total_re, own_block, 0, keepdims=False)
    cur_im = lax.dynamic_index_in_dim(total_im, own_block, 0, keepdims=False)
    cur_ny = lax.dynamic_index_in_dim(total_ny, own_block, 0, keepdims=False)
    nxt_re = lax.dynamic_index_in_dim(total_re, next_block, 0, keepdims=False)
    nxt_im = lax.dynamic_index_in_dim(total_im, next_block, 0, keepdims=False)
    nxt_ny = lax.dynamic_index_in_dim(total_ny, next_block, 0, keepdims=False)
    upper = rows_inverse(tables, cur_re * parity, cur_im * parity, cur_ny)
    lower = rows_inverse(tables, nxt_re, nxt_im, nxt_ny)
    grad_filters = upper + lower * valid
    return (convolved, correlated, grad_filters)


def on_device(query_gate, key_gate, value_proj, grad_out, long_filters):
    query_cols, key_cols, value_cols, grad_cols = (
        lax.all_to_all(query_gate, "ch", split_axis=1, concat_axis=0, tiled=True),
        lax.all_to_all(key_gate, "ch", split_axis=1, concat_axis=0, tiled=True),
        lax.all_to_all(value_proj, "ch", split_axis=1, concat_axis=0, tiled=True),
        lax.all_to_all(grad_out, "ch", split_axis=1, concat_axis=0, tiled=True),
    )
    query_vals = query_cols.astype(jnp.float32)
    key_vals = key_cols.astype(jnp.float32)
    value_vals = value_cols.astype(jnp.float32)
    grad_vals = grad_cols.astype(jnp.float32)
    signal = (key_vals * value_vals).astype(jnp.bfloat16)
    upstream = (grad_vals * query_vals).astype(jnp.bfloat16)
    tables = make_tables(signal.shape[0])
    convolved, correlated, grad_filters = by_blocks(tables, signal, upstream, long_filters)
    conv_half = convolved.astype(jnp.bfloat16)
    corr_half = correlated.astype(jnp.bfloat16)
    conv_wide = lax.optimization_barrier(conv_half).astype(jnp.float32)
    corr_wide = lax.optimization_barrier(corr_half).astype(jnp.float32)
    grad_query = (grad_vals * conv_wide).astype(jnp.bfloat16)
    grad_key = (corr_wide * value_vals).astype(jnp.bfloat16)
    grad_value = (corr_wide * key_vals).astype(jnp.bfloat16)
    query_rows, key_rows, value_rows = (
        lax.all_to_all(grad_query, "ch", split_axis=0, concat_axis=1, tiled=True),
        lax.all_to_all(grad_key, "ch", split_axis=0, concat_axis=1, tiled=True),
        lax.all_to_all(grad_value, "ch", split_axis=0, concat_axis=1, tiled=True),
    )
    return (query_rows, key_rows, value_rows, grad_filters)


TAPS_BLOCK = 128
CHUNK_CH = 128
MESH = pl.DeviceIdType.MESH
NT = (((1,), (1,)), ((), ()))


def exchange_kernel(
    nctx, nch, chunks,
    query_hbm, key_hbm, value_hbm, grad_hbm, taps_ref,
    conv_ref, corr_ref, filt_ref, key_ref, value_ref, grad_ref,
    query_ref, staged, landed, back, taps, sums, toeplitz, xt, ut, yt, zt,
    in_send, in_recv, out_send, out_recv, tap_send, tap_recv, sum_send, sum_recv, local_sem, load_sem,
):
    ctx = lax.axis_index("ctx")
    ch = lax.axis_index("ch")
    ndev = nctx * nch
    me = ctx * nch + ch
    tokens = query_ref.shape[0]
    chans = query_ref.shape[1] // ndev
    groups = chans // GROUP_CH
    span = taps_ref.shape[1]
    seq = tokens * ndev
    block = TAPS_BLOCK
    nblocks = seq // block
    per_block = block // tokens
    chunk_groups = CHUNK_CH // GROUP_CH

    rounds = []
    for order in range(nch):
        step = -(order + 1) // 2 if order % 2 else order // 2
        offset = (nch // 2 + step) % nch
        other_ch = lax.rem(ch + offset, nch)
        turns = []
        for turn in range(1, nctx + 1):
            if offset or turn < nctx:
                other_ctx = lax.rem(ctx + turn, nctx)
                turns.append((other_ctx, other_ch, other_ctx * nch + other_ch))
        rounds.append((other_ch, turns))
    partners = [partner for _, turns in rounds for partner in turns]

    def columns(owner_ctx, owner_ch, chunk):
        start = owner_ch * (nctx * chans) + owner_ctx * chans + chunk * CHUNK_CH
        return pl.ds(pl.multiple_of(start, 128), CHUNK_CH)

    def gate(cols):
        staged[0:tokens, cols] = (
            key_ref[:, cols].astype(jnp.float32) * value_ref[:, cols].astype(jnp.float32)
        ).astype(jnp.bfloat16)
        staged[tokens:, cols] = (
            grad_ref[:, cols].astype(jnp.float32) * query_ref[:, cols].astype(jnp.float32)
        ).astype(jnp.bfloat16)

    def send_in(chunk, turns):
        for other_ctx, other_ch, other in turns:
            pltpu.make_async_remote_copy(
                src_ref=staged.at[:, columns(other_ctx, other_ch, chunk)],
                dst_ref=landed.at[chunk, me],
                send_sem=in_send.at[chunk],
                recv_sem=in_recv.at[chunk],
                device_id=(other_ctx, other_ch),
                device_id_type=MESH,
            ).start()

    def send_out(chunk):
        own = columns(ctx, ch, chunk)
        for other_ctx, other_ch, other in partners:
            for half, dst in ((0, conv_ref), (tokens, corr_ref)):
                pltpu.make_async_remote_copy(
                    src_ref=back.at[chunk, other, pl.ds(half, tokens)],
                    dst_ref=dst.at[:, own],
                    send_sem=out_send.at[chunk],
                    recv_sem=out_recv.at[chunk],
                    device_id=(other_ctx, other_ch),
                    device_id_type=MESH,
                ).start()

    def all_of(sem, chunk):
        whole = landed.at[chunk, pl.ds(0, ndev - 1)]
        pltpu.make_async_copy(whole, whole, sem.at[chunk]).wait()

    def tap_copy(step, sender):
        other = (ctx + step) % nctx
        slot = ctx if sender else other
        return pltpu.make_async_remote_copy(
            src_ref=taps_ref.at[pl.ds(pl.multiple_of(other * groups, 8), groups), :],
            dst_ref=taps.at[:, pl.ds(pl.multiple_of(slot * span, 128), span)],
            send_sem=tap_send.at[step],
            recv_sem=tap_recv.at[slot],
            device_id=(other, ch),
            device_id_type=MESH,
        )

    def sum_copy(step, sender):
        other = (ctx + step) % nctx
        slot = ctx if sender else other
        return pltpu.make_async_remote_copy(
            src_ref=sums.at[:, pl.ds(pl.multiple_of(other * span, 128), span)],
            dst_ref=filt_ref.at[pl.ds(pl.multiple_of(slot * groups, 8), groups), :],
            send_sem=sum_send.at[step],
            recv_sem=sum_recv.at[slot],
            device_id=(other, ch),
            device_id_type=MESH,
        )

    def own_in(chunk):
        return pltpu.make_async_copy(
            staged.at[:, columns(ctx, ch, chunk)], landed.at[chunk, me], local_sem.at[chunk]
        )

    def own_out(chunk, half):
        dst = (conv_ref, corr_ref)[half]
        return pltpu.make_async_copy(
            back.at[chunk, me, pl.ds(half * tokens, tokens)],
            dst.at[:, columns(ctx, ch, chunk)],
            local_sem.at[chunks + 2 * chunk + half],
        )

    def each(count, body, unroll=1):
        def step(n, carry):
            body(n)
            return carry

        lax.fori_loop(0, count, step, 0, unroll=unroll)

    def load(which, order):
        src, dst = (
            (key_hbm, key_ref),
            (value_hbm, value_ref),
            (grad_hbm, grad_ref),
            (query_hbm, query_ref),
        )[which]
        piece = nctx * chans
        cols = pl.ds(pl.multiple_of(rounds[order][0] * piece, 128), piece)
        return pltpu.make_async_copy(src.at[:, cols], dst.at[:, cols], load_sem.at[which, order])

    barrier = pltpu.get_barrier_semaphore()
    for other_ctx, other_ch, _ in partners:
        pl.semaphore_signal(barrier, inc=1, device_id=(other_ctx, other_ch), device_id_type=MESH)
    for order in range(nch):
        for which in range(4):
            load(which, order).start()
    own_taps = pltpu.make_async_copy(
        taps_ref.at[pl.ds(pl.multiple_of(ctx * groups, 8), groups), :],
        taps.at[:, pl.ds(pl.multiple_of(ctx * span, 128), span)],
        local_sem.at[3 * chunks],
    )
    own_taps.start()
    for chunk in range(chunks):
        for order, (other_ch, turns) in enumerate(rounds):
            if chunk == 0:
                for which in range(4):
                    load(which, order).wait()
            for owner in range(nctx):
                gate(columns(owner, other_ch, chunk))
            if chunk == 0 and order == 0:
                pl.semaphore_wait(barrier, ndev - 1)
                for step in range(1, nctx):
                    tap_copy(step, True).start()
            send_in(chunk, turns)
        own_in(chunk).start()
    own_taps.wait()
    for step in range(1, nctx):
        tap_copy(step, False).wait_recv()

    row_id = lax.broadcasted_iota(jnp.int32, (block, block), 0)
    col_id = lax.broadcasted_iota(jnp.int32, (block, block), 1)
    flip = (row_id + col_id == block - 1).astype(jnp.bfloat16)
    zeros = jnp.zeros((block, block), jnp.bfloat16)
    width = block + seq

    doubling = [8 << n for n in range((block // 8).bit_length() - 1)]

    def spread_diagonals(row):
        wide = pltpu.roll(jnp.broadcast_to(row, (8, width)), 0, 1, stride=1, stride_axis=0)
        for rows in doubling:
            wide = jnp.concatenate([wide, pltpu.roll(wide, rows, 1)], axis=0)
        return wide[:, block:]

    def sum_diagonals(values):
        for rows in doubling[::-1]:
            values = values[:rows] + pltpu.roll(values[rows:], rows, 1)
        values = pltpu.roll(values, 1, 1, stride=1, stride_axis=0)[:, block:]
        return jnp.sum(values, axis=0, keepdims=True)

    def later(stack):
        padded = jnp.concatenate([stack, zeros], axis=0)
        return jnp.concatenate(
            [padded[k * GROUP_CH : k * GROUP_CH + block] for k in range(nblocks)], axis=1
        )

    def earlier(stack):
        padded = jnp.concatenate([zeros, stack], axis=0)
        return jnp.concatenate(
            [padded[block - k * GROUP_CH : 2 * block - k * GROUP_CH] for k in range(nblocks)],
            axis=1,
        )

    def turn_in(chunk):
        for i in range(nblocks):
            src = pl.ds(i * per_block, per_block)
            for rows, dst in ((pl.ds(0, tokens), xt), (pl.ds(tokens, tokens), ut)):
                tile = landed[chunk, src, rows, :].reshape(block, CHUNK_CH)
                dst[chunk, :, i] = tile.T.reshape(chunk_groups, GROUP_CH, block)

    def build(group):
        row = taps[pl.ds(group, 1), :]
        row = jnp.concatenate([jnp.zeros((1, block), jnp.float32), row], axis=1)
        wide = spread_diagonals(row)
        high = wide.astype(jnp.bfloat16)
        low = (wide - high.astype(jnp.float32)).astype(jnp.bfloat16)
        for which, part in ((0, high), (1, low)):
            for k in range(nblocks):
                toeplitz[group, which, k] = part[:, k * block : (k + 1) * block]

    def convolve(chunk, g):
        x_cat = earlier(xt[chunk, g].reshape(block, block))
        u_cat = later(ut[chunk, g].reshape(block, block))
        conv = jnp.zeros((block, block), jnp.float32)
        corr = jnp.zeros((block, block), jnp.float32)
        for which in range(2):
            part = toeplitz[chunk * chunk_groups + g, which]
            tall = part.reshape(nblocks * block, block)
            flat = jnp.concatenate([part[k] for k in range(nblocks)], axis=1)
            conv = conv + jnp.dot(x_cat, tall, preferred_element_type=jnp.float32)
            corr = corr + lax.dot_general(u_cat, flat, NT, preferred_element_type=jnp.float32)
        yt[:, pl.ds(pl.multiple_of(g * GROUP_CH, GROUP_CH), GROUP_CH), :] = (
            conv.astype(jnp.bfloat16).reshape(nblocks, GROUP_CH, block)
        )
        zt[:, pl.ds(pl.multiple_of(g * GROUP_CH, GROUP_CH), GROUP_CH), :] = (
            corr.astype(jnp.bfloat16).reshape(nblocks, GROUP_CH, block)
        )

    def turn_out(chunk):
        for i in range(nblocks):
            dst = pl.ds(i * per_block, per_block)
            back[chunk, dst, 0:tokens, :] = yt[i].T.reshape(per_block, tokens, CHUNK_CH)
            back[chunk, dst, tokens:, :] = zt[i].T.reshape(per_block, tokens, CHUNK_CH)

    def correlate(chunk, g):
        stack_x = xt[chunk, g].reshape(block, block)
        u_cat = later(ut[chunk, g].reshape(block, block))
        turned = lax.dot_general(
            flip, stack_x, NT, preferred_element_type=jnp.float32
        ).astype(jnp.bfloat16)
        pairs = jnp.dot(turned, u_cat, preferred_element_type=jnp.float32)
        pairs = jnp.concatenate([pairs, jnp.zeros((block, block), jnp.float32)], axis=1)
        sums[pl.ds(chunk * chunk_groups + g, 1), :] = sum_diagonals(pairs)

    each(groups, build, unroll=2)
    for chunk in range(chunks):
        own_in(chunk).wait()
        all_of(in_recv, chunk)
        turn_in(chunk)
        each(chunk_groups, lambda g: convolve(chunk, g), unroll=2)
        turn_out(chunk)
        send_out(chunk)
        own_out(chunk, 0).start()
        own_out(chunk, 1).start()

    for chunk in range(chunks):
        each(chunk_groups, lambda g: correlate(chunk, g), unroll=2)

    for step in range(1, nctx):
        sum_copy(step, True).start()
    own_sums = pltpu.make_async_copy(
        sums.at[:, pl.ds(pl.multiple_of(ctx * span, 128), span)],
        filt_ref.at[pl.ds(pl.multiple_of(ctx * groups, 8), groups), :],
        local_sem.at[3 * chunks + 1],
    )
    own_sums.start()

    for step in range(1, nctx):
        tap_copy(step, True).wait_send()
    for chunk in range(chunks):
        all_of(in_send, chunk)
        all_of(out_send, chunk)
        all_of(out_recv, chunk)
        own_out(chunk, 0).wait()
        own_out(chunk, 1).wait()
    for step in range(1, nctx):
        sum_copy(step, True).wait_send()
        sum_copy(step, False).wait_recv()
    own_sums.wait()


def one_exchange(nctx, nch, query_gate, key_gate, value_proj, grad_out, long_filters):
    tokens, model = query_gate.shape
    ndev = nctx * nch
    chans = model // ndev
    groups = chans // GROUP_CH
    chunks = chans // CHUNK_CH
    seq = tokens * ndev
    nblocks = seq // TAPS_BLOCK
    chunk_groups = CHUNK_CH // GROUP_CH
    vmem = pl.BlockSpec(memory_space=pltpu.VMEM)
    half = jnp.bfloat16
    sem = pltpu.SemaphoreType.DMA
    convolved, correlated, grad_filters, key_near, value_near, grad_near = pl.pallas_call(
        functools.partial(exchange_kernel, nctx, nch, chunks),
        out_shape=(
            jax.ShapeDtypeStruct((tokens, model), half),
            jax.ShapeDtypeStruct((tokens, model), half),
            jax.ShapeDtypeStruct(long_filters.shape, jnp.float32),
        )
        + (jax.ShapeDtypeStruct((tokens, model), half),) * 3,
        in_specs=[pl.BlockSpec(memory_space=pltpu.HBM)] * 4 + [vmem],
        out_specs=(vmem,) * 6,
        scratch_shapes=[
            pltpu.VMEM((tokens, model), half),
            pltpu.VMEM((2 * tokens, model), half),
            pltpu.VMEM((chunks, ndev, 2 * tokens, CHUNK_CH), half),
            pltpu.VMEM((chunks, ndev, 2 * tokens, CHUNK_CH), half),
            pltpu.VMEM((groups, seq), jnp.float32),
            pltpu.VMEM((groups, seq), jnp.float32),
            pltpu.VMEM((groups, 2, nblocks, TAPS_BLOCK, TAPS_BLOCK), half),
            pltpu.VMEM((chunks, chunk_groups, nblocks, GROUP_CH, TAPS_BLOCK), half),
            pltpu.VMEM((chunks, chunk_groups, nblocks, GROUP_CH, TAPS_BLOCK), half),
            pltpu.VMEM((nblocks, CHUNK_CH, TAPS_BLOCK), half),
            pltpu.VMEM((nblocks, CHUNK_CH, TAPS_BLOCK), half),
            sem((chunks,)),
            sem((chunks,)),
            sem((chunks,)),
            sem((chunks,)),
            sem((nctx,)),
            sem((nctx,)),
            sem((nctx,)),
            sem((nctx,)),
            sem((3 * chunks + 2,)),
            sem((4, nch)),
        ],
        compiler_params=pltpu.CompilerParams(
            collective_id=0, has_side_effects=True, vmem_limit_bytes=51 * 1024 * 1024
        ),
        name="exchange_and_convolve",
    )(query_gate, key_gate, value_proj, grad_out, long_filters)
    convolved = convolved.astype(jnp.float32)
    correlated = correlated.astype(jnp.float32)
    return (
        (grad_near.astype(jnp.float32) * convolved).astype(half),
        (correlated * value_near.astype(jnp.float32)).astype(half),
        (correlated * key_near.astype(jnp.float32)).astype(half),
        grad_filters,
    )


def fits_one_exchange(nctx, nch, query_shape, filter_shape):
    tokens, model = query_shape
    ndev = nctx * nch
    return (
        model % (ndev * CHUNK_CH) == 0
        and tokens % 16 == 0
        and TAPS_BLOCK % tokens == 0
        and tokens * ndev == TAPS_BLOCK * (TAPS_BLOCK // GROUP_CH)
        and filter_shape[1] % 128 == 0
        and nctx * filter_shape[0] * nch * GROUP_CH == model * nctx
    )


def solution(mesh):
    nctx, nch = mesh.shape["ctx"], mesh.shape["ch"]

    def local(query_gate, key_gate, value_proj, grad_out, long_filters):
        args = (query_gate, key_gate, value_proj, grad_out, long_filters)
        if fits_one_exchange(nctx, nch, query_gate.shape, long_filters.shape):
            return one_exchange(nctx, nch, *args)
        return on_device(*args)

    in_specs = (
        P(("ctx", "ch"), None),
        P(("ctx", "ch"), None),
        P(("ctx", "ch"), None),
        P(("ctx", "ch"), None),
        P("ch", "ctx"),
    )
    out_specs = (
        P(("ctx", "ch"), None),
        P(("ctx", "ch"), None),
        P(("ctx", "ch"), None),
        P("ch", "ctx"),
    )
    return jax.shard_map(
        local, mesh=mesh, in_specs=in_specs, out_specs=out_specs, check_vma=False
    )
```

```python
import functools
import math

import jax
import jax.numpy as jnp
from jax import lax
from jax.experimental import pallas as pl
from jax.experimental.pallas import tpu as pltpu
from jax.sharding import PartitionSpec as P

GROUP_CH = 16


HIGHEST_MODE = lax.Precision.HIGHEST
SPLIT_MODE = lax.Precision.HIGH


def passed_along(value, axis, steps):
    count = lax.axis_size(axis)
    leading, last = (max(0, -steps), min(count, count - steps))
    return lax.ppermute(value, axis, [(source, source + steps) for source in range(leading, last)])


def make_tables(block_len):
    period = 2 * block_len
    steps = lax.iota(jnp.int32, block_len)
    phase = steps[:, None] * steps[None, :] % period
    angle = phase.astype(jnp.float32) * (math.pi / block_len)
    cosine = jnp.cos(angle)
    sine = jnp.sin(angle)
    parity = 1.0 - 2.0 * (steps % 2).astype(jnp.float32)
    weights = jnp.where(steps == 0, 1.0, 2.0).astype(jnp.float32) / period
    return (
        cosine,
        -sine,
        parity,
        cosine * weights[None, :],
        -sine * weights[None, :],
        parity / period,
    )


def columns_forward(tables, values):
    return (
        jnp.dot(tables[0], values, precision=SPLIT_MODE),
        jnp.dot(tables[1], values, precision=SPLIT_MODE),
        jnp.dot(tables[2], values, precision=SPLIT_MODE),
    )


def columns_inverse(tables, real_part, imag_part, nyquist):
    return (
        jnp.dot(tables[3], real_part, precision=SPLIT_MODE)
        + jnp.dot(tables[4], imag_part, precision=SPLIT_MODE)
        + tables[5][:, None] * nyquist[None, :]
    )


def rows_forward(tables, values):
    return (
        jnp.dot(values, tables[0], precision=HIGHEST_MODE),
        jnp.dot(values, tables[1], precision=HIGHEST_MODE),
        jnp.dot(values, tables[2], precision=HIGHEST_MODE),
    )


def rows_inverse(tables, real_part, imag_part, nyquist):
    return (
        jnp.dot(real_part, tables[3].T, precision=SPLIT_MODE)
        + jnp.dot(imag_part, tables[4].T, precision=SPLIT_MODE)
        + nyquist[:, None] * tables[5][None, :]
    )


def spread_groups(rows):
    groups, block_len = rows.shape
    return jnp.broadcast_to(rows.T[:, :, None], (block_len, groups, GROUP_CH)).reshape(
        block_len, groups * GROUP_CH
    )


def spread_vector(vector):
    return jnp.broadcast_to(vector[:, None], (vector.shape[0], GROUP_CH)).reshape(-1)


def group_rows(matrix):
    block_len, chans = matrix.shape
    return matrix.reshape(block_len, chans // GROUP_CH, GROUP_CH).sum(axis=2).T


def group_vector(vector):
    return vector.reshape(-1, GROUP_CH).sum(axis=1)


def by_blocks(tables, signal, upstream, long_filters):
    block_len, chans = signal.shape
    groups = long_filters.shape[0]
    nblocks = lax.axis_size("ctx")
    own_block = lax.axis_index("ctx")
    parity = tables[2]
    prev_taps = passed_along(long_filters, "ctx", 1)
    both_re, both_im, both_ny = rows_forward(
        tables, jnp.concatenate([prev_taps, long_filters], axis=0)
    )
    own_re = both_re[:groups] + both_re[groups:] * parity
    own_im = both_im[:groups] + both_im[groups:] * parity
    own_ny = both_ny[:groups] + both_ny[groups:]
    lag_re, lag_im, lag_ny = (
        lax.all_gather(own_re[None], "ctx", axis=0, tiled=True),
        lax.all_gather(own_im[None], "ctx", axis=0, tiled=True),
        lax.all_gather(own_ny[None], "ctx", axis=0, tiled=True),
    )
    mine_re, mine_im, mine_ny = columns_forward(tables, upstream.astype(jnp.float32))
    mine_re = mine_re * parity[:, None]
    mine_im = mine_im * parity[:, None]

    def pick(lag_index):
        return (
            spread_groups(lax.dynamic_index_in_dim(lag_re, lag_index, 0, keepdims=False)),
            spread_groups(lax.dynamic_index_in_dim(lag_im, lag_index, 0, keepdims=False)),
            spread_vector(lax.dynamic_index_in_dim(lag_ny, lag_index, 0, keepdims=False)),
        )

    def add_earlier(totals, block_vals, lag_index):
        conv_re, conv_im, conv_ny, back_re, back_im, back_ny, corr_re, corr_im, corr_ny = totals
        sig_re, sig_im, sig_ny = columns_forward(tables, block_vals)
        tap_re, tap_im, tap_ny = pick(lag_index)
        conv_re = conv_re + tap_re * sig_re - tap_im * sig_im
        conv_im = conv_im + tap_re * sig_im + tap_im * sig_re
        conv_ny = conv_ny + tap_ny * sig_ny
        corr_re = corr_re.at[lag_index].add(group_rows(mine_re * sig_re + mine_im * sig_im))
        corr_im = corr_im.at[lag_index].add(group_rows(mine_im * sig_re - mine_re * sig_im))
        corr_ny = corr_ny.at[lag_index].add(group_vector(mine_ny * sig_ny))
        return (conv_re, conv_im, conv_ny, back_re, back_im, back_ny, corr_re, corr_im, corr_ny)

    def add_later(totals, block_vals, lag_index):
        conv_re, conv_im, conv_ny, back_re, back_im, back_ny, corr_re, corr_im, corr_ny = totals
        up_re, up_im, up_ny = columns_forward(tables, block_vals)
        up_re = up_re * parity[:, None]
        up_im = up_im * parity[:, None]
        tap_re, tap_im, tap_ny = pick(lag_index)
        back_re = back_re + tap_re * up_re + tap_im * up_im
        back_im = back_im + tap_re * up_im - tap_im * up_re
        back_ny = back_ny + tap_ny * up_ny
        return (conv_re, conv_im, conv_ny, back_re, back_im, back_ny, corr_re, corr_im, corr_ny)

    plane = jnp.zeros((block_len, chans), jnp.float32)
    edge = jnp.zeros((chans,), jnp.float32)
    stack = jnp.zeros((nblocks, groups, block_len), jnp.float32)
    stack_edge = jnp.zeros((nblocks, groups), jnp.float32)
    initial = (plane, plane, edge, plane, plane, edge, stack, stack, stack_edge)
    sig_piece = lax.all_gather(signal, "ctx", axis=0, tiled=True)
    up_piece = lax.all_gather(upstream, "ctx", axis=0, tiled=True)
    piece_blocks = sig_piece.shape[0] // block_len

    def one_block(offset, running):
        sig_vals = lax.dynamic_slice_in_dim(sig_piece, offset * block_len, block_len, 0).astype(
            jnp.float32
        )
        up_vals = lax.dynamic_slice_in_dim(up_piece, offset * block_len, block_len, 0).astype(
            jnp.float32
        )
        running = lax.cond(
            offset <= own_block,
            lambda current: add_earlier(current, sig_vals, own_block - offset),
            lambda current: current,
            running,
        )
        running = lax.cond(
            offset >= own_block,
            lambda current: add_later(current, up_vals, offset - own_block),
            lambda current: current,
            running,
        )
        return running

    totals = lax.fori_loop(0, piece_blocks, one_block, initial)
    conv_re, conv_im, conv_ny, back_re, back_im, back_ny, corr_re, corr_im, corr_ny = totals
    convolved = columns_inverse(
        tables, conv_re * parity[:, None], conv_im * parity[:, None], conv_ny
    )
    correlated = columns_inverse(tables, back_re, back_im, back_ny)
    total_re, total_im, total_ny = lax.psum((corr_re, corr_im, corr_ny), "ctx")
    next_block = jnp.minimum(own_block + 1, nblocks - 1)
    valid = (own_block + 1 < nblocks).astype(jnp.float32)
    cur_re = lax.dynamic_index_in_dim(total_re, own_block, 0, keepdims=False)
    cur_im = lax.dynamic_index_in_dim(total_im, own_block, 0, keepdims=False)
    cur_ny = lax.dynamic_index_in_dim(total_ny, own_block, 0, keepdims=False)
    nxt_re = lax.dynamic_index_in_dim(total_re, next_block, 0, keepdims=False)
    nxt_im = lax.dynamic_index_in_dim(total_im, next_block, 0, keepdims=False)
    nxt_ny = lax.dynamic_index_in_dim(total_ny, next_block, 0, keepdims=False)
    upper = rows_inverse(tables, cur_re * parity, cur_im * parity, cur_ny)
    lower = rows_inverse(tables, nxt_re, nxt_im, nxt_ny)
    grad_filters = upper + lower * valid
    return (convolved, correlated, grad_filters)


def on_device(query_gate, key_gate, value_proj, grad_out, long_filters):
    query_cols, key_cols, value_cols, grad_cols = (
        lax.all_to_all(query_gate, "ch", split_axis=1, concat_axis=0, tiled=True),
        lax.all_to_all(key_gate, "ch", split_axis=1, concat_axis=0, tiled=True),
        lax.all_to_all(value_proj, "ch", split_axis=1, concat_axis=0, tiled=True),
        lax.all_to_all(grad_out, "ch", split_axis=1, concat_axis=0, tiled=True),
    )
    query_vals = query_cols.astype(jnp.float32)
    key_vals = key_cols.astype(jnp.float32)
    value_vals = value_cols.astype(jnp.float32)
    grad_vals = grad_cols.astype(jnp.float32)
    signal = (key_vals * value_vals).astype(jnp.bfloat16)
    upstream = (grad_vals * query_vals).astype(jnp.bfloat16)
    tables = make_tables(signal.shape[0])
    convolved, correlated, grad_filters = by_blocks(tables, signal, upstream, long_filters)
    conv_half = convolved.astype(jnp.bfloat16)
    corr_half = correlated.astype(jnp.bfloat16)
    conv_wide = lax.optimization_barrier(conv_half).astype(jnp.float32)
    corr_wide = lax.optimization_barrier(corr_half).astype(jnp.float32)
    grad_query = (grad_vals * conv_wide).astype(jnp.bfloat16)
    grad_key = (corr_wide * value_vals).astype(jnp.bfloat16)
    grad_value = (corr_wide * key_vals).astype(jnp.bfloat16)
    query_rows, key_rows, value_rows = (
        lax.all_to_all(grad_query, "ch", split_axis=0, concat_axis=1, tiled=True),
        lax.all_to_all(grad_key, "ch", split_axis=0, concat_axis=1, tiled=True),
        lax.all_to_all(grad_value, "ch", split_axis=0, concat_axis=1, tiled=True),
    )
    return (query_rows, key_rows, value_rows, grad_filters)


TAPS_BLOCK = 128
CHUNK_CH = 128
LOAD_PIECES = 4
MESH = pl.DeviceIdType.MESH
NT = (((1,), (1,)), ((), ()))


def exchange_kernel(
    nctx, nch, chunks,
    query_hbm, key_hbm, value_hbm, grad_hbm, taps_ref,
    conv_ref, corr_ref, filt_ref, key_ref, value_ref, grad_ref,
    query_ref, staged, landed, back, taps, sums, toeplitz, xt, ut, yt, zt,
    in_send, in_recv, out_send, out_recv, tap_send, tap_recv, sum_send, sum_recv, local_sem, load_sem,
):
    ctx = lax.axis_index("ctx")
    ch = lax.axis_index("ch")
    ndev = nctx * nch
    me = ctx * nch + ch
    tokens = query_ref.shape[0]
    chans = query_ref.shape[1] // ndev
    groups = chans // GROUP_CH
    span = taps_ref.shape[1]
    seq = tokens * ndev
    block = TAPS_BLOCK
    nblocks = seq // block
    per_block = block // tokens
    chunk_groups = CHUNK_CH // GROUP_CH

    offsets = []
    for order in range(nch // 2):
        far = nch // 2 + (-(order + 1) // 2 if order % 2 else order // 2)
        offsets.append((far, (far + nch // 2) % nch))
    partners = []
    for pair in offsets:
        for turn in range(1, nctx + 1):
            for offset in pair:
                if offset or turn < nctx:
                    other_ch = lax.rem(ch + offset, nch)
                    other_ctx = lax.rem(ctx + turn, nctx)
                    partners.append((other_ctx, other_ch, other_ctx * nch + other_ch))

    def columns(owner_ctx, owner_ch, chunk):
        start = owner_ch * (nctx * chans) + owner_ctx * chans + chunk * CHUNK_CH
        return pl.ds(pl.multiple_of(start, 128), CHUNK_CH)

    def gate(cols):
        staged[0:tokens, cols] = (
            key_ref[:, cols].astype(jnp.float32) * value_ref[:, cols].astype(jnp.float32)
        ).astype(jnp.bfloat16)
        staged[tokens:, cols] = (
            grad_ref[:, cols].astype(jnp.float32) * query_ref[:, cols].astype(jnp.float32)
        ).astype(jnp.bfloat16)

    def send_in(chunk):
        for other_ctx, other_ch, other in partners:
            pltpu.make_async_remote_copy(
                src_ref=staged.at[:, columns(other_ctx, other_ch, chunk)],
                dst_ref=landed.at[chunk, me],
                send_sem=in_send.at[chunk],
                recv_sem=in_recv.at[chunk],
                device_id=(other_ctx, other_ch),
                device_id_type=MESH,
            ).start()

    def send_out(chunk):
        own = columns(ctx, ch, chunk)
        for other_ctx, other_ch, other in partners:
            for half, dst in ((0, conv_ref), (tokens, corr_ref)):
                pltpu.make_async_remote_copy(
                    src_ref=back.at[chunk, other, pl.ds(half, tokens)],
                    dst_ref=dst.at[:, own],
                    send_sem=out_send.at[chunk],
                    recv_sem=out_recv.at[chunk],
                    device_id=(other_ctx, other_ch),
                    device_id_type=MESH,
                ).start()

    def all_of(sem, chunk):
        whole = landed.at[chunk, pl.ds(0, ndev - 1)]
        pltpu.make_async_copy(whole, whole, sem.at[chunk]).wait()

    def tap_copy(step, sender):
        other = (ctx + step) % nctx
        slot = ctx if sender else other
        return pltpu.make_async_remote_copy(
            src_ref=taps_ref.at[pl.ds(pl.multiple_of(other * groups, 8), groups), :],
            dst_ref=taps.at[:, pl.ds(pl.multiple_of(slot * span, 128), span)],
            send_sem=tap_send.at[step],
            recv_sem=tap_recv.at[slot],
            device_id=(other, ch),
            device_id_type=MESH,
        )

    def sum_copy(step, sender):
        other = (ctx + step) % nctx
        slot = ctx if sender else other
        return pltpu.make_async_remote_copy(
            src_ref=sums.at[:, pl.ds(pl.multiple_of(other * span, 128), span)],
            dst_ref=filt_ref.at[pl.ds(pl.multiple_of(slot * groups, 8), groups), :],
            send_sem=sum_send.at[step],
            recv_sem=sum_recv.at[slot],
            device_id=(other, ch),
            device_id_type=MESH,
        )

    def own_in(chunk):
        return pltpu.make_async_copy(
            staged.at[:, columns(ctx, ch, chunk)], landed.at[chunk, me], local_sem.at[chunk]
        )

    def own_out(chunk, half):
        dst = (conv_ref, corr_ref)[half]
        return pltpu.make_async_copy(
            back.at[chunk, me, pl.ds(half * tokens, tokens)],
            dst.at[:, columns(ctx, ch, chunk)],
            local_sem.at[chunks + 2 * chunk + half],
        )

    def each(count, body, unroll=1):
        def step(n, carry):
            body(n)
            return carry

        lax.fori_loop(0, count, step, 0, unroll=unroll)

    pieces = LOAD_PIECES
    piece = nctx * nch * chans // pieces

    def load(which, part):
        src, dst = (
            (query_hbm, query_ref),
            (key_hbm, key_ref),
            (value_hbm, value_ref),
            (grad_hbm, grad_ref),
        )[which]
        cols = pl.ds(part * piece, piece)
        return pltpu.make_async_copy(src.at[:, cols], dst.at[:, cols], load_sem.at[which, part])

    for part in range(pieces):
        for which in range(4):
            load(which, part).start()

    barrier = pltpu.get_barrier_semaphore()

    for other_ctx, other_ch, _ in partners:
        pl.semaphore_signal(barrier, inc=1, device_id=(other_ctx, other_ch), device_id_type=MESH)

    def gate_chunk(chunk, first, count):
        each(
            count,
            lambda n: gate(
                pl.ds(pl.multiple_of((first + n) * chans + chunk * CHUNK_CH, 128), CHUNK_CH)
            ),
            unroll=4,
        )

    own_taps = pltpu.make_async_copy(
        taps_ref.at[pl.ds(pl.multiple_of(ctx * groups, 8), groups), :],
        taps.at[:, pl.ds(pl.multiple_of(ctx * span, 128), span)],
        local_sem.at[3 * chunks],
    )
    own_taps.start()
    for part in range(pieces):
        for which in range(4):
            load(which, part).wait()
        gate_chunk(0, part * (ndev // pieces), ndev // pieces)
    pl.semaphore_wait(barrier, ndev - 1)
    for step in range(1, nctx):
        tap_copy(step, True).start()
    send_in(0)
    own_in(0).start()
    for chunk in range(1, chunks):
        gate_chunk(chunk, 0, ndev)
        send_in(chunk)
        own_in(chunk).start()
    own_taps.wait()
    for step in range(1, nctx):
        tap_copy(step, False).wait_recv()

    row_id = lax.broadcasted_iota(jnp.int32, (block, block), 0)
    col_id = lax.broadcasted_iota(jnp.int32, (block, block), 1)
    flip = (row_id + col_id == block - 1).astype(jnp.bfloat16)
    zeros = jnp.zeros((block, block), jnp.bfloat16)
    width = block + seq

    doubling = [8 << n for n in range((block // 8).bit_length() - 1)]

    def spread_diagonals(row):
        wide = pltpu.roll(jnp.broadcast_to(row, (8, width)), 0, 1, stride=1, stride_axis=0)
        for rows in doubling:
            wide = jnp.concatenate([wide, pltpu.roll(wide, rows, 1)], axis=0)
        return wide[:, block:]

    def sum_diagonals(values):
        for rows in doubling[::-1]:
            values = values[:rows] + pltpu.roll(values[rows:], rows, 1)
        values = pltpu.roll(values, 1, 1, stride=1, stride_axis=0)[:, block:]
        return jnp.sum(values, axis=0, keepdims=True)

    def later(stack):
        padded = jnp.concatenate([stack, zeros], axis=0)
        return jnp.concatenate(
            [padded[k * GROUP_CH : k * GROUP_CH + block] for k in range(nblocks)], axis=1
        )

    def earlier(stack):
        padded = jnp.concatenate([zeros, stack], axis=0)
        return jnp.concatenate(
            [padded[block - k * GROUP_CH : 2 * block - k * GROUP_CH] for k in range(nblocks)],
            axis=1,
        )

    def turn_in(chunk):
        for i in range(nblocks):
            src = pl.ds(i * per_block, per_block)
            for rows, dst in ((pl.ds(0, tokens), xt), (pl.ds(tokens, tokens), ut)):
                tile = landed[chunk, src, rows, :].reshape(block, CHUNK_CH)
                dst[chunk, :, i] = tile.T.reshape(chunk_groups, GROUP_CH, block)

    def build(group):
        row = taps[pl.ds(group, 1), :]
        row = jnp.concatenate([jnp.zeros((1, block), jnp.float32), row], axis=1)
        wide = spread_diagonals(row)
        high = wide.astype(jnp.bfloat16)
        low = (wide - high.astype(jnp.float32)).astype(jnp.bfloat16)
        for which, part in ((0, high), (1, low)):
            for k in range(nblocks):
                toeplitz[group, which, k] = part[:, k * block : (k + 1) * block]

    def convolve(chunk, g):
        x_cat = earlier(xt[chunk, g].reshape(block, block))
        u_cat = later(ut[chunk, g].reshape(block, block))
        conv = jnp.zeros((block, block), jnp.float32)
        corr = jnp.zeros((block, block), jnp.float32)
        for which in range(2):
            part = toeplitz[chunk * chunk_groups + g, which]
            tall = part.reshape(nblocks * block, block)
            flat = jnp.concatenate([part[k] for k in range(nblocks)], axis=1)
            conv = conv + jnp.dot(x_cat, tall, preferred_element_type=jnp.float32)
            corr = corr + lax.dot_general(u_cat, flat, NT, preferred_element_type=jnp.float32)
        yt[:, pl.ds(pl.multiple_of(g * GROUP_CH, GROUP_CH), GROUP_CH), :] = (
            conv.astype(jnp.bfloat16).reshape(nblocks, GROUP_CH, block)
        )
        zt[:, pl.ds(pl.multiple_of(g * GROUP_CH, GROUP_CH), GROUP_CH), :] = (
            corr.astype(jnp.bfloat16).reshape(nblocks, GROUP_CH, block)
        )

    def turn_out(chunk):
        for i in range(nblocks):
            dst = pl.ds(i * per_block, per_block)
            back[chunk, dst, 0:tokens, :] = yt[i].T.reshape(per_block, tokens, CHUNK_CH)
            back[chunk, dst, tokens:, :] = zt[i].T.reshape(per_block, tokens, CHUNK_CH)

    def correlate(chunk, g):
        stack_x = xt[chunk, g].reshape(block, block)
        u_cat = later(ut[chunk, g].reshape(block, block))
        turned = lax.dot_general(
            flip, stack_x, NT, preferred_element_type=jnp.float32
        ).astype(jnp.bfloat16)
        pairs = jnp.dot(turned, u_cat, preferred_element_type=jnp.float32)
        pairs = jnp.concatenate([pairs, jnp.zeros((block, block), jnp.float32)], axis=1)
        sums[pl.ds(chunk * chunk_groups + g, 1), :] = sum_diagonals(pairs)

    each(groups, build, unroll=2)
    for chunk in range(chunks):
        own_in(chunk).wait()
        all_of(in_recv, chunk)
        turn_in(chunk)
        each(chunk_groups, lambda g: convolve(chunk, g), unroll=2)
        turn_out(chunk)
        send_out(chunk)
        own_out(chunk, 0).start()
        own_out(chunk, 1).start()

    for chunk in range(chunks):
        each(chunk_groups, lambda g: correlate(chunk, g), unroll=2)

    for step in range(1, nctx):
        sum_copy(step, True).start()
    own_sums = pltpu.make_async_copy(
        sums.at[:, pl.ds(pl.multiple_of(ctx * span, 128), span)],
        filt_ref.at[pl.ds(pl.multiple_of(ctx * groups, 8), groups), :],
        local_sem.at[3 * chunks + 1],
    )
    own_sums.start()

    for step in range(1, nctx):
        tap_copy(step, True).wait_send()
    for chunk in range(chunks):
        all_of(in_send, chunk)
        all_of(out_send, chunk)
        all_of(out_recv, chunk)
        own_out(chunk, 0).wait()
        own_out(chunk, 1).wait()
    for step in range(1, nctx):
        sum_copy(step, True).wait_send()
        sum_copy(step, False).wait_recv()
    own_sums.wait()


def one_exchange(nctx, nch, query_gate, key_gate, value_proj, grad_out, long_filters):
    tokens, model = query_gate.shape
    ndev = nctx * nch
    chans = model // ndev
    groups = chans // GROUP_CH
    chunks = chans // CHUNK_CH
    seq = tokens * ndev
    nblocks = seq // TAPS_BLOCK
    chunk_groups = CHUNK_CH // GROUP_CH
    vmem = pl.BlockSpec(memory_space=pltpu.VMEM)
    half = jnp.bfloat16
    sem = pltpu.SemaphoreType.DMA
    convolved, correlated, grad_filters, key_near, value_near, grad_near = pl.pallas_call(
        functools.partial(exchange_kernel, nctx, nch, chunks),
        out_shape=(
            jax.ShapeDtypeStruct((tokens, model), half),
            jax.ShapeDtypeStruct((tokens, model), half),
            jax.ShapeDtypeStruct(long_filters.shape, jnp.float32),
        )
        + (jax.ShapeDtypeStruct((tokens, model), half),) * 3,
        in_specs=[pl.BlockSpec(memory_space=pltpu.HBM)] * 4 + [vmem],
        out_specs=(vmem,) * 6,
        scratch_shapes=[
            pltpu.VMEM((tokens, model), half),
            pltpu.VMEM((2 * tokens, model), half),
            pltpu.VMEM((chunks, ndev, 2 * tokens, CHUNK_CH), half),
            pltpu.VMEM((chunks, ndev, 2 * tokens, CHUNK_CH), half),
            pltpu.VMEM((groups, seq), jnp.float32),
            pltpu.VMEM((groups, seq), jnp.float32),
            pltpu.VMEM((groups, 2, nblocks, TAPS_BLOCK, TAPS_BLOCK), half),
            pltpu.VMEM((chunks, chunk_groups, nblocks, GROUP_CH, TAPS_BLOCK), half),
            pltpu.VMEM((chunks, chunk_groups, nblocks, GROUP_CH, TAPS_BLOCK), half),
            pltpu.VMEM((nblocks, CHUNK_CH, TAPS_BLOCK), half),
            pltpu.VMEM((nblocks, CHUNK_CH, TAPS_BLOCK), half),
            sem((chunks,)),
            sem((chunks,)),
            sem((chunks,)),
            sem((chunks,)),
            sem((nctx,)),
            sem((nctx,)),
            sem((nctx,)),
            sem((nctx,)),
            sem((3 * chunks + 2,)),
            sem((4, LOAD_PIECES)),
        ],
        compiler_params=pltpu.CompilerParams(
            collective_id=0, has_side_effects=True, vmem_limit_bytes=51 * 1024 * 1024
        ),
        name="exchange_and_convolve",
    )(query_gate, key_gate, value_proj, grad_out, long_filters)
    steps = 4
    part = pl.BlockSpec((tokens, model // steps), lambda i: (0, i))
    share = pl.BlockSpec((long_filters.shape[0] // steps, long_filters.shape[1]), lambda i: (i, 0))
    return pl.pallas_call(
        finish_kernel,
        grid=(steps,),
        out_shape=(jax.ShapeDtypeStruct((tokens, model), half),) * 3
        + (jax.ShapeDtypeStruct(long_filters.shape, jnp.float32),),
        in_specs=[part] * 5 + [share],
        out_specs=(part, part, part, share),
        name="multiply_gates",
    )(convolved, correlated, key_near, value_near, grad_near, grad_filters)


def finish_kernel(conv, corr, key, value, grad, filt, grad_query, grad_key, grad_value, grad_filt):
    back = corr[...].astype(jnp.float32)
    grad_query[...] = (grad[...].astype(jnp.float32) * conv[...].astype(jnp.float32)).astype(
        jnp.bfloat16
    )
    grad_key[...] = (back * value[...].astype(jnp.float32)).astype(jnp.bfloat16)
    grad_value[...] = (back * key[...].astype(jnp.float32)).astype(jnp.bfloat16)
    grad_filt[...] = filt[...]


def fits_one_exchange(nctx, nch, query_shape, filter_shape):
    tokens, model = query_shape
    ndev = nctx * nch
    return (
        model % (ndev * CHUNK_CH) == 0
        and tokens % 16 == 0
        and TAPS_BLOCK % tokens == 0
        and tokens * ndev == TAPS_BLOCK * (TAPS_BLOCK // GROUP_CH)
        and filter_shape[1] % 128 == 0
        and nctx * filter_shape[0] * nch * GROUP_CH == model * nctx
    )


def solution(mesh):
    nctx, nch = mesh.shape["ctx"], mesh.shape["ch"]

    def local(query_gate, key_gate, value_proj, grad_out, long_filters):
        args = (query_gate, key_gate, value_proj, grad_out, long_filters)
        if fits_one_exchange(nctx, nch, query_gate.shape, long_filters.shape):
            return one_exchange(nctx, nch, *args)
        return on_device(*args)

    in_specs = (
        P(("ctx", "ch"), None),
        P(("ctx", "ch"), None),
        P(("ctx", "ch"), None),
        P(("ctx", "ch"), None),
        P("ch", "ctx"),
    )
    out_specs = (
        P(("ctx", "ch"), None),
        P(("ctx", "ch"), None),
        P(("ctx", "ch"), None),
        P("ch", "ctx"),
    )
    return jax.shard_map(
        local, mesh=mesh, in_specs=in_specs, out_specs=out_specs, check_vma=False
    )
```
